32 devices in a mesh: doc: 8 (over y, x, core), filt: 4 (over z).
Axes of the slice: x: 2, y: 2, z: 4, core: 2. Of those that a mesh axis runs over, the one named last changes fastest.
Arguments:
- embedded: bfloat16 [16, 256, 256], P('doc'), may hold values from -8 to 8
- lengths: int32 [16], P('doc'), may hold values from 1 to 256, 1638 in all
- conv_weight: bfloat16 [256, 15, 1024], P(None, None, 'filt'), may hold values from -0.15625 to 0.15625
- head_weight: bfloat16 [3, 1024], P(None, 'filt'), may hold values from -0.109375 to 0.109375
- occupation: int32 [16], P('doc'), may hold values from 0 to 839
- cohort: int32 [16], P('doc'), may hold values from 0 to 39
- education: int32 [16], P('doc'), may hold values from 0 to 7
- occ_table: float32 [840], replicated, may hold values from -3 to 3
- cohort_table: float32 [40], replicated, may hold values from -3 to 3
- edu_table: float32 [8], replicated, may hold values from -3 to 3
- wage: float32 [16], P('doc'), may hold values from -8 to 8
Outputs:
- conv_grad: float32 [256, 15, 1024], P('doc', None, 'filt')
- head_grad: float32 [3, 1024], P(None, 'filt')
- occ_grad: float32 [840], replicated
- cohort_grad: float32 [40], replicated
- edu_grad: float32 [8], replicated
- prediction: float32 [16], P('doc')
The draws below stay inside these ranges and needn't reach their ends.
All inputs are finite; a program needn't handle non-finite values. No bound on the sum of `lengths` on one device may be relied on, other than what follows from the above.
Results may differ from the reference program's by a relative error of at most 0.0029.
Values sent between devices are 32-bit elements; how exact they have to be, the bound alone decides.
No kernel may reach another device: no remote copies, remote signals or barrier semaphores. Data moves between devices by JAX's collectives and lax.ppermute only.
A program may use at most 64 MiB of HBM per device.

```python
import math
import jax
import jax.numpy as jnp
import numpy as np
from jax import lax

E = 256
F = 1024
TAPS = 15
OCC = 840
COH = 40
EDU = 8
SEQ = 256
POSTS = 16


def draw_embedded(key, part):
    first_key, second_key = jax.random.split(key)
    scale = jnp.exp(jax.random.uniform(first_key, (POSTS, 1, 1), jnp.float32, math.log(0.5), math.log(2.0)))
    values = jnp.clip(jax.random.normal(second_key, (POSTS, SEQ, E), jnp.float32), -4.0, 4.0) * scale
    return values.astype(jnp.bfloat16)


def set_ends(array, own_key, smallest, largest):
    index_at = [jax.random.randint(jax.random.fold_in(own_key, axis), (), 0, length) for axis, length in enumerate(array.shape)]
    widest = array.shape.index(max(array.shape))
    next_to = index_at[:widest] + [(index_at[widest] + 1) % array.shape[widest]] + index_at[widest + 1:]
    return array.at[tuple(index_at)].set(smallest).at[tuple(next_to)].set(largest)


def level_of(stream_key, shape, shards, least, largest):
    gain = 1.0
    for dim, blocks in shards:
        heights = jax.random.uniform(jax.random.fold_in(jax.random.fold_in(stream_key, 6), dim), (blocks,), jnp.float32, least / len(shards), largest / len(shards))
        gain = gain * jnp.repeat(jnp.exp(heights), shape[dim] // blocks).reshape((-1,) + (1,) * (len(shape) - 1 - dim))
    return gain


def rank_table(number_of, skew):
    loads = [(1 << 20) // math.isqrt(grade ** skew) + 1 for grade in range(1, number_of + 1)]
    scale = 1 + sum(loads) // (1 << 30)
    return np.cumsum(np.array([max(1, weight // scale) for weight in loads]))


def ranked_ids(stream_key, shape, number_of, lean):
    listing = rank_table(number_of, lean)
    ticket = jax.random.randint(jax.random.fold_in(stream_key, 1), shape, 0, int(listing[number_of - 1]))
    grade = jnp.searchsorted(jnp.asarray(listing, jnp.int32), ticket, side="right")
    return jax.random.permutation(jax.random.fold_in(stream_key, 2), number_of)[grade].astype(jnp.int32)


def split_up(count, total, most, skew):
    loads = [(1 << 20) // math.isqrt(grade ** skew) + 1 for grade in range(2, count + 1)]
    surplus, counts = total - most - (count - 1), [1] * (count - 1)
    while surplus > 0:
        free = [i for i in range(count - 1) if counts[i] < most]
        mass, left = sum([loads[i] for i in free]), surplus
        for i in free:
            addition = min(most - counts[i], max(1, left * loads[i] // mass), surplus)
            counts[i] = counts[i] + addition
            surplus = surplus - addition
    return np.array([most] + counts)


def uneven(key, amount, total, reach, lean):
    if amount == 2:
        one = jax.random.randint(key, (), max(1, total - reach), min(reach, total - 1) + 1)
        return jnp.stack([one, total - one])
    tallies = jnp.asarray(split_up(amount, total, reach, lean), jnp.int32)
    pairs = (amount - 1) // 2
    giver, sink = tallies[1:1 + 2 * pairs:2], tallies[2:2 + 2 * pairs:2]
    margin = jnp.minimum(giver - 1, reach - sink)
    passed = jax.random.randint(jax.random.fold_in(key, 1), (pairs,), 0, 1 << 20) % (margin + 1)
    tallies = tallies.at[1:1 + 2 * pairs:2].set(giver - passed).at[2:2 + 2 * pairs:2].set(sink + passed)
    return tallies[jax.random.permutation(jax.random.fold_in(key, 2), amount)]


def centred(key, extent, width, most, cuts=(), held_as=jnp.bfloat16):
    factor_of = level_of(key, extent, cuts, -0.22, 0.18) if cuts else 1.0
    entries = jax.random.normal(key, extent, jnp.float32) * width * factor_of
    return jnp.minimum(jnp.maximum(entries, -most), most).astype(held_as)


def setup_inputs(seed: int = 0) -> dict:
    splits = jax.random.split(jax.random.key(seed), 12)
    return {
        "embedded": draw_embedded(jax.random.fold_in(splits[11], 71), 0),
        "lengths": uneven(splits[1], POSTS, POSTS * SEQ * 2 // 5, SEQ, 2).astype(jnp.int32),
        "conv_weight": centred(splits[2], (E, TAPS, F), (E * 5) ** -0.5, 0.15625, ((2, 4),)),
        "head_weight": centred(splits[3], (3, F), (3 * F) ** -0.5, 0.109375, ((1, 4),)),
        "occupation": set_ends(ranked_ids(splits[4], (POSTS,), OCC, 2), jax.random.fold_in(splits[4], 3), 0, OCC - 1).astype(jnp.int32),
        "cohort": set_ends(jax.random.randint(splits[5], (POSTS,), 0, COH), jax.random.fold_in(splits[5], 1), 0, COH - 1).astype(jnp.int32),
        "education": set_ends(jax.random.randint(splits[6], (POSTS,), 0, EDU), jax.random.fold_in(splits[6], 1), 0, EDU - 1).astype(jnp.int32),
        "occ_table": centred(splits[7], (OCC,), 0.5, 3.0, (), jnp.float32),
        "cohort_table": centred(splits[8], (COH,), 0.5, 3.0, (), jnp.float32),
        "edu_table": centred(splits[9], (EDU,), 0.5, 3.0, (), jnp.float32),
        "wage": centred(splits[10], (POSTS,), 2.0, 8.0, ((0, 8),), jnp.float32),
    }


TAU = 0.05
WIDTH_LIST = ((3, 0), (5, 3), (7, 8))


def reference(embedded, lengths, conv_weight, head_weight, occupation, cohort, education, occ_table, cohort_table, edu_table, wage):
    positions = jnp.arange(SEQ, dtype=jnp.int32)
    head = head_weight.astype(jnp.float32)
    offsets = occ_table[occupation] + cohort_table[cohort] + edu_table[education]
    matrices = []
    for taps, first in WIDTH_LIST:
        matrices.append(jnp.transpose(conv_weight[:, first:first + taps, :], (1, 0, 2)).reshape(taps * E, F))

    def one_post(carry, item):
        tokens, length, extra, goal = item
        valid = positions < length
        masked = jnp.where(valid[:, None], tokens, jnp.zeros_like(tokens))
        padded = jnp.pad(masked, ((3, 3), (0, 0)))
        columns = jnp.stack([padded[offset:offset + SEQ] for offset in range(7)], axis=1)
        features = []
        shares = []
        pieces = []
        for index in range(3):
            taps = WIDTH_LIST[index][0]
            half = (taps - 1) // 2
            window = columns[:, 3 - half:3 + half + 1, :].reshape(SEQ, taps * E)
            conv = jnp.dot(window, matrices[index], preferred_element_type=jnp.float32)
            score = jnp.where(valid[:, None], conv / TAU, -jnp.inf)
            top = jnp.max(score, axis=0)
            expd = jnp.exp(score - top[None, :])
            total = jnp.sum(expd, axis=0)
            features.append(TAU * (top + jnp.log(total)))
            shares.append(expd / total[None, :])
            pieces.append(window)
        feature = jnp.stack(features)
        pred = jnp.sum(feature * head) + extra
        resid = pred - goal
        grads = []
        for index in range(3):
            taps = WIDTH_LIST[index][0]
            slope = (resid * head[index][None, :] * shares[index]).astype(jnp.bfloat16)
            term = jnp.dot(pieces[index].T, slope, preferred_element_type=jnp.float32)
            grads.append(jnp.transpose(term.reshape(taps, E, F), (1, 0, 2)))
        conv_total = carry[0] + jnp.concatenate(grads, axis=1)
        head_total = carry[1] + resid * feature
        return (conv_total, head_total), (pred, resid)

    start = (jnp.zeros((E, TAPS, F), jnp.float32), jnp.zeros((3, F), jnp.float32))
    (conv_grad, head_grad), (prediction, residual) = lax.scan(one_post, start, (embedded, lengths, offsets, wage))
    occ_grad = jax.ops.segment_sum(residual, occupation, OCC)
    cohort_grad = jax.ops.segment_sum(residual, cohort, COH)
    edu_grad = jax.ops.segment_sum(residual, education, EDU)
    return conv_grad, head_grad, occ_grad, cohort_grad, edu_grad, prediction
```

```python
import functools

import jax
import jax.numpy as jnp
import numpy as np
from jax import lax
from jax.experimental import pallas as pl
from jax.experimental.pallas import tpu as pltpu
from jax.sharding import PartitionSpec as P

TAU = 0.05
WIDTH_LIST = ((3, 0), (5, 3), (7, 8))
TAPS = 15
REACH = 3
PAD = 8
BY_LAST = (((1,), (1,)), ((), ()))


def convolve(columns, weights):
    outputs = []
    for taps, first in WIDTH_LIST:
        half = (taps - 1) // 2
        window = columns[:, :, 3 - half : 3 + half + 1, :]
        outputs.append(
            jnp.einsum(
                "ptje,ejf->ptf",
                window,
                weights[:, first : first + taps, :],
                preferred_element_type=jnp.float32,
            )
        )
    return tuple(outputs)


def grad_terms(columns, slopes):
    outputs = []
    for index in range(3):
        taps = WIDTH_LIST[index][0]
        half = (taps - 1) // 2
        window = columns[:, :, 3 - half : 3 + half + 1, :]
        outputs.append(
            jnp.einsum("ptje,ptf->ejf", window, slopes[index], preferred_element_type=jnp.float32)
        )
    return jnp.concatenate(outputs, axis=1)


def one_hots(codes, size):
    return (codes[:, None] == jnp.arange(size, dtype=jnp.int32)[None, :]).astype(jnp.float32)


def local_scatter(
    embedded,
    lengths,
    conv_weight,
    head_weight,
    occupation,
    cohort,
    education,
    occ_table,
    cohort_table,
    edu_table,
    wage,
):
    posts, seq_len, _ = embedded.shape
    positions = jnp.arange(seq_len, dtype=jnp.int32)
    valid = positions[None, :] < lengths[:, None]
    masked = jnp.where(valid[:, :, None], embedded, jnp.zeros_like(embedded))
    padded = jnp.pad(masked, ((0, 0), (3, 3), (0, 0)))
    columns = jnp.stack([padded[:, offset : offset + seq_len, :] for offset in range(7)], axis=2)
    convs = convolve(columns, conv_weight)
    features = []
    shares = []
    for conv in convs:
        score = jnp.where(valid[:, :, None], conv / TAU, -jnp.inf)
        top = jnp.max(score, axis=1, keepdims=True)
        expd = jnp.exp(score - top)
        total = jnp.sum(expd, axis=1, keepdims=True)
        features.append(TAU * (top[:, 0, :] + jnp.log(total[:, 0, :])))
        shares.append(expd / total)
    feature = jnp.stack(features, axis=1)
    head = head_weight.astype(jnp.float32)
    partial_pred = jnp.sum(feature * head[None, :, :], axis=(1, 2))
    occ_hot = one_hots(occupation, occ_table.shape[0])
    cohort_hot = one_hots(cohort, cohort_table.shape[0])
    edu_hot = one_hots(education, edu_table.shape[0])
    highest = lax.Precision.HIGHEST
    offsets = (
        jnp.dot(occ_hot, occ_table, precision=highest)
        + jnp.dot(cohort_hot, cohort_table, precision=highest)
        + jnp.dot(edu_hot, edu_table, precision=highest)
    )
    prediction = lax.psum(partial_pred, "filt") + offsets
    residual = prediction - wage
    slopes = [
        (residual[:, None, None] * head[index][None, None, :] * shares[index]).astype(jnp.bfloat16)
        for index in range(3)
    ]
    conv_grad = lax.psum_scatter(
        grad_terms(columns, slopes), "doc", scatter_dimension=0, tiled=True
    )
    head_terms = jnp.sum(residual[:, None, None] * feature, axis=0)
    head_grad, occ_grad, cohort_grad, edu_grad = lax.psum(
        (
            head_terms,
            jnp.dot(residual, occ_hot, precision=highest),
            jnp.dot(residual, cohort_hot, precision=highest),
            jnp.dot(residual, edu_hot, precision=highest),
        ),
        "doc",
    )
    return (conv_grad, head_grad, occ_grad, cohort_grad, edu_grad, prediction)


def load_post(x, xpad):
    rows, width = x.shape
    xpad[0:PAD, :] = jnp.zeros((PAD, width), jnp.float32)
    xpad[PAD + rows :, :] = jnp.zeros((PAD, width), jnp.float32)
    xpad[PAD : PAD + rows, :] = x


def make_cols(xpad, cols):
    rows, width = cols.shape[0], xpad.shape[1]
    for offset in range(2 * REACH + 1):
        start = PAD - REACH + offset
        cols[:, offset * width : (offset + 1) * width] = xpad[start : start + rows, :].astype(
            jnp.bfloat16
        )


def forward(index, cols, w_ref, valid):
    taps, first = WIDTH_LIST[index]
    half = taps // 2
    width = w_ref.shape[0] // TAPS
    conv = jnp.dot(
        cols[:, (REACH - half) * width : (REACH + half + 1) * width],
        w_ref[first * width : (first + taps) * width, :],
        preferred_element_type=jnp.float32,
    )
    score = jnp.where(valid, conv * np.float32(1.0 / TAU), -jnp.inf)
    top = jnp.max(score, axis=0, keepdims=True)
    expd = jnp.exp(score - top)
    total = jnp.sum(expd, axis=0, keepdims=True)
    return top, total, expd


def select_rows(d_ref, cols, slice_e):
    rows = cols.shape[0]
    width = cols.shape[1] // (2 * REACH + 1)
    me = d_ref[0]
    row = lax.broadcasted_iota(jnp.int32, (2 * slice_e, width), 0)
    lane = lax.broadcasted_iota(jnp.int32, (2 * slice_e, width), 1)
    wanted = jnp.where(row < slice_e, me * slice_e + row, (me ^ 1) * slice_e + row - slice_e)
    pick = (lane == wanted).astype(jnp.bfloat16)
    middle = cols[:, REACH * width : (REACH + 1) * width]
    across = lax.dot_general(pick, middle, BY_LAST, preferred_element_type=jnp.float32)
    place = lax.broadcasted_iota(jnp.int32, (2 * slice_e, rows), 1)
    parts = []
    for offset in range(-REACH, REACH + 1):
        if offset:
            moved = pltpu.roll(across, (-offset) % rows, 1)
            inside = (place + offset >= 0) & (place + offset < rows)
            parts.append(jnp.where(inside, moved, 0.0))
        else:
            parts.append(across)
    return jnp.concatenate(parts, axis=0).astype(jnp.bfloat16)


def add_grad(index, at, slope, own_ref, other_ref, slice_e):
    taps, first = WIDTH_LIST[index]
    half = taps // 2
    step = 2 * slice_e
    term = jnp.dot(
        at[(REACH - half) * step : (REACH + half + 1) * step],
        slope,
        preferred_element_type=jnp.float32,
    )
    for j in range(taps):
        place = slice(((first + j) * slice_e), (first + j + 1) * slice_e)
        own_ref[place, :] += term[j * step : j * step + slice_e]
        other_ref[place, :] += term[j * step + slice_e : (j + 1) * step]


def own_kernel(len_ref, x_ref, w_ref, head_ref, part_ref, feat_ref, share_ref, xpad, cols):
    posts, rows, _ = x_ref.shape
    head = head_ref[...].astype(jnp.float32)

    def post(p, carry):
        load_post(x_ref[p], xpad)
        make_cols(xpad, cols)
        valid = lax.broadcasted_iota(jnp.int32, (rows, head.shape[1]), 0) < len_ref[p]
        part = jnp.zeros((1, head.shape[1]), jnp.float32)
        for index in range(3):
            top, total, expd = forward(index, cols, w_ref, valid)
            feature = np.float32(TAU) * (top + jnp.log(total))
            feat_ref[p, index : index + 1, :] = feature
            part = part + feature * head[index : index + 1]
            share_ref[p, index] = expd / total
        part_ref[p] = jnp.broadcast_to(jnp.sum(part, axis=1, keepdims=True), part_ref.shape[1:])
        return carry

    lax.fori_loop(0, posts, post, 0)


def first_kernel(
    n_other,
    slice_e,
    d_ref,
    len_ref,
    res_ref,
    own_ref,
    share_ref,
    *refs,
):
    others = refs[:n_other]
    w_ref, head_ref, acc_own, acc_other, feat_ref, xpads, cols = refs[n_other:]
    posts, rows, _ = own_ref.shape
    head = head_ref[...].astype(jnp.float32)
    acc_own[...] = jnp.zeros_like(acc_own)
    acc_other[...] = jnp.zeros_like(acc_other)
    for p in range(posts):
        load_post(own_ref[p], xpads.at[p])
    for p in range(n_other):
        load_post(others[p][...], xpads.at[posts + p])

    def own(p, carry):
        make_cols(xpads.at[p], cols)
        at = select_rows(d_ref, cols, slice_e)
        for index in range(3):
            scale = res_ref[p] * head[index : index + 1]
            slope = (scale * share_ref[p, index]).astype(jnp.bfloat16)
            add_grad(index, at, slope, acc_own, acc_other, slice_e)
        return carry

    def other(p, carry):
        make_cols(xpads.at[posts + p], cols)
        at = select_rows(d_ref, cols, slice_e)
        valid = lax.broadcasted_iota(jnp.int32, (rows, head.shape[1]), 0) < len_ref[posts + p]
        for index in range(3):
            top, total, expd = forward(index, cols, w_ref, valid)
            feat_ref[p, index : index + 1, :] = np.float32(TAU) * (top + jnp.log(total))
            scale = res_ref[posts + p] * head[index : index + 1]
            slope = (scale * (expd / total)).astype(jnp.bfloat16)
            add_grad(index, at, slope, acc_own, acc_other, slice_e)
        return carry

    lax.fori_loop(0, posts, own, 0)
    lax.fori_loop(0, n_other, other, 0)


def last_kernel(n_other, slice_e, d_ref, len_ref, res_ref, in_own, in_other, *refs):
    others = refs[:n_other]
    w_ref, head_ref, acc_own, acc_other, feat_ref, xpads, cols = refs[n_other:]
    rows = others[0].shape[0]
    head = head_ref[...].astype(jnp.float32)
    acc_own[...] = in_own[...]
    acc_other[...] = in_other[...]
    for p in range(n_other):
        load_post(others[p][...], xpads.at[p])

    def other(p, carry):
        make_cols(xpads.at[p], cols)
        at = select_rows(d_ref, cols, slice_e)
        valid = lax.broadcasted_iota(jnp.int32, (rows, head.shape[1]), 0) < len_ref[p]
        for index in range(3):
            top, total, expd = forward(index, cols, w_ref, valid)
            feat_ref[p, index : index + 1, :] = np.float32(TAU) * (top + jnp.log(total))
            scale = res_ref[p] * head[index : index + 1]
            slope = (scale * (expd / total)).astype(jnp.bfloat16)
            add_grad(index, at, slope, acc_own, acc_other, slice_e)
        return carry

    lax.fori_loop(0, n_other, other, 0)


def tree_sum(values):
    while len(values) > 1:
        values = [values[i] + values[i + 1] for i in range(0, len(values), 2)]
    return values[0]


def local_gather(n_doc, n_filt, *args):
    (
        embedded,
        lengths,
        conv_weight,
        head_weight,
        occupation,
        cohort,
        education,
        occ_table,
        cohort_table,
        edu_table,
        wage,
    ) = args
    posts, seq_len, dims = embedded.shape
    filters = conv_weight.shape[2]
    slice_e = dims // n_doc
    f32 = jnp.float32
    me = lax.axis_index("doc").astype(jnp.int32).reshape(1)
    partners = list(range(2, n_doc, 2))

    def swap(x, k, axis="doc"):
        size = n_doc if axis == "doc" else n_filt
        return lax.ppermute(x, axis, [(i, i ^ k) for i in range(size)])

    weights = jnp.transpose(conv_weight, (1, 0, 2)).reshape(TAPS * dims, filters)
    valid = jnp.arange(seq_len, dtype=jnp.int32)[None, :] < lengths[:, None]
    payload = jnp.where(valid[:, :, None], embedded, jnp.zeros_like(embedded)).astype(f32)
    pieces = [payload[p] for p in range(posts)]

    far = [k for k in partners if bin(k).count("1") > 1]
    near = [k for k in partners if bin(k).count("1") == 1]
    got = {}
    for k in far:
        for p in range(posts):
            got[k, p] = swap(pieces[p], k)
    for k in near:
        got[k, 0] = swap(pieces[0], k)

    vmem = pl.BlockSpec(memory_space=pltpu.VMEM)
    smem = pl.BlockSpec(memory_space=pltpu.SMEM)
    params = pltpu.CompilerParams(vmem_limit_bytes=48 << 20)
    pad_shape = (seq_len + 2 * PAD, dims)
    cols_shape = (seq_len, (2 * REACH + 1) * dims)

    part, feat_own, share_own = pl.pallas_call(
        own_kernel,
        in_specs=[smem, vmem, vmem, vmem],
        out_specs=[vmem] * 3,
        out_shape=[
            jax.ShapeDtypeStruct((posts, 8, 128), f32),
            jax.ShapeDtypeStruct((posts, 3, filters), f32),
            jax.ShapeDtypeStruct((posts, 3, seq_len, filters), f32),
        ],
        scratch_shapes=[pltpu.VMEM(pad_shape, f32), pltpu.VMEM(cols_shape, jnp.bfloat16)],
        compiler_params=params,
    )(lengths, payload, weights, head_weight)

    mine = part[:, 0, 0]
    parts = [mine] + [swap(mine, k, "filt") for k in range(1, n_filt)]
    offsets = (
        jnp.sum(one_hots(occupation, occ_table.shape[0]) * occ_table[None, :], axis=1)
        + jnp.sum(one_hots(cohort, cohort_table.shape[0]) * cohort_table[None, :], axis=1)
        + jnp.sum(one_hots(education, edu_table.shape[0]) * edu_table[None, :], axis=1)
    )
    prediction = tree_sum(parts) + offsets
    residual = prediction - wage

    facts = jnp.stack(
        [residual]
        + [v.astype(f32) for v in (lengths, occupation, cohort, education)]
    )
    told = {0: facts}
    for k in far + near:
        told[k] = swap(facts, k)
    pieces_late, _ = lax.optimization_barrier((pieces[1:], facts))
    for k in near:
        for p in range(1, posts):
            got[k, p] = swap(pieces_late[p - 1], k)

    early = [(k, p) for k in far for p in range(posts)] + [(k, 0) for k in near]
    late = [(k, p) for k in near for p in range(1, posts)]
    order = [(0, p) for p in range(posts)] + early
    res_first = jnp.stack([told[k][0, p] for k, p in order])
    len_first = jnp.stack([told[k][1, p] for k, p in order]).astype(jnp.int32)
    res_last = jnp.stack([told[k][0, p] for k, p in late])
    len_last = jnp.stack([told[k][1, p] for k, p in late]).astype(jnp.int32)

    acc_shape = jax.ShapeDtypeStruct((TAPS * slice_e, filters), f32)

    acc_own, acc_other, feat_early = pl.pallas_call(
        functools.partial(first_kernel, len(early), slice_e),
        in_specs=[smem, smem, smem] + [vmem] * (2 + len(early) + 2),
        out_specs=[vmem] * 3,
        out_shape=[acc_shape, acc_shape, jax.ShapeDtypeStruct((len(early), 3, filters), f32)],
        scratch_shapes=[
            pltpu.VMEM((posts + len(early),) + pad_shape, f32),
            pltpu.VMEM(cols_shape, jnp.bfloat16),
        ],
        compiler_params=params,
    )(
        me,
        len_first,
        res_first,
        payload,
        share_own,
        *[got[key] for key in early],
        weights,
        head_weight,
    )
    acc_own, acc_other, feat_late = pl.pallas_call(
        functools.partial(last_kernel, len(late), slice_e),
        in_specs=[smem, smem, smem] + [vmem] * (2 + len(late) + 2),
        out_specs=[vmem] * 3,
        out_shape=[acc_shape, acc_shape, jax.ShapeDtypeStruct((len(late), 3, filters), f32)],
        scratch_shapes=[
            pltpu.VMEM((len(late),) + pad_shape, f32),
            pltpu.VMEM(cols_shape, jnp.bfloat16),
        ],
        compiler_params=params,
    )(
        me,
        len_last,
        res_last,
        acc_own,
        acc_other,
        *[got[key] for key in late],
        weights,
        head_weight,
    )

    features = {(0, p): feat_own[p] for p in range(posts)}
    features.update({key: feat_early[i] for i, key in enumerate(early)})
    features.update({key: feat_late[i] for i, key in enumerate(late)})
    sizes = (occ_table.shape[0], cohort_table.shape[0], edu_table.shape[0])

    def device_terms(k):
        head_term = sum(told[k][0, p] * features[k, p] for p in range(posts))
        codes = [
            jnp.sum(told[k][0][:, None] * one_hots(told[k][2 + i].astype(jnp.int32), size), axis=0)
            for i, size in enumerate(sizes)
        ]
        return jnp.concatenate([head_term.reshape(-1)] + codes)

    sums = tree_sum([device_terms(k) for k in range(0, n_doc, 2)])
    rows = -(-sums.shape[0] // filters)
    tail = jnp.pad(sums, (0, rows * filters - sums.shape[0])).reshape(rows, filters)
    other_grad = swap(acc_other, 1)
    sums = sums + swap(tail, 1).reshape(-1)[: sums.shape[0]]
    conv_grad = jnp.transpose((acc_own + other_grad).reshape(TAPS, slice_e, filters), (1, 0, 2))
    head_grad = sums[: 3 * filters].reshape(3, filters)
    outs = []
    start = 3 * filters
    for size in sizes:
        outs.append(sums[start : start + size])
        start += size
    return (conv_grad, head_grad, *outs, prediction)


def solution(mesh):
    n_doc, n_filt = mesh.shape["doc"], mesh.shape["filt"]
    if n_doc == 8 and n_filt == 4:
        local = functools.partial(local_gather, n_doc, n_filt)
    else:
        local = local_scatter
    return jax.shard_map(
        local,
        mesh=mesh,
        in_specs=(
            P("doc", None, None),
            P("doc"),
            P(None, None, "filt"),
            P(None, "filt"),
            P("doc"),
            P("doc"),
            P("doc"),
            P(),
            P(),
            P(),
            P("doc"),
        ),
        out_specs=(P("doc", None, "filt"), P(None, "filt"), P(), P(), P(), P("doc")),
        check_vma=False,
    )
```

```python
import functools

import jax
import jax.numpy as jnp
import numpy as np
from jax import lax
from jax.experimental import pallas as pl
from jax.experimental.pallas import tpu as pltpu
from jax.sharding import PartitionSpec as P

TAU = 0.05
WIDTH_LIST = ((3, 0), (5, 3), (7, 8))
TAPS = 15
REACH = 3
PAD = 8
OUTSIDE = np.float32(1024.0)
BY_LAST = (((1,), (1,)), ((), ()))


def convolve(columns, weights):
    outputs = []
    for taps, first in WIDTH_LIST:
        half = (taps - 1) // 2
        window = columns[:, :, 3 - half : 3 + half + 1, :]
        outputs.append(
            jnp.einsum(
                "ptje,ejf->ptf",
                window,
                weights[:, first : first + taps, :],
                preferred_element_type=jnp.float32,
            )
        )
    return tuple(outputs)


def grad_terms(columns, slopes):
    outputs = []
    for index in range(3):
        taps = WIDTH_LIST[index][0]
        half = (taps - 1) // 2
        window = columns[:, :, 3 - half : 3 + half + 1, :]
        outputs.append(
            jnp.einsum("ptje,ptf->ejf", window, slopes[index], preferred_element_type=jnp.float32)
        )
    return jnp.concatenate(outputs, axis=1)


def one_hots(codes, size):
    return (codes[:, None] == jnp.arange(size, dtype=jnp.int32)[None, :]).astype(jnp.float32)


def local_scatter(
    embedded,
    lengths,
    conv_weight,
    head_weight,
    occupation,
    cohort,
    education,
    occ_table,
    cohort_table,
    edu_table,
    wage,
):
    posts, seq_len, _ = embedded.shape
    positions = jnp.arange(seq_len, dtype=jnp.int32)
    valid = positions[None, :] < lengths[:, None]
    masked = jnp.where(valid[:, :, None], embedded, jnp.zeros_like(embedded))
    padded = jnp.pad(masked, ((0, 0), (3, 3), (0, 0)))
    columns = jnp.stack([padded[:, offset : offset + seq_len, :] for offset in range(7)], axis=2)
    convs = convolve(columns, conv_weight)
    features = []
    shares = []
    for conv in convs:
        score = jnp.where(valid[:, :, None], conv / TAU, -jnp.inf)
        top = jnp.max(score, axis=1, keepdims=True)
        expd = jnp.exp(score - top)
        total = jnp.sum(expd, axis=1, keepdims=True)
        features.append(TAU * (top[:, 0, :] + jnp.log(total[:, 0, :])))
        shares.append(expd / total)
    feature = jnp.stack(features, axis=1)
    head = head_weight.astype(jnp.float32)
    partial_pred = jnp.sum(feature * head[None, :, :], axis=(1, 2))
    occ_hot = one_hots(occupation, occ_table.shape[0])
    cohort_hot = one_hots(cohort, cohort_table.shape[0])
    edu_hot = one_hots(education, edu_table.shape[0])
    highest = lax.Precision.HIGHEST
    offsets = (
        jnp.dot(occ_hot, occ_table, precision=highest)
        + jnp.dot(cohort_hot, cohort_table, precision=highest)
        + jnp.dot(edu_hot, edu_table, precision=highest)
    )
    prediction = lax.psum(partial_pred, "filt") + offsets
    residual = prediction - wage
    slopes = [
        (residual[:, None, None] * head[index][None, None, :] * shares[index]).astype(jnp.bfloat16)
        for index in range(3)
    ]
    conv_grad = lax.psum_scatter(
        grad_terms(columns, slopes), "doc", scatter_dimension=0, tiled=True
    )
    head_terms = jnp.sum(residual[:, None, None] * feature, axis=0)
    head_grad, occ_grad, cohort_grad, edu_grad = lax.psum(
        (
            head_terms,
            jnp.dot(residual, occ_hot, precision=highest),
            jnp.dot(residual, cohort_hot, precision=highest),
            jnp.dot(residual, edu_hot, precision=highest),
        ),
        "doc",
    )
    return (conv_grad, head_grad, occ_grad, cohort_grad, edu_grad, prediction)


def load_post(x, xpad):
    rows, width = x.shape
    xpad[0:PAD, :] = jnp.zeros((PAD, width), jnp.float32)
    xpad[PAD + rows :, :] = jnp.zeros((PAD, width), jnp.float32)
    xpad[PAD : PAD + rows, :] = jnp.where(x < OUTSIDE, x, 0.0)


def length_of(x):
    inside = (x[:, 0:128] < OUTSIDE).astype(jnp.float32)
    return jnp.max(jnp.sum(inside, axis=0, keepdims=True)).astype(jnp.int32)


def make_cols(xpad, cols):
    rows, width = cols.shape[0], xpad.shape[1]
    for offset in range(2 * REACH + 1):
        start = PAD - REACH + offset
        cols[:, offset * width : (offset + 1) * width] = xpad[start : start + rows, :].astype(
            jnp.bfloat16
        )


def forward(cols, w_ref, head, length, feat, share):
    width = w_ref.shape[0] // TAPS
    valid = lax.broadcasted_iota(jnp.int32, (cols.shape[0], head.shape[1]), 0) < length
    part = jnp.zeros((1, head.shape[1]), jnp.float32)
    for index, (taps, first) in enumerate(WIDTH_LIST):
        half = taps // 2
        conv = jnp.dot(
            cols[:, (REACH - half) * width : (REACH + half + 1) * width],
            w_ref[first * width : (first + taps) * width, :],
            preferred_element_type=jnp.float32,
        )
        score = jnp.where(valid, conv * np.float32(1.0 / TAU), -jnp.inf)
        top = jnp.max(score, axis=0, keepdims=True)
        expd = jnp.exp(score - top)
        total = jnp.sum(expd, axis=0, keepdims=True)
        feature = np.float32(TAU) * (top + jnp.log(total))
        feat[index : index + 1, :] = feature
        part = part + feature * head[index : index + 1]
        share[index] = expd * (head[index : index + 1] / total)
    return part


def pick_rows(d_ref, cols, slice_e):
    rows = cols.shape[0]
    width = cols.shape[1] // (2 * REACH + 1)
    me = d_ref[0]
    row = lax.broadcasted_iota(jnp.int32, (2 * slice_e, width), 0)
    lane = lax.broadcasted_iota(jnp.int32, (2 * slice_e, width), 1)
    wanted = jnp.where(row < slice_e, me * slice_e + row, (me ^ 1) * slice_e + row - slice_e)
    pick = (lane == wanted).astype(jnp.bfloat16)
    middle = cols[:, REACH * width : (REACH + 1) * width]
    across = lax.dot_general(pick, middle, BY_LAST, preferred_element_type=jnp.float32)
    place = lax.broadcasted_iota(jnp.int32, (2 * slice_e, rows), 1)
    parts = []
    for offset in range(-REACH, REACH + 1):
        if offset:
            moved = pltpu.roll(across, (-offset) % rows, 1)
            inside = (place + offset >= 0) & (place + offset < rows)
            parts.append(jnp.where(inside, moved, 0.0))
        else:
            parts.append(across)
    return jnp.concatenate(parts, axis=0).astype(jnp.bfloat16)


def backward(cols, d_ref, residual, share, acc_own, acc_other, slice_e):
    at = pick_rows(d_ref, cols, slice_e)
    step = 2 * slice_e
    for index, (taps, first) in enumerate(WIDTH_LIST):
        half = taps // 2
        slope = (residual * share[index]).astype(jnp.bfloat16)
        term = jnp.dot(
            at[(REACH - half) * step : (REACH + half + 1) * step],
            slope,
            preferred_element_type=jnp.float32,
        )
        for j in range(taps):
            place = slice((first + j) * slice_e, (first + j + 1) * slice_e)
            acc_own[place, :] += term[j * step : j * step + slice_e]
            acc_other[place, :] += term[j * step + slice_e : (j + 1) * step]


def mask_kernel(len_ref, x_ref, *piece_refs):
    rows, width = x_ref.shape[1:]
    place = lax.broadcasted_iota(jnp.int32, (rows, width), 0)
    for p, piece in enumerate(piece_refs):
        piece[...] = jnp.where(place < len_ref[p], x_ref[p].astype(jnp.float32), OUTSIDE)


def own_kernel(len_ref, pieces, w_ref, head_ref, part_ref, feat_ref, share_ref, xpads, cols):
    posts = pieces.shape[0]
    head = head_ref[...].astype(jnp.float32)
    part_ref[...] = jnp.zeros_like(part_ref)

    def post(p, carry):
        load_post(pieces[p], xpads.at[p])
        make_cols(xpads.at[p], cols)
        part = forward(cols, w_ref, head, len_ref[p], feat_ref.at[p], share_ref.at[p])
        part_ref[pl.ds(p, 1), :] = jnp.broadcast_to(
            jnp.sum(part, axis=1, keepdims=True), (1, part_ref.shape[1])
        )
        return carry

    lax.fori_loop(0, posts, post, 0)


def facts_kernel(*refs):
    occ_ref, coh_ref, edu_ref, wage_ref, occ_t, coh_t, edu_t = refs[:7]
    one, two, pieces, facts_ref, pred_ref, pack_ref = refs[7:]
    posts, rows, _ = pieces.shape
    pred = one[...] + two[...]
    lanes = pred.shape[1]
    lane = lax.broadcasted_iota(jnp.int32, (1, lanes), 1)
    facts_ref[...] = jnp.zeros_like(facts_ref)
    out = jnp.zeros((1, lanes), jnp.float32)
    for p in range(posts):
        offset = occ_t[occ_ref[p]] + coh_t[coh_ref[p]] + edu_t[edu_ref[p]]
        value = pred[p : p + 1] + offset
        out = jnp.where(lane == p, value, out)
        facts_ref[p : p + 1, :] = value - wage_ref[p]
        for kind, ref in enumerate((occ_ref, coh_ref, edu_ref)):
            row = (kind + 1) * posts + p
            facts_ref[row : row + 1, :] = jnp.full(
                (1, lanes), ref[p].astype(jnp.float32), jnp.float32
            )
    pred_ref[...] = out[:, :posts]
    pack_ref[0:rows, :] = pieces[posts - 1]
    pack_ref[rows:, :] = jnp.zeros((pack_ref.shape[0] - rows, pack_ref.shape[1]), jnp.float32)
    pack_ref[rows:, 0:lanes] = facts_ref[...]


def first_kernel(
    n_near,
    slice_e,
    d_ref,
    share_own,
    facts,
    own,
    far,
    far_facts,
    *refs,
):
    near = refs[:n_near]
    w_ref, head_ref, acc_own, acc_other, feat_far, feat_near, share_near = refs[n_near : n_near + 7]
    xpads, share, cols = refs[n_near + 7 :]
    posts = own.shape[0]
    head = head_ref[...].astype(jnp.float32)
    acc_own[...] = jnp.zeros_like(acc_own)
    acc_other[...] = jnp.zeros_like(acc_other)

    def own_post(p, carry):
        load_post(own[p], xpads.at[0])
        make_cols(xpads.at[0], cols)
        residual = facts[pl.ds(p, 1), 0:1]
        backward(cols, d_ref, residual, share_own.at[p], acc_own, acc_other, slice_e)
        return carry

    def far_post(p, carry):
        load_post(far[p], xpads.at[0])
        make_cols(xpads.at[0], cols)
        forward(cols, w_ref, head, length_of(far[p]), feat_far.at[p], share)
        residual = far_facts[pl.ds(p, 1), 0:1]
        backward(cols, d_ref, residual, share, acc_own, acc_other, slice_e)
        return carry

    lax.fori_loop(0, posts, own_post, 0)
    lax.fori_loop(0, posts, far_post, 0)
    for k in range(n_near):
        load_post(near[k][...], xpads.at[k])
    lens = [length_of(near[k]) for k in range(n_near)]

    def near_post(k, carry):
        make_cols(xpads.at[k], cols)
        length = lens[0]
        for i in range(1, n_near):
            length = jnp.where(k == i, lens[i], length)
        forward(cols, w_ref, head, length, feat_near.at[k], share_near.at[k])
        return carry

    lax.fori_loop(0, n_near, near_post, 0)


def last_kernel(n_near, sizes, slice_e, d_ref, in_own, in_other, share_near, *refs):
    near = refs[:n_near]
    packs = refs[n_near : 2 * n_near]
    facts, far_facts, feat_own, feat_far, feat_near = refs[2 * n_near : 2 * n_near + 5]
    w_ref, head_ref, acc_own, acc_other, sums_ref = refs[2 * n_near + 5 : 2 * n_near + 10]
    xpads, facs, feat_last, share, cols = refs[2 * n_near + 10 :]
    posts = feat_own.shape[0]
    rows = near[0].shape[0]
    head = head_ref[...].astype(jnp.float32)
    filters = head.shape[1]
    acc_own[...] = in_own[...]
    acc_other[...] = in_other[...]
    lens = []
    for k in range(n_near):
        load_post(near[k][...], xpads.at[2 * k])
        load_post(packs[k][0:rows, :], xpads.at[2 * k + 1])
        facs[k] = packs[k][rows:, :]
        lens.append(length_of(packs[k].at[0:rows]))

    def near_post(k, carry):
        make_cols(xpads.at[2 * k], cols)
        backward(
            cols, d_ref, facs[k, 0:1, 0:1], share_near.at[k], acc_own, acc_other, slice_e
        )
        make_cols(xpads.at[2 * k + 1], cols)
        length = lens[0]
        for i in range(1, n_near):
            length = jnp.where(k == i, lens[i], length)
        forward(cols, w_ref, head, length, feat_last.at[k], share)
        backward(cols, d_ref, facs[k, 1:2, 0:1], share, acc_own, acc_other, slice_e)
        return carry

    lax.fori_loop(0, n_near, near_post, 0)

    def chip_terms(told, feature):
        n_rows = code_rows(sizes, filters)
        place = lax.broadcasted_iota(jnp.int32, (n_rows, filters), 0) * filters
        place = place + lax.broadcasted_iota(jnp.int32, (n_rows, filters), 1)
        head_term = jnp.zeros((3, filters), jnp.float32)
        code_term = jnp.zeros((n_rows, filters), jnp.float32)
        for p in range(posts):
            residual = told[p : p + 1, 0:1]
            head_term = head_term + residual * feature[p]
            for kind, start in enumerate(code_starts(sizes, filters)):
                at_row = (kind + 1) * posts + p
                code = told[at_row : at_row + 1, 0:1].astype(jnp.int32) + start
                code_term = code_term + jnp.where(place == code, residual, 0.0)
        return head_term, code_term

    terms = [
        chip_terms(facts[...], [feat_own[p] for p in range(posts)]),
        *[
            chip_terms(facs[k], [feat_near[k, 0:3, :], feat_last[k, 0:3, :]])
            for k in range(n_near)
        ],
        chip_terms(far_facts[...], [feat_far[p, 0:3, :] for p in range(posts)]),
    ]
    sums_ref[...] = jnp.zeros_like(sums_ref)
    sums_ref[0:3, :] = tree_sum([term[0] for term in terms])
    sums_ref[3 : 3 + code_rows(sizes, filters), :] = tree_sum([term[1] for term in terms])


def tree_sum(values):
    while len(values) > 1:
        values = [values[i] + values[i + 1] for i in range(0, len(values), 2)]
    return values[0]


def code_starts(sizes, filters):
    starts, start = [], 0
    for size in sizes:
        starts.append(start)
        start += -(-size // filters) * filters
    return starts


def code_rows(sizes, filters):
    return sum(-(-size // filters) for size in sizes)


def sums_kernel(sizes, mine_ref, came_ref, head_ref, *code_refs):
    filters = mine_ref.shape[1]
    head_ref[...] = mine_ref[0:3, :] + came_ref[0:3, :]
    row = 3
    for size, ref in zip(sizes, code_refs):
        for start in range(0, size, filters):
            count = min(filters, size - start)
            total = mine_ref[row : row + 1, :] + came_ref[row : row + 1, :]
            ref[:, start : start + count] = total[:, :count]
            row += 1


def add_kernel(mine_ref, came_ref, out_ref):
    out_ref[...] = mine_ref[...] + came_ref[...]


def local_gather(n_doc, n_filt, *args):
    (
        embedded,
        lengths,
        conv_weight,
        head_weight,
        occupation,
        cohort,
        education,
        occ_table,
        cohort_table,
        edu_table,
        wage,
    ) = args
    posts, seq_len, dims = embedded.shape
    filters = conv_weight.shape[2]
    slice_e = dims // n_doc
    sizes = (occ_table.shape[0], cohort_table.shape[0], edu_table.shape[0])
    f32 = jnp.float32
    me = lax.axis_index("doc").astype(jnp.int32).reshape(1)
    vmem = pl.BlockSpec(memory_space=pltpu.VMEM)
    smem = pl.BlockSpec(memory_space=pltpu.SMEM)
    pad_shape = (seq_len + 2 * PAD, dims)
    cols = pltpu.VMEM((seq_len, (2 * REACH + 1) * dims), jnp.bfloat16)
    share_shape = (3, seq_len, filters)

    def swap(x, k, axis="doc"):
        size = n_doc if axis == "doc" else n_filt
        return lax.ppermute(x, axis, [(i, i ^ k) for i in range(size)])

    def call(kernel, n_smem, n_vmem, out, scratch=()):
        return pl.pallas_call(
            kernel,
            in_specs=[smem] * n_smem + [vmem] * n_vmem,
            out_specs=[vmem] * len(out),
            out_shape=[jax.ShapeDtypeStruct(shape, f32) for shape in out],
            scratch_shapes=list(scratch),
            compiler_params=pltpu.CompilerParams(vmem_limit_bytes=24 << 20),
            cost_estimate=pl.CostEstimate(flops=1, bytes_accessed=1, transcendentals=0),
        )

    def mask_all(len_ref, x_ref, all_ref, first_ref):
        mask_kernel(len_ref, x_ref, *[all_ref.at[p] for p in range(posts)])
        first_ref[...] = all_ref[0]

    weights = jnp.transpose(conv_weight, (1, 0, 2)).reshape(TAPS * dims, filters)
    pieces, piece = call(mask_all, 1, 1, [(posts, seq_len, dims), (seq_len, dims)])(
        lengths, embedded
    )

    near = [k for k in range(2, n_doc, 2) if bin(k).count("1") == 1]
    far = sum(near)
    first = [swap(piece, k) for k in near]
    far_pieces = swap(pieces, far)

    part, feat_own, share_own = call(
        own_kernel,
        1,
        3,
        [(8, 128), (posts, 3, filters), (posts,) + share_shape],
        [pltpu.VMEM((posts,) + pad_shape, f32), cols],
    )(lengths, pieces, weights, head_weight)

    k = 1
    while 2 * k < n_filt:
        part = part + swap(part, k, "filt")
        k *= 2
    other = swap(part, k, "filt")
    first, other = lax.optimization_barrier((first, other))
    n_facts = -(-4 * posts // 8) * 8
    facts, prediction, pack = call(
        facts_kernel,
        7,
        3,
        [(n_facts, 128), (1, posts), (seq_len + n_facts, dims)],
    )(occupation, cohort, education, wage, occ_table, cohort_table, edu_table, part, other, pieces)

    far_facts = swap(facts, far)
    packs = [swap(pack, k) for k in near]

    acc_shape = (TAPS * slice_e, filters)
    n_near = len(near)
    acc_own, acc_other, feat_far, feat_near, share_near = call(
        functools.partial(first_kernel, n_near, slice_e),
        1,
        5 + n_near + 2,
        [acc_shape, acc_shape, (posts, 8, filters), (n_near, 8, filters), (n_near,) + share_shape],
        [pltpu.VMEM((n_near,) + pad_shape, f32), pltpu.VMEM(share_shape, f32), cols],
    )(me, share_own, facts, pieces, far_pieces, far_facts, *first, weights, head_weight)
    acc_own, acc_other, sums = call(
        functools.partial(last_kernel, n_near, sizes, slice_e),
        1,
        3 + 2 * n_near + 5 + 2,
        [acc_shape, acc_shape, (-(-(3 + code_rows(sizes, filters)) // 8) * 8, filters)],
        [
            pltpu.VMEM((2 * n_near,) + pad_shape, f32),
            pltpu.VMEM((n_near, n_facts, dims), f32),
            pltpu.VMEM((n_near, 8, filters), f32),
            pltpu.VMEM(share_shape, f32),
            cols,
        ],
    )(
        me,
        acc_own,
        acc_other,
        share_near,
        *first,
        *packs,
        facts,
        far_facts,
        feat_own,
        feat_far,
        feat_near,
        weights,
        head_weight,
    )

    head_grad, *codes = call(
        functools.partial(sums_kernel, sizes),
        0,
        2,
        [(3, filters)] + [(1, size) for size in sizes],
    )(sums, swap(sums, 1))
    codes = [code.reshape(size) for code, size in zip(codes, sizes)]
    (grad,) = call(add_kernel, 0, 2, [acc_shape])(acc_own, swap(acc_other, 1))
    conv_grad = jnp.transpose(grad.reshape(TAPS, slice_e, filters), (1, 0, 2))
    return (conv_grad, head_grad, *codes, prediction.reshape(posts))


def solution(mesh):
    n_doc, n_filt = mesh.shape["doc"], mesh.shape["filt"]
    if n_doc == 8 and n_filt in (2, 4):
        local = functools.partial(local_gather, n_doc, n_filt)
    else:
        local = local_scatter
    return jax.shard_map(
        local,
        mesh=mesh,
        in_specs=(
            P("doc", None, None),
            P("doc"),
            P(None, None, "filt"),
            P(None, "filt"),
            P("doc"),
            P("doc"),
            P("doc"),
            P(),
            P(),
            P(),
            P("doc"),
        ),
        out_specs=(P("doc", None, "filt"), P(None, "filt"), P(), P(), P(), P("doc")),
        check_vma=False,
    )
```

```python
import functools

import jax
import jax.numpy as jnp
import numpy as np
from jax import lax
from jax.experimental import pallas as pl
from jax.experimental.pallas import tpu as pltpu
from jax.sharding import PartitionSpec as P

TAU = 0.05
WIDTH_LIST = ((3, 0), (5, 3), (7, 8))
TAPS = 15
REACH = 3
PAD = 8
OUTSIDE = np.float32(1024.0)
BY_LAST = (((1,), (1,)), ((), ()))


def convolve(columns, weights):
    outputs = []
    for taps, first in WIDTH_LIST:
        half = (taps - 1) // 2
        window = columns[:, :, 3 - half : 3 + half + 1, :]
        outputs.append(
            jnp.einsum(
                "ptje,ejf->ptf",
                window,
                weights[:, first : first + taps, :],
                preferred_element_type=jnp.float32,
            )
        )
    return tuple(outputs)


def grad_terms(columns, slopes):
    outputs = []
    for index in range(3):
        taps = WIDTH_LIST[index][0]
        half = (taps - 1) // 2
        window = columns[:, :, 3 - half : 3 + half + 1, :]
        outputs.append(
            jnp.einsum("ptje,ptf->ejf", window, slopes[index], preferred_element_type=jnp.float32)
        )
    return jnp.concatenate(outputs, axis=1)


def one_hots(codes, size):
    return (codes[:, None] == jnp.arange(size, dtype=jnp.int32)[None, :]).astype(jnp.float32)


def local_scatter(
    embedded,
    lengths,
    conv_weight,
    head_weight,
    occupation,
    cohort,
    education,
    occ_table,
    cohort_table,
    edu_table,
    wage,
):
    posts, seq_len, _ = embedded.shape
    positions = jnp.arange(seq_len, dtype=jnp.int32)
    valid = positions[None, :] < lengths[:, None]
    masked = jnp.where(valid[:, :, None], embedded, jnp.zeros_like(embedded))
    padded = jnp.pad(masked, ((0, 0), (3, 3), (0, 0)))
    columns = jnp.stack([padded[:, offset : offset + seq_len, :] for offset in range(7)], axis=2)
    convs = convolve(columns, conv_weight)
    features = []
    shares = []
    for conv in convs:
        score = jnp.where(valid[:, :, None], conv / TAU, -jnp.inf)
        top = jnp.max(score, axis=1, keepdims=True)
        expd = jnp.exp(score - top)
        total = jnp.sum(expd, axis=1, keepdims=True)
        features.append(TAU * (top[:, 0, :] + jnp.log(total[:, 0, :])))
        shares.append(expd / total)
    feature = jnp.stack(features, axis=1)
    head = head_weight.astype(jnp.float32)
    partial_pred = jnp.sum(feature * head[None, :, :], axis=(1, 2))
    occ_hot = one_hots(occupation, occ_table.shape[0])
    cohort_hot = one_hots(cohort, cohort_table.shape[0])
    edu_hot = one_hots(education, edu_table.shape[0])
    highest = lax.Precision.HIGHEST
    offsets = (
        jnp.dot(occ_hot, occ_table, precision=highest)
        + jnp.dot(cohort_hot, cohort_table, precision=highest)
        + jnp.dot(edu_hot, edu_table, precision=highest)
    )
    prediction = lax.psum(partial_pred, "filt") + offsets
    residual = prediction - wage
    slopes = [
        (residual[:, None, None] * head[index][None, None, :] * shares[index]).astype(jnp.bfloat16)
        for index in range(3)
    ]
    conv_grad = lax.psum_scatter(
        grad_terms(columns, slopes), "doc", scatter_dimension=0, tiled=True
    )
    head_terms = jnp.sum(residual[:, None, None] * feature, axis=0)
    head_grad, occ_grad, cohort_grad, edu_grad = lax.psum(
        (
            head_terms,
            jnp.dot(residual, occ_hot, precision=highest),
            jnp.dot(residual, cohort_hot, precision=highest),
            jnp.dot(residual, edu_hot, precision=highest),
        ),
        "doc",
    )
    return (conv_grad, head_grad, occ_grad, cohort_grad, edu_grad, prediction)


def load_post(x, xpad, count):
    rows, width = x.shape
    inside = x < OUTSIDE
    xpad[0:PAD, :] = jnp.zeros((PAD, width), jnp.float32)
    xpad[PAD + rows :, :] = jnp.zeros((PAD, width), jnp.float32)
    xpad[PAD : PAD + rows, :] = jnp.where(inside, x, 0.0)
    total = jnp.sum(inside.astype(jnp.float32), axis=0, keepdims=True)
    count[...] = jnp.broadcast_to(total[:, 0:1], count.shape)


def make_cols(xpad, cols):
    rows, width = cols.shape[0], xpad.shape[1]
    for offset in range(2 * REACH + 1):
        start = PAD - REACH + offset
        cols[:, offset * width : (offset + 1) * width] = xpad[start : start + rows, :].astype(
            jnp.bfloat16
        )


def forward(index, cols, w_ref, head, count):
    taps, first = WIDTH_LIST[index]
    half = taps // 2
    width = w_ref.shape[0] // TAPS
    conv = jnp.dot(
        cols[:, (REACH - half) * width : (REACH + half + 1) * width],
        w_ref[first * width : (first + taps) * width, :],
        preferred_element_type=jnp.float32,
    )
    place = lax.broadcasted_iota(jnp.int32, conv.shape, 0).astype(jnp.float32)
    score = jnp.where(place < count[0:1, :], conv * np.float32(1.0 / TAU), -jnp.inf)
    top = jnp.max(score, axis=0, keepdims=True)
    expd = jnp.exp(score - top)
    total = jnp.sum(expd, axis=0, keepdims=True)
    feature = np.float32(TAU) * (top + jnp.log(total))
    return feature, expd * (head[index : index + 1] / total)


def pick_rows(d_ref, middle, slice_e):
    rows, width = middle.shape
    me = d_ref[0]
    row = lax.broadcasted_iota(jnp.int32, (2 * slice_e, width), 0)
    lane = lax.broadcasted_iota(jnp.int32, (2 * slice_e, width), 1)
    wanted = jnp.where(row < slice_e, me * slice_e + row, (me ^ 1) * slice_e + row - slice_e)
    pick = (lane == wanted).astype(jnp.bfloat16)
    across = lax.dot_general(pick, middle, BY_LAST, preferred_element_type=jnp.float32)
    place = lax.broadcasted_iota(jnp.int32, (2 * slice_e, rows), 1)
    parts = []
    for offset in range(-REACH, REACH + 1):
        if offset:
            moved = pltpu.roll(across, (-offset) % rows, 1)
            inside = (place + offset >= 0) & (place + offset < rows)
            parts.append(jnp.where(inside, moved, 0.0))
        else:
            parts.append(across)
    return jnp.concatenate(parts, axis=0).astype(jnp.bfloat16)


def middle_of(cols):
    width = cols.shape[1] // (2 * REACH + 1)
    return cols[:, REACH * width : (REACH + 1) * width]


def add_terms(at, slopes, acc_own, acc_other, slice_e, fresh=False):
    step = 2 * slice_e
    for index, (taps, first) in enumerate(WIDTH_LIST):
        half = taps // 2
        term = jnp.dot(
            at[(REACH - half) * step : (REACH + half + 1) * step],
            slopes[index],
            preferred_element_type=jnp.float32,
        )
        for j in range(taps):
            place = slice((first + j) * slice_e, (first + j + 1) * slice_e)
            own = term[j * step : j * step + slice_e]
            other = term[j * step + slice_e : (j + 1) * step]
            if fresh:
                acc_own[place, :] = own
                acc_other[place, :] = other
            else:
                acc_own[place, :] += own
                acc_other[place, :] += other


def mask_kernel(len_any, x_any, pieces, x_ref, len_ref, sems):
    posts, rows, width = x_ref.shape
    copies = [pltpu.make_async_copy(len_any, len_ref, sems.at[posts])]
    copies += [pltpu.make_async_copy(x_any.at[p], x_ref.at[p], sems.at[p]) for p in range(posts)]
    for copy in copies:
        copy.start()
    place = lax.broadcasted_iota(jnp.int32, (rows, width), 0)
    copies[0].wait()
    for p in range(posts):
        copies[1 + p].wait()
        pieces[p] = jnp.where(place < len_ref[p], x_ref[p].astype(jnp.float32), OUTSIDE)


def own_kernel(*refs):
    small = refs[:8]
    w_any, pieces, part_ref, feat_ref, share_ref, base_ref = refs[8:14]
    held = refs[14:22]
    w_ref, xpad, cols, counts, small_sems, w_sems = refs[22:]
    posts = pieces.shape[0]
    width = w_ref.shape[0] // TAPS
    loads = []
    for tap in range(TAPS):
        place = pl.ds(tap * width, width)
        loads.append(pltpu.make_async_copy(w_any.at[place], w_ref.at[place], w_sems.at[tap]))
    copies = [pltpu.make_async_copy(small[i], held[i], small_sems.at[i]) for i in range(8)]
    for load in loads[::-1]:
        load.start()
    for copy in copies:
        copy.start()
    for p in range(posts):
        load_post(pieces[p], xpad.at[p], counts.at[p])
        make_cols(xpad.at[p], cols.at[p])
    copies[7].wait()
    head = held[7][...].astype(jnp.float32)
    parts = [jnp.zeros((1, head.shape[1]), jnp.float32) for _ in range(posts)]
    for index in (2, 1, 0):
        taps, first = WIDTH_LIST[index]
        for load in loads[first : first + taps]:
            load.wait()
        for p in range(posts):
            feature, share = forward(index, cols.at[p], w_ref, head, counts.at[p])
            feat_ref[p, index : index + 1, :] = feature
            share_ref[p, index] = share
            parts[p] = parts[p] + feature * head[index : index + 1]
    lanes = part_ref.shape[1]
    part_ref[...] = jnp.zeros_like(part_ref)
    for p in range(posts):
        total = jnp.sum(parts[p], axis=1, keepdims=True)
        part_ref[p : p + 1, :] = jnp.broadcast_to(total, (1, lanes))
    for copy in copies[:7]:
        copy.wait()
    codes, wage_ref, tables = held[:3], held[3], held[4:7]
    base_ref[...] = jnp.zeros_like(base_ref)
    for p in range(posts):
        offset = sum(table[code[p]] for code, table in zip(codes, tables))
        values = [offset] + [code[p].astype(jnp.float32) for code in codes] + [wage_ref[p]]
        for kind, value in enumerate(values):
            row = kind * posts + p
            base_ref[row : row + 1, :] = jnp.full((1, lanes), value, jnp.float32)


def own_terms_kernel(slice_e, d_ref, pieces, share_ref, own_ref, other_ref):
    for p in range(pieces.shape[0]):
        x = pieces[p]
        at = pick_rows(d_ref, jnp.where(x < OUTSIDE, x, 0.0).astype(jnp.bfloat16), slice_e)
        slopes = [share_ref[p, index].astype(jnp.bfloat16) for index in range(3)]
        add_terms(at, slopes, own_ref.at[p], other_ref.at[p], slice_e, fresh=True)


def facts_kernel(one, two, base, keep_own, keep_other, facts_ref, pred_ref):
    posts = pred_ref.shape[0]
    facts_ref[...] = base[...]
    for p in range(posts):
        value = one[p : p + 1, :] + two[p : p + 1, :] + base[p : p + 1, :]
        pred_ref[pl.ds(p, 1)] = value[0, 0:1]
        facts_ref[p : p + 1, :] = value - base[4 * posts + p : 4 * posts + p + 1, :]


def first_kernel(n_near, slice_e, d_ref, terms_own, terms_other, facts, *refs):
    near = refs[:n_near]
    w_ref, head_ref, acc_own, acc_other, feat_near, near_own, near_other = refs[n_near : n_near + 7]
    xs, sems, xpads, counts, cols = refs[n_near + 7 :]
    posts = terms_own.shape[0]
    copies = []
    for k in range(n_near):
        for p in range(posts):
            i = k * posts + p
            copies.append(pltpu.make_async_copy(near[k].at[p], xs.at[i], sems.at[i]))
            copies[-1].start()
    head = head_ref[...].astype(jnp.float32)
    for acc, terms in ((acc_own, terms_own), (acc_other, terms_other)):
        acc[...] = sum(facts[p : p + 1, 0:1] * terms[p] for p in range(posts))
    for i, copy in enumerate(copies):
        copy.wait()
        load_post(xs[i], xpads.at[i], counts.at[i])

    def near_posts(k, carry):
        for p in range(posts):
            make_cols(xpads.at[k * posts + p], cols.at[p])
        for p in range(posts):
            i = k * posts + p
            slopes = []
            for index in range(3):
                feature, share = forward(index, cols.at[p], w_ref, head, counts.at[i])
                feat_near[i, index : index + 1, :] = feature
                slopes.append(share.astype(jnp.bfloat16))
            at = pick_rows(d_ref, middle_of(cols.at[p]), slice_e)
            add_terms(at, slopes, near_own.at[i], near_other.at[i], slice_e, fresh=True)
        return carry

    lax.fori_loop(0, n_near, near_posts, 0)


def last_kernel(n_near, sizes, slice_e, d_ref, in_own, in_other, near_own, near_other, *refs):
    near_facts = refs[:n_near]
    facts, far_facts, feat_own, feat_near, far = refs[n_near : n_near + 5]
    w_ref, head_ref, acc_own, acc_other = refs[n_near + 5 : n_near + 9]
    xs, sems, xpads, counts, cols = refs[n_near + 9 :]
    posts = feat_own.shape[0]
    copies = []
    for p in range(posts):
        copies.append(pltpu.make_async_copy(far.at[p], xs.at[p], sems.at[p]))
        copies[-1].start()
    n_rows, filters = in_own.shape
    head = head_ref[...].astype(jnp.float32)
    for acc, start, terms in ((acc_own, in_own, near_own), (acc_other, in_other, near_other)):
        total = start[...]
        for k in range(n_near):
            for p in range(posts):
                total = total + near_facts[k][p : p + 1, 0:1] * terms[k * posts + p]
        acc[0:n_rows, :] = total

    for p in range(posts):
        copies[p].wait()
        load_post(xs[p], xpads.at[p], counts.at[p])
        make_cols(xpads.at[p], cols.at[p])
    slopes = [[], [], []]
    feat_far = [[], []]
    for p in range(posts):
        for index in range(3):
            feature, share = forward(index, cols.at[p], w_ref, head, counts.at[p])
            feat_far[p].append(feature)
            slopes[index].append((far_facts[p : p + 1, 0:1] * share).astype(jnp.bfloat16))
    at = jnp.concatenate([pick_rows(d_ref, middle_of(cols.at[p]), slice_e) for p in range(posts)], axis=1)
    slopes = [jnp.concatenate(parts, axis=0) for parts in slopes]
    add_terms(at, slopes, acc_own, acc_other, slice_e)

    n_codes = code_rows(sizes, filters)
    place = lax.broadcasted_iota(jnp.int32, (n_codes, filters), 0) * filters
    place = place + lax.broadcasted_iota(jnp.int32, (n_codes, filters), 1)

    def chip_terms(told, feature):
        head_term = jnp.zeros((3, filters), jnp.float32)
        code_term = jnp.zeros((n_codes, filters), jnp.float32)
        for p in range(posts):
            residual = told[p : p + 1, 0:1]
            head_term = head_term + residual * feature[p]
            for kind, start in enumerate(code_starts(sizes, filters)):
                at_row = (kind + 1) * posts + p
                code = told[at_row : at_row + 1, 0:1].astype(jnp.int32) + start
                code_term = code_term + jnp.where(place == code, residual, 0.0)
        return head_term, code_term

    terms = [
        chip_terms(facts[...], [feat_own[p] for p in range(posts)]),
        *[
            chip_terms(
                near_facts[k][...], [feat_near[k * posts + p, 0:3, :] for p in range(posts)]
            )
            for k in range(n_near)
        ],
        chip_terms(far_facts[...], [jnp.concatenate(parts, axis=0) for parts in feat_far]),
    ]
    acc_other[n_rows:, :] = jnp.zeros((acc_other.shape[0] - n_rows, filters), jnp.float32)
    acc_other[n_rows : n_rows + 3, :] = tree_sum([term[0] for term in terms])
    acc_other[n_rows + 3 : n_rows + 3 + n_codes, :] = tree_sum([term[1] for term in terms])


def tree_sum(values):
    while len(values) > 1:
        values = [values[i] + values[i + 1] for i in range(0, len(values), 2)]
    return values[0]


def code_starts(sizes, filters):
    starts, start = [], 0
    for size in sizes:
        starts.append(start)
        start += -(-size // filters) * filters
    return starts


def code_rows(sizes, filters):
    return sum(-(-size // filters) for size in sizes)


def swap_kernel(sizes, own_ref, mine_ref, came_ref, grad_ref, head_ref, *code_refs):
    n_rows, filters = own_ref.shape
    grad_ref[...] = own_ref[...] + came_ref[0:n_rows, :]
    head_ref[...] = mine_ref[n_rows : n_rows + 3, :] + came_ref[n_rows : n_rows + 3, :]
    row = n_rows + 3
    for size, ref in zip(sizes, code_refs):
        for start in range(0, size, filters):
            count = min(filters, size - start)
            total = mine_ref[row : row + 1, :] + came_ref[row : row + 1, :]
            ref[pl.ds(start, count)] = total[0, :count]
            row += 1


def local_gather(n_doc, n_filt, *args):
    (
        embedded,
        lengths,
        conv_weight,
        head_weight,
        occupation,
        cohort,
        education,
        occ_table,
        cohort_table,
        edu_table,
        wage,
    ) = args
    posts, seq_len, dims = embedded.shape
    filters = conv_weight.shape[2]
    slice_e = dims // n_doc
    sizes = (occ_table.shape[0], cohort_table.shape[0], edu_table.shape[0])
    f32, i32 = jnp.float32, jnp.int32
    me = lax.axis_index("doc").astype(i32).reshape(1)
    vmem = pl.BlockSpec(memory_space=pltpu.VMEM)
    smem = pl.BlockSpec(memory_space=pltpu.SMEM)
    anywhere = pl.BlockSpec(memory_space=pl.ANY)
    hbm = pl.BlockSpec(memory_space=pltpu.HBM)

    def arrived_scratch(n):
        return [pltpu.VMEM((n, seq_len, dims), f32), pltpu.SemaphoreType.DMA((n,))]

    def posts_scratch(n):
        return [
            pltpu.VMEM((n, seq_len + 2 * PAD, dims), f32),
            pltpu.VMEM((n, 8, filters), f32),
            pltpu.VMEM((posts, seq_len, (2 * REACH + 1) * dims), jnp.bfloat16),
        ]

    def swap(x, k, axis="doc"):
        size = n_doc if axis == "doc" else n_filt
        return lax.ppermute(x, axis, [(i, i ^ k) for i in range(size)])

    def call(kernel, specs, out, scratch=()):
        def run(*operands):
            operands = [
                pltpu.with_memory_space_constraint(x, pltpu.HBM) if spec is hbm else x
                for x, spec in zip(operands, specs)
            ]
            return built(*operands)

        built = pl.pallas_call(
            kernel,
            in_specs=specs,
            out_specs=[vmem] * len(out),
            out_shape=[jax.ShapeDtypeStruct(shape, f32) for shape in out],
            scratch_shapes=list(scratch),
            compiler_params=pltpu.CompilerParams(vmem_limit_bytes=24 << 20),
            cost_estimate=pl.CostEstimate(flops=1, bytes_accessed=1, transcendentals=0),
        )
        return run

    weights = jnp.transpose(conv_weight, (1, 0, 2)).reshape(TAPS * dims, filters)
    (pieces,) = call(
        mask_kernel,
        [hbm] * 2,
        [(posts, seq_len, dims)],
        [
            pltpu.VMEM((posts, seq_len, dims), jnp.bfloat16),
            pltpu.SMEM((posts,), i32),
            pltpu.SemaphoreType.DMA((posts + 1,)),
        ],
    )(lengths, embedded)

    near = [k for k in range(2, n_doc, 2) if bin(k).count("1") == 1][::-1]
    far = sum(near)
    n_near = len(near)
    near_pieces = [swap(pieces, k) for k in near]
    far_pieces = swap(pieces, far)

    n_facts = -(-5 * posts // 8) * 8
    part, feat_own, share_own, base = call(
        own_kernel,
        [hbm] * 9 + [vmem],
        [(8, 128), (posts, 3, filters), (posts, 3, seq_len, filters), (n_facts, 128)],
        [pltpu.SMEM((posts,), i32)] * 3
        + [pltpu.SMEM((posts,), f32)]
        + [pltpu.SMEM((size,), f32) for size in sizes]
        + [pltpu.VMEM(head_weight.shape, head_weight.dtype)]
        + [pltpu.VMEM(weights.shape, weights.dtype)]
        + [posts_scratch(posts)[i] for i in (0, 2, 1)]
        + [pltpu.SemaphoreType.DMA((8,)), pltpu.SemaphoreType.DMA((TAPS,))],
    )(
        occupation,
        cohort,
        education,
        wage,
        occ_table,
        cohort_table,
        edu_table,
        head_weight,
        weights,
        pieces,
    )
    acc_shape = (TAPS * slice_e, filters)
    terms_own, terms_other = call(
        functools.partial(own_terms_kernel, slice_e),
        [smem] + [vmem] * 2,
        [(posts,) + acc_shape] * 2,
    )(me, pieces, share_own)

    k = 1
    while 2 * k < n_filt:
        part = part + swap(part, k, "filt")
        part, terms_own, terms_other = lax.optimization_barrier((part, terms_own, terms_other))
        k *= 2
    other = swap(part, k, "filt")
    near_pieces, other = lax.optimization_barrier((near_pieces, other))
    facts, prediction = call(
        facts_kernel, [vmem] * 3 + [anywhere] * 2, [(n_facts, 128), (posts,)]
    )(part, other, base, terms_own, terms_other)

    near_facts = [swap(facts, k) for k in near]
    far_facts = swap(facts, far)

    near_shape = (n_near * posts,) + acc_shape
    acc_own, acc_other, feat_near, near_own, near_other = call(
        functools.partial(first_kernel, n_near, slice_e),
        [smem] + [vmem] * 3 + [hbm] * n_near + [vmem] * 2,
        [acc_shape, acc_shape, (n_near * posts, 8, filters), near_shape, near_shape],
        arrived_scratch(n_near * posts) + posts_scratch(n_near * posts),
    )(me, terms_own, terms_other, facts, *near_pieces, weights, head_weight)
    extra = -(-(3 + code_rows(sizes, filters)) // 8) * 8
    acc_own, acc_other = call(
        functools.partial(last_kernel, n_near, sizes, slice_e),
        [smem] + [vmem] * (4 + n_near + 4) + [hbm] + [vmem] * 2,
        [acc_shape, (acc_shape[0] + extra, filters)],
        arrived_scratch(posts) + posts_scratch(posts),
    )(
        me,
        acc_own,
        acc_other,
        near_own,
        near_other,
        *near_facts,
        facts,
        far_facts,
        feat_own,
        feat_near,
        far_pieces,
        weights,
        head_weight,
    )

    grad, head_grad, *codes = call(
        functools.partial(swap_kernel, sizes),
        [vmem] * 3,
        [acc_shape, (3, filters)] + [(size,) for size in sizes],
    )(acc_own, acc_other, swap(acc_other, 1))
    conv_grad = jnp.transpose(grad.reshape(TAPS, slice_e, filters), (1, 0, 2))
    return (conv_grad, head_grad, *codes, prediction)


def solution(mesh):
    n_doc, n_filt = mesh.shape["doc"], mesh.shape["filt"]
    if n_doc == 8 and n_filt in (2, 4):
        local = functools.partial(local_gather, n_doc, n_filt)
    else:
        local = local_scatter
    return jax.shard_map(
        local,
        mesh=mesh,
        in_specs=(
            P("doc", None, None),
            P("doc"),
            P(None, None, "filt"),
            P(None, "filt"),
            P("doc"),
            P("doc"),
            P("doc"),
            P(),
            P(),
            P(),
            P("doc"),
        ),
        out_specs=(P("doc", None, "filt"), P(None, "filt"), P(), P(), P(), P("doc")),
        check_vma=False,
    )
```

```python
import functools

import jax
import jax.numpy as jnp
import numpy as np
from jax import lax
from jax.experimental import pallas as pl
from jax.experimental.pallas import tpu as pltpu
from jax.sharding import PartitionSpec as P

TAU = 0.05
WIDTH_LIST = ((3, 0), (5, 3), (7, 8))
TAPS = 15
REACH = 3
PAD = 8
OUTSIDE = np.float32(1024.0)
BY_LAST = (((1,), (1,)), ((), ()))


def convolve(columns, weights):
    outputs = []
    for taps, first in WIDTH_LIST:
        half = (taps - 1) // 2
        window = columns[:, :, 3 - half : 3 + half + 1, :]
        outputs.append(
            jnp.einsum(
                "ptje,ejf->ptf",
                window,
                weights[:, first : first + taps, :],
                preferred_element_type=jnp.float32,
            )
        )
    return tuple(outputs)


def grad_terms(columns, slopes):
    outputs = []
    for index in range(3):
        taps = WIDTH_LIST[index][0]
        half = (taps - 1) // 2
        window = columns[:, :, 3 - half : 3 + half + 1, :]
        outputs.append(
            jnp.einsum("ptje,ptf->ejf", window, slopes[index], preferred_element_type=jnp.float32)
        )
    return jnp.concatenate(outputs, axis=1)


def one_hots(codes, size):
    return (codes[:, None] == jnp.arange(size, dtype=jnp.int32)[None, :]).astype(jnp.float32)


def local_scatter(
    embedded,
    lengths,
    conv_weight,
    head_weight,
    occupation,
    cohort,
    education,
    occ_table,
    cohort_table,
    edu_table,
    wage,
):
    posts, seq_len, _ = embedded.shape
    positions = jnp.arange(seq_len, dtype=jnp.int32)
    valid = positions[None, :] < lengths[:, None]
    masked = jnp.where(valid[:, :, None], embedded, jnp.zeros_like(embedded))
    padded = jnp.pad(masked, ((0, 0), (3, 3), (0, 0)))
    columns = jnp.stack([padded[:, offset : offset + seq_len, :] for offset in range(7)], axis=2)
    convs = convolve(columns, conv_weight)
    features = []
    shares = []
    for conv in convs:
        score = jnp.where(valid[:, :, None], conv / TAU, -jnp.inf)
        top = jnp.max(score, axis=1, keepdims=True)
        expd = jnp.exp(score - top)
        total = jnp.sum(expd, axis=1, keepdims=True)
        features.append(TAU * (top[:, 0, :] + jnp.log(total[:, 0, :])))
        shares.append(expd / total)
    feature = jnp.stack(features, axis=1)
    head = head_weight.astype(jnp.float32)
    partial_pred = jnp.sum(feature * head[None, :, :], axis=(1, 2))
    occ_hot = one_hots(occupation, occ_table.shape[0])
    cohort_hot = one_hots(cohort, cohort_table.shape[0])
    edu_hot = one_hots(education, edu_table.shape[0])
    highest = lax.Precision.HIGHEST
    offsets = (
        jnp.dot(occ_hot, occ_table, precision=highest)
        + jnp.dot(cohort_hot, cohort_table, precision=highest)
        + jnp.dot(edu_hot, edu_table, precision=highest)
    )
    prediction = lax.psum(partial_pred, "filt") + offsets
    residual = prediction - wage
    slopes = [
        (residual[:, None, None] * head[index][None, None, :] * shares[index]).astype(jnp.bfloat16)
        for index in range(3)
    ]
    conv_grad = lax.psum_scatter(
        grad_terms(columns, slopes), "doc", scatter_dimension=0, tiled=True
    )
    head_terms = jnp.sum(residual[:, None, None] * feature, axis=0)
    head_grad, occ_grad, cohort_grad, edu_grad = lax.psum(
        (
            head_terms,
            jnp.dot(residual, occ_hot, precision=highest),
            jnp.dot(residual, cohort_hot, precision=highest),
            jnp.dot(residual, edu_hot, precision=highest),
        ),
        "doc",
    )
    return (conv_grad, head_grad, occ_grad, cohort_grad, edu_grad, prediction)


def load_post(x, xpad, count):
    rows, width = x.shape
    inside = x < OUTSIDE
    xpad[0:PAD, :] = jnp.zeros((PAD, width), jnp.float32)
    xpad[PAD + rows :, :] = jnp.zeros((PAD, width), jnp.float32)
    xpad[PAD : PAD + rows, :] = jnp.where(inside, x, 0.0)
    total = jnp.sum(inside.astype(jnp.float32), axis=0, keepdims=True)
    count[...] = jnp.broadcast_to(total[:, 0:1], count.shape)


def make_cols(xpad, cols):
    rows, width = cols.shape[0], xpad.shape[1]
    for offset in range(2 * REACH + 1):
        start = PAD - REACH + offset
        cols[:, offset * width : (offset + 1) * width] = xpad[start : start + rows, :].astype(
            jnp.bfloat16
        )


def forward(index, cols, w_ref, head, count):
    taps, first = WIDTH_LIST[index]
    half = taps // 2
    width = w_ref.shape[0] // TAPS
    conv = jnp.dot(
        cols[:, (REACH - half) * width : (REACH + half + 1) * width],
        w_ref[first * width : (first + taps) * width, :],
        preferred_element_type=jnp.float32,
    )
    place = lax.broadcasted_iota(jnp.int32, conv.shape, 0).astype(jnp.float32)
    score = jnp.where(place < count[0:1, :], conv * np.float32(1.0 / TAU), -jnp.inf)
    top = jnp.max(score, axis=0, keepdims=True)
    expd = jnp.exp(score - top)
    total = jnp.sum(expd, axis=0, keepdims=True)
    feature = np.float32(TAU) * (top + jnp.log(total))
    return feature, expd * (head[index : index + 1] / total)


def pick_rows(d_ref, middle, slice_e):
    rows, width = middle.shape
    me = d_ref[0]
    row = lax.broadcasted_iota(jnp.int32, (2 * slice_e, width), 0)
    lane = lax.broadcasted_iota(jnp.int32, (2 * slice_e, width), 1)
    wanted = jnp.where(row < slice_e, me * slice_e + row, (me ^ 1) * slice_e + row - slice_e)
    pick = (lane == wanted).astype(jnp.bfloat16)
    across = lax.dot_general(pick, middle, BY_LAST, preferred_element_type=jnp.float32)
    place = lax.broadcasted_iota(jnp.int32, (2 * slice_e, rows), 1)
    parts = []
    for offset in range(-REACH, REACH + 1):
        if offset:
            moved = pltpu.roll(across, (-offset) % rows, 1)
            inside = (place + offset >= 0) & (place + offset < rows)
            parts.append(jnp.where(inside, moved, 0.0))
        else:
            parts.append(across)
    return jnp.concatenate(parts, axis=0).astype(jnp.bfloat16)


def middle_of(cols):
    width = cols.shape[1] // (2 * REACH + 1)
    return cols[:, REACH * width : (REACH + 1) * width]


def add_terms(at, slopes, acc_own, acc_other, slice_e, fresh=False):
    step = 2 * slice_e
    for index, (taps, first) in enumerate(WIDTH_LIST):
        half = taps // 2
        term = jnp.dot(
            at[(REACH - half) * step : (REACH + half + 1) * step],
            slopes[index],
            preferred_element_type=jnp.float32,
        )
        for j in range(taps):
            place = slice((first + j) * slice_e, (first + j + 1) * slice_e)
            own = term[j * step : j * step + slice_e]
            other = term[j * step + slice_e : (j + 1) * step]
            if fresh:
                acc_own[place, :] = own
                acc_other[place, :] = other
            else:
                acc_own[place, :] += own
                acc_other[place, :] += other


def mask_kernel(d_ref, len_any, x_any, pieces, x_ref, len_ref, sems):
    posts, rows, width = x_ref.shape
    copies = [pltpu.make_async_copy(len_any, len_ref, sems.at[posts])]
    copies += [pltpu.make_async_copy(x_any.at[p], x_ref.at[p], sems.at[p]) for p in range(posts)]
    for copy in copies:
        copy.start()
    place = lax.broadcasted_iota(jnp.int32, (rows, width), 0)
    copies[0].wait()
    for p in range(posts):
        copies[1 + p].wait()
        pieces[p] = jnp.where(place < len_ref[p], x_ref[p].astype(jnp.float32), OUTSIDE)


def own_kernel(*refs):
    small = refs[:8]
    w_any, pieces, part_ref, feat_ref, share_ref, base_ref = refs[8:14]
    held = refs[14:22]
    w_ref, xpad, cols, counts, small_sems, w_sems = refs[22:]
    posts = pieces.shape[0]
    width = w_ref.shape[0] // TAPS
    loads = []
    for tap in range(TAPS):
        place = pl.ds(tap * width, width)
        loads.append(pltpu.make_async_copy(w_any.at[place], w_ref.at[place], w_sems.at[tap]))
    copies = [pltpu.make_async_copy(small[i], held[i], small_sems.at[i]) for i in range(8)]
    for load in loads[::-1]:
        load.start()
    for copy in copies:
        copy.start()
    for p in range(posts):
        load_post(pieces[p], xpad.at[p], counts.at[p])
        make_cols(xpad.at[p], cols.at[p])
    copies[7].wait()
    head = held[7][...].astype(jnp.float32)
    parts = [jnp.zeros((1, head.shape[1]), jnp.float32) for _ in range(posts)]
    for index in (2, 1, 0):
        taps, first = WIDTH_LIST[index]
        for load in loads[first : first + taps]:
            load.wait()
        for p in range(posts):
            feature, share = forward(index, cols.at[p], w_ref, head, counts.at[p])
            feat_ref[p, index : index + 1, :] = feature
            share_ref[p, index] = share
            parts[p] = parts[p] + feature * head[index : index + 1]
    lanes = part_ref.shape[1]
    part_ref[...] = jnp.zeros_like(part_ref)
    for p in range(posts):
        total = jnp.sum(parts[p], axis=1, keepdims=True)
        part_ref[p : p + 1, :] = jnp.broadcast_to(total, (1, lanes))
    for copy in copies[:7]:
        copy.wait()
    codes, wage_ref, tables = held[:3], held[3], held[4:7]
    base_ref[...] = jnp.zeros_like(base_ref)
    for p in range(posts):
        offset = sum(table[code[p]] for code, table in zip(codes, tables))
        values = [offset] + [code[p].astype(jnp.float32) for code in codes] + [wage_ref[p]]
        for kind, value in enumerate(values):
            row = kind * posts + p
            base_ref[row : row + 1, :] = jnp.full((1, lanes), value, jnp.float32)


def own_terms_kernel(slice_e, d_ref, pieces, share_ref, own_ref, other_ref):
    for p in range(pieces.shape[0]):
        x = pieces[p]
        at = pick_rows(d_ref, jnp.where(x < OUTSIDE, x, 0.0).astype(jnp.bfloat16), slice_e)
        slopes = [share_ref[p, index].astype(jnp.bfloat16) for index in range(3)]
        add_terms(at, slopes, own_ref.at[p], other_ref.at[p], slice_e, fresh=True)


def facts_kernel(n_keep, one, two, base, *refs):
    facts_ref, pred_ref = refs[n_keep:]
    posts = pred_ref.shape[0]
    facts_ref[...] = base[...]
    for p in range(posts):
        value = one[p : p + 1, :] + two[p : p + 1, :] + base[p : p + 1, :]
        pred_ref[pl.ds(p, 1)] = value[0, 0:1]
        facts_ref[p : p + 1, :] = value - base[4 * posts + p : 4 * posts + p + 1, :]


def near_kernel(n_keep, slice_e, d_ref, x_ref, w_ref, head_ref, *refs):
    feat_ref, own_ref, other_ref, xpads, counts, cols = refs[n_keep:]
    posts = x_ref.shape[0]
    head = head_ref[...].astype(jnp.float32)
    for p in range(posts):
        load_post(x_ref[p], xpads.at[p], counts.at[p])
        make_cols(xpads.at[p], cols.at[p])
    for p in range(posts):
        slopes = []
        for index in range(3):
            feature, share = forward(index, cols.at[p], w_ref, head, counts.at[p])
            feat_ref[p, index : index + 1, :] = feature
            slopes.append(share.astype(jnp.bfloat16))
        at = pick_rows(d_ref, middle_of(cols.at[p]), slice_e)
        add_terms(at, slopes, own_ref.at[p], other_ref.at[p], slice_e, fresh=True)


def scaled_sum(start, facts, terms):
    total = start
    for fact, term in zip(facts, terms):
        for p in range(term.shape[0]):
            total = total + fact[p : p + 1, 0:1] * term[p]
    return total


def last_kernel(n_near, sizes, slice_e, d_ref, far, *refs):
    facts = refs[: 2 + n_near]
    feats = refs[2 + n_near : 3 + 2 * n_near]
    terms = refs[3 + 2 * n_near : 4 + 3 * n_near]
    w_ref, head_ref, acc_own, acc_other, xpads, counts, cols = refs[4 + 3 * n_near :]
    posts = far.shape[0]
    n_rows, filters = acc_own.shape
    head = head_ref[...].astype(jnp.float32)
    for p in range(posts):
        load_post(far[p], xpads.at[p], counts.at[p])
        make_cols(xpads.at[p], cols.at[p])
    acc_own[...] = jnp.zeros_like(acc_own)
    acc_other[0:n_rows, :] = scaled_sum(jnp.zeros_like(acc_own), facts, terms)
    slopes = [[], [], []]
    feat_far = [[], []]
    for p in range(posts):
        for index in range(3):
            feature, share = forward(index, cols.at[p], w_ref, head, counts.at[p])
            feat_far[p].append(feature)
            slopes[index].append((facts[-1][p : p + 1, 0:1] * share).astype(jnp.bfloat16))
    at = jnp.concatenate(
        [pick_rows(d_ref, middle_of(cols.at[p]), slice_e) for p in range(posts)], axis=1
    )
    slopes = [jnp.concatenate(parts, axis=0) for parts in slopes]
    add_terms(at, slopes, acc_own, acc_other, slice_e)

    n_codes = code_rows(sizes, filters)
    place = lax.broadcasted_iota(jnp.int32, (n_codes, filters), 0) * filters
    place = place + lax.broadcasted_iota(jnp.int32, (n_codes, filters), 1)

    def chip_terms(told, feature):
        head_term = jnp.zeros((3, filters), jnp.float32)
        code_term = jnp.zeros((n_codes, filters), jnp.float32)
        for p in range(posts):
            residual = told[p : p + 1, 0:1]
            head_term = head_term + residual * feature[p]
            for kind, start in enumerate(code_starts(sizes, filters)):
                at_row = (kind + 1) * posts + p
                code = told[at_row : at_row + 1, 0:1].astype(jnp.int32) + start
                code_term = code_term + jnp.where(place == code, residual, 0.0)
        return head_term, code_term

    features = [[feat[p, 0:3, :] for p in range(posts)] for feat in feats]
    features.append([jnp.concatenate(parts, axis=0) for parts in feat_far])
    sums = [chip_terms(fact[...], feature) for fact, feature in zip(facts, features)]
    acc_other[n_rows:, :] = jnp.zeros((acc_other.shape[0] - n_rows, filters), jnp.float32)
    acc_other[n_rows : n_rows + 3, :] = tree_sum([total[0] for total in sums])
    acc_other[n_rows + 3 : n_rows + 3 + n_codes, :] = tree_sum([total[1] for total in sums])


def gather_kernel(n, acc, *refs):
    refs[-1][...] = scaled_sum(acc[...], refs[:n], refs[n : 2 * n])


def tree_sum(values):
    while len(values) > 1:
        values = [values[i] + values[i + 1] for i in range(0, len(values), 2)]
    return values[0]


def code_starts(sizes, filters):
    starts, start = [], 0
    for size in sizes:
        starts.append(start)
        start += -(-size // filters) * filters
    return starts


def code_rows(sizes, filters):
    return sum(-(-size // filters) for size in sizes)


def swap_kernel(sizes, own_ref, mine_ref, came_ref, grad_ref, head_ref, *code_refs):
    n_rows, filters = own_ref.shape
    grad_ref[...] = own_ref[...] + came_ref[0:n_rows, :]
    head_ref[...] = mine_ref[n_rows : n_rows + 3, :] + came_ref[n_rows : n_rows + 3, :]
    row = n_rows + 3
    for size, ref in zip(sizes, code_refs):
        for start in range(0, size, filters):
            count = min(filters, size - start)
            total = mine_ref[row : row + 1, :] + came_ref[row : row + 1, :]
            ref[pl.ds(start, count)] = total[0, :count]
            row += 1


def local_gather(n_doc, n_filt, *args):
    (
        embedded,
        lengths,
        conv_weight,
        head_weight,
        occupation,
        cohort,
        education,
        occ_table,
        cohort_table,
        edu_table,
        wage,
    ) = args
    posts, seq_len, dims = embedded.shape
    filters = conv_weight.shape[2]
    slice_e = dims // n_doc
    sizes = (occ_table.shape[0], cohort_table.shape[0], edu_table.shape[0])
    f32, i32 = jnp.float32, jnp.int32
    me = lax.axis_index("doc").astype(i32).reshape(1)
    vmem = pl.BlockSpec(memory_space=pltpu.VMEM)
    smem = pl.BlockSpec(memory_space=pltpu.SMEM)
    anywhere = pl.BlockSpec(memory_space=pl.ANY)
    hbm = pl.BlockSpec(memory_space=pltpu.HBM)

    def posts_scratch(n):
        return [
            pltpu.VMEM((n, seq_len + 2 * PAD, dims), f32),
            pltpu.VMEM((n, 8, filters), f32),
            pltpu.VMEM((posts, seq_len, (2 * REACH + 1) * dims), jnp.bfloat16),
        ]

    def swap(x, k, axis="doc"):
        size = n_doc if axis == "doc" else n_filt
        return lax.ppermute(x, axis, [(i, i ^ k) for i in range(size)])

    held = pl.BlockSpec(memory_space=pltpu.VMEM)
    spaces = {id(hbm): pltpu.HBM, id(held): pltpu.VMEM}

    def call(kernel, specs, out, scratch=(), stay=()):
        def run(*operands):
            operands = [
                pltpu.with_memory_space_constraint(x, spaces[id(spec)])
                if id(spec) in spaces
                else x
                for x, spec in zip(operands, specs)
            ]
            return built(*operands)

        built = pl.pallas_call(
            kernel,
            in_specs=specs,
            out_specs=[vmem] * len(out),
            out_shape=[
                pltpu.VMEM(shape, f32) if i in stay else jax.ShapeDtypeStruct(shape, f32)
                for i, shape in enumerate(out)
            ],
            scratch_shapes=list(scratch),
            compiler_params=pltpu.CompilerParams(vmem_limit_bytes=24 << 20),
            cost_estimate=pl.CostEstimate(flops=1, bytes_accessed=1, transcendentals=0),
        )
        return run

    weights = jnp.transpose(conv_weight, (1, 0, 2)).reshape(TAPS * dims, filters)
    (pieces,) = call(
        mask_kernel,
        [smem] + [hbm] * 2,
        [(posts, seq_len, dims)],
        [
            pltpu.VMEM((posts, seq_len, dims), jnp.bfloat16),
            pltpu.SMEM((posts,), i32),
            pltpu.SemaphoreType.DMA((posts + 1,)),
        ],
    )(me, lengths, embedded)

    near = [k for k in range(2, n_doc, 2) if bin(k).count("1") == 1][::-1]
    far = sum(near)
    n_near = len(near)
    near_pieces = [swap(pieces, k) for k in near]
    far_pieces = swap(pieces, far)

    n_facts = -(-5 * posts // 8) * 8
    part, feat_own, share_own, base = call(
        own_kernel,
        [hbm] * 9 + [vmem],
        [(8, 128), (posts, 3, filters), (posts, 3, seq_len, filters), (n_facts, 128)],
        [pltpu.SMEM((posts,), i32)] * 3
        + [pltpu.SMEM((posts,), f32)]
        + [pltpu.SMEM((size,), f32) for size in sizes]
        + [pltpu.VMEM(head_weight.shape, head_weight.dtype)]
        + [pltpu.VMEM(weights.shape, weights.dtype)]
        + [posts_scratch(posts)[i] for i in (0, 2, 1)]
        + [pltpu.SemaphoreType.DMA((8,)), pltpu.SemaphoreType.DMA((TAPS,))],
        stay=(2,),
    )(
        occupation,
        cohort,
        education,
        wage,
        occ_table,
        cohort_table,
        edu_table,
        head_weight,
        weights,
        pieces,
    )
    acc_shape = (TAPS * slice_e, filters)
    terms_own, terms_other = call(
        functools.partial(own_terms_kernel, slice_e),
        [smem, vmem, held],
        [(posts,) + acc_shape] * 2,
    )(me, pieces, share_own)

    terms = [(terms_own, terms_other)]
    k = 1
    while 2 * k < n_filt:
        part = part + swap(part, k, "filt")
        part, *terms[0] = lax.optimization_barrier((part, *terms[0]))
        k *= 2
    other = swap(part, k, "filt")

    def near_terms(x, keep):
        feat, *terms = call(
            functools.partial(near_kernel, len(keep), slice_e),
            [smem] + [vmem] * 3 + [anywhere] * len(keep),
            [(posts, 8, filters)] + [(posts,) + acc_shape] * 2,
            posts_scratch(posts),
        )(me, x, weights, head_weight, *keep)
        return feat, terms

    feats = [feat_own]
    feat, term = near_terms(near_pieces[0], ())
    other, feat, *term = lax.optimization_barrier((other, feat, *term))
    feats.append(feat)
    terms.append(term)
    keep = [x for pair in terms for x in pair]
    facts, prediction = call(
        functools.partial(facts_kernel, len(keep)),
        [vmem] * 3 + [anywhere] * len(keep),
        [(n_facts, 128), (posts,)],
    )(part, other, base, *keep)

    all_facts = [facts] + [swap(facts, k) for k in near] + [swap(facts, far)]
    for x in near_pieces[1:]:
        feat, term = near_terms(x, keep)
        feats.append(feat)
        terms.append(term)
    extra = -(-(3 + code_rows(sizes, filters)) // 8) * 8
    acc_own, acc_other = call(
        functools.partial(last_kernel, n_near, sizes, slice_e),
        [smem] + [vmem] * (4 + 3 * n_near + 3),
        [acc_shape, (acc_shape[0] + extra, filters)],
        posts_scratch(posts),
    )(
        me,
        far_pieces,
        *all_facts,
        *feats,
        *[pair[1] for pair in terms],
        weights,
        head_weight,
    )

    came = swap(acc_other, 1)
    (total,) = call(
        functools.partial(gather_kernel, 1 + n_near),
        [vmem] * (1 + 2 * (1 + n_near)),
        [acc_shape],
    )(acc_own, *all_facts[:-1], *[pair[0] for pair in terms])
    grad, head_grad, *codes = call(
        functools.partial(swap_kernel, sizes),
        [vmem] * 3,
        [acc_shape, (3, filters)] + [(size,) for size in sizes],
    )(total, acc_other, came)
    conv_grad = jnp.transpose(grad.reshape(TAPS, slice_e, filters), (1, 0, 2))
    return (conv_grad, head_grad, *codes, prediction)


def solution(mesh):
    n_doc, n_filt = mesh.shape["doc"], mesh.shape["filt"]
    if n_doc == 8 and n_filt in (2, 4):
        local = functools.partial(local_gather, n_doc, n_filt)
    else:
        local = local_scatter
    return jax.shard_map(
        local,
        mesh=mesh,
        in_specs=(
            P("doc", None, None),
            P("doc"),
            P(None, None, "filt"),
            P(None, "filt"),
            P("doc"),
            P("doc"),
            P("doc"),
            P(),
            P(),
            P(),
            P("doc"),
        ),
        out_specs=(P("doc", None, "filt"), P(None, "filt"), P(), P(), P(), P("doc")),
        check_vma=False,
    )
```

```python
import functools

import jax
import jax.numpy as jnp
import numpy as np
from jax import lax
from jax.experimental import pallas as pl
from jax.experimental.pallas import tpu as pltpu
from jax.sharding import PartitionSpec as P

TAU = 0.05
WIDTH_LIST = ((3, 0), (5, 3), (7, 8))
TAPS = 15
REACH = 3
PAD = 8
OUTSIDE = np.float32(1024.0)
BY_LAST = (((1,), (1,)), ((), ()))


def convolve(columns, weights):
    outputs = []
    for taps, first in WIDTH_LIST:
        half = (taps - 1) // 2
        window = columns[:, :, 3 - half : 3 + half + 1, :]
        outputs.append(
            jnp.einsum(
                "ptje,ejf->ptf",
                window,
                weights[:, first : first + taps, :],
                preferred_element_type=jnp.float32,
            )
        )
    return tuple(outputs)


def grad_terms(columns, slopes):
    outputs = []
    for index in range(3):
        taps = WIDTH_LIST[index][0]
        half = (taps - 1) // 2
        window = columns[:, :, 3 - half : 3 + half + 1, :]
        outputs.append(
            jnp.einsum("ptje,ptf->ejf", window, slopes[index], preferred_element_type=jnp.float32)
        )
    return jnp.concatenate(outputs, axis=1)


def one_hots(codes, size):
    return (codes[:, None] == jnp.arange(size, dtype=jnp.int32)[None, :]).astype(jnp.float32)


def local_scatter(
    embedded,
    lengths,
    conv_weight,
    head_weight,
    occupation,
    cohort,
    education,
    occ_table,
    cohort_table,
    edu_table,
    wage,
):
    posts, seq_len, _ = embedded.shape
    positions = jnp.arange(seq_len, dtype=jnp.int32)
    valid = positions[None, :] < lengths[:, None]
    masked = jnp.where(valid[:, :, None], embedded, jnp.zeros_like(embedded))
    padded = jnp.pad(masked, ((0, 0), (3, 3), (0, 0)))
    columns = jnp.stack([padded[:, offset : offset + seq_len, :] for offset in range(7)], axis=2)
    convs = convolve(columns, conv_weight)
    features = []
    shares = []
    for conv in convs:
        score = jnp.where(valid[:, :, None], conv / TAU, -jnp.inf)
        top = jnp.max(score, axis=1, keepdims=True)
        expd = jnp.exp(score - top)
        total = jnp.sum(expd, axis=1, keepdims=True)
        features.append(TAU * (top[:, 0, :] + jnp.log(total[:, 0, :])))
        shares.append(expd / total)
    feature = jnp.stack(features, axis=1)
    head = head_weight.astype(jnp.float32)
    partial_pred = jnp.sum(feature * head[None, :, :], axis=(1, 2))
    occ_hot = one_hots(occupation, occ_table.shape[0])
    cohort_hot = one_hots(cohort, cohort_table.shape[0])
    edu_hot = one_hots(education, edu_table.shape[0])
    highest = lax.Precision.HIGHEST
    offsets = (
        jnp.dot(occ_hot, occ_table, precision=highest)
        + jnp.dot(cohort_hot, cohort_table, precision=highest)
        + jnp.dot(edu_hot, edu_table, precision=highest)
    )
    prediction = lax.psum(partial_pred, "filt") + offsets
    residual = prediction - wage
    slopes = [
        (residual[:, None, None] * head[index][None, None, :] * shares[index]).astype(jnp.bfloat16)
        for index in range(3)
    ]
    conv_grad = lax.psum_scatter(
        grad_terms(columns, slopes), "doc", scatter_dimension=0, tiled=True
    )
    head_terms = jnp.sum(residual[:, None, None] * feature, axis=0)
    head_grad, occ_grad, cohort_grad, edu_grad = lax.psum(
        (
            head_terms,
            jnp.dot(residual, occ_hot, precision=highest),
            jnp.dot(residual, cohort_hot, precision=highest),
            jnp.dot(residual, edu_hot, precision=highest),
        ),
        "doc",
    )
    return (conv_grad, head_grad, occ_grad, cohort_grad, edu_grad, prediction)


def load_post(x, xpad, count):
    rows, width = x.shape
    inside = x < OUTSIDE
    xpad[0:PAD, :] = jnp.zeros((PAD, width), jnp.float32)
    xpad[PAD + rows :, :] = jnp.zeros((PAD, width), jnp.float32)
    xpad[PAD : PAD + rows, :] = jnp.where(inside, x, 0.0)
    total = jnp.sum(inside.astype(jnp.float32), axis=0, keepdims=True)
    count[...] = jnp.broadcast_to(total[:, 0:1], count.shape)


def make_cols(xpad, cols):
    rows, width = cols.shape[0], xpad.shape[1]
    for offset in range(2 * REACH + 1):
        start = PAD - REACH + offset
        cols[:, offset * width : (offset + 1) * width] = xpad[start : start + rows, :].astype(
            jnp.bfloat16
        )


def forward(index, cols, w_ref, head, count):
    taps, first = WIDTH_LIST[index]
    half = taps // 2
    width = w_ref.shape[0] // TAPS
    conv = jnp.dot(
        cols[:, (REACH - half) * width : (REACH + half + 1) * width],
        w_ref[first * width : (first + taps) * width, :],
        preferred_element_type=jnp.float32,
    )
    place = lax.broadcasted_iota(jnp.int32, conv.shape, 0).astype(jnp.float32)
    score = jnp.where(place < count[0:1, :], conv * np.float32(1.0 / TAU), -jnp.inf)
    top = jnp.max(score, axis=0, keepdims=True)
    expd = jnp.exp(score - top)
    total = jnp.sum(expd, axis=0, keepdims=True)
    feature = np.float32(TAU) * (top + jnp.log(total))
    return feature, expd * (head[index : index + 1] / total)


def pick_rows(d_ref, middle, slice_e):
    rows, width = middle.shape
    me = d_ref[0]
    row = lax.broadcasted_iota(jnp.int32, (2 * slice_e, width), 0)
    lane = lax.broadcasted_iota(jnp.int32, (2 * slice_e, width), 1)
    wanted = jnp.where(row < slice_e, me * slice_e + row, (me ^ 1) * slice_e + row - slice_e)
    pick = (lane == wanted).astype(jnp.bfloat16)
    across = lax.dot_general(pick, middle, BY_LAST, preferred_element_type=jnp.float32)
    place = lax.broadcasted_iota(jnp.int32, (2 * slice_e, rows), 1)
    parts = []
    for offset in range(-REACH, REACH + 1):
        if offset:
            moved = pltpu.roll(across, (-offset) % rows, 1)
            inside = (place + offset >= 0) & (place + offset < rows)
            parts.append(jnp.where(inside, moved, 0.0))
        else:
            parts.append(across)
    return jnp.concatenate(parts, axis=0).astype(jnp.bfloat16)


def middle_of(cols):
    width = cols.shape[1] // (2 * REACH + 1)
    return cols[:, REACH * width : (REACH + 1) * width]


def add_terms(at, slopes, acc_own, acc_other, slice_e, fresh=False):
    step = 2 * slice_e
    for index, (taps, first) in enumerate(WIDTH_LIST):
        half = taps // 2
        term = jnp.dot(
            at[(REACH - half) * step : (REACH + half + 1) * step],
            slopes[index],
            preferred_element_type=jnp.float32,
        )
        for j in range(taps):
            place = slice((first + j) * slice_e, (first + j + 1) * slice_e)
            own = term[j * step : j * step + slice_e]
            other = term[j * step + slice_e : (j + 1) * step]
            if fresh:
                acc_own[place, :] = own
                acc_other[place, :] = other
            else:
                acc_own[place, :] += own
                acc_other[place, :] += other


def mask_kernel(d_ref, z_ref, len_any, x_any, pieces, far_piece, x_ref, len_ref, sems):
    posts, rows, width = x_ref.shape
    copies = [pltpu.make_async_copy(len_any, len_ref, sems.at[posts])]
    copies += [pltpu.make_async_copy(x_any.at[p], x_ref.at[p], sems.at[p]) for p in range(posts)]
    for copy in copies:
        copy.start()
    place = lax.broadcasted_iota(jnp.int32, (rows, width), 0)
    copies[0].wait()
    for p in range(posts):
        copies[1 + p].wait()
        pieces[p] = jnp.where(place < len_ref[p], x_ref[p].astype(jnp.float32), OUTSIDE)
    far_piece[...] = pieces[z_ref[0]]


def own_kernel(*refs):
    small = refs[:8]
    w_any, pieces, part_ref, feat_ref, share_ref, base_ref, w_ref = refs[8:15]
    held = refs[15:23]
    xpad, cols, counts, small_sems, w_sems = refs[23:]
    posts = pieces.shape[0]
    width = w_ref.shape[0] // TAPS
    loads = []
    for tap in range(TAPS):
        place = pl.ds(tap * width, width)
        loads.append(pltpu.make_async_copy(w_any.at[place], w_ref.at[place], w_sems.at[tap]))
    copies = [pltpu.make_async_copy(small[i], held[i], small_sems.at[i]) for i in range(8)]
    for load in loads[::-1]:
        load.start()
    for copy in copies:
        copy.start()
    for p in range(posts):
        load_post(pieces[p], xpad.at[p], counts.at[p])
        make_cols(xpad.at[p], cols.at[p])
    copies[7].wait()
    head = held[7][...].astype(jnp.float32)
    parts = [jnp.zeros((1, head.shape[1]), jnp.float32) for _ in range(posts)]
    for index in (2, 1, 0):
        taps, first = WIDTH_LIST[index]
        for load in loads[first : first + taps]:
            load.wait()
        for p in range(posts):
            feature, share = forward(index, cols.at[p], w_ref, head, counts.at[p])
            feat_ref[p, index : index + 1, :] = feature
            share_ref[p, index] = share
            parts[p] = parts[p] + feature * head[index : index + 1]
    lanes = part_ref.shape[1]
    part_ref[...] = jnp.zeros_like(part_ref)
    for p in range(posts):
        total = jnp.sum(parts[p], axis=1, keepdims=True)
        part_ref[p : p + 1, :] = jnp.broadcast_to(total, (1, lanes))
    for copy in copies[:7]:
        copy.wait()
    codes, wage_ref, tables = held[:3], held[3], held[4:7]
    base_ref[...] = jnp.zeros_like(base_ref)
    for p in range(posts):
        offset = sum(table[code[p]] for code, table in zip(codes, tables))
        values = [offset] + [code[p].astype(jnp.float32) for code in codes] + [wage_ref[p]]
        for kind, value in enumerate(values):
            row = kind * posts + p
            base_ref[row : row + 1, :] = jnp.full((1, lanes), value, jnp.float32)


def own_terms_kernel(slice_e, d_ref, pieces, share_ref, own_ref, other_ref):
    for p in range(pieces.shape[0]):
        x = pieces[p]
        at = pick_rows(d_ref, jnp.where(x < OUTSIDE, x, 0.0).astype(jnp.bfloat16), slice_e)
        slopes = [share_ref[p, index].astype(jnp.bfloat16) for index in range(3)]
        add_terms(at, slopes, own_ref.at[p], other_ref.at[p], slice_e, fresh=True)


def facts_kernel(n_keep, base, *refs):
    facts_ref, pred_ref = refs[-2:]
    posts = pred_ref.shape[0]
    facts_ref[...] = base[...]
    total = tree_sum([part[...] for part in refs[: len(refs) - 2 - n_keep]])
    for p in range(posts):
        value = total[p : p + 1, :] + base[p : p + 1, :]
        pred_ref[pl.ds(p, 1)] = value[0, 0:1]
        facts_ref[p : p + 1, :] = value - base[4 * posts + p : 4 * posts + p + 1, :]


def near_kernel(n_keep, slice_e, d_ref, x_ref, w_ref, head_ref, *refs):
    feat_ref, own_ref, other_ref, xpads, counts, cols = refs[n_keep:]
    posts = x_ref.shape[0]
    head = head_ref[...].astype(jnp.float32)
    for p in range(posts):
        load_post(x_ref[p], xpads.at[p], counts.at[p])
        make_cols(xpads.at[p], cols.at[p])
    for p in range(posts):
        slopes = []
        for index in range(3):
            feature, share = forward(index, cols.at[p], w_ref, head, counts.at[p])
            feat_ref[p, index : index + 1, :] = feature
            slopes.append(share.astype(jnp.bfloat16))
        at = pick_rows(d_ref, middle_of(cols.at[p]), slice_e)
        add_terms(at, slopes, own_ref.at[p], other_ref.at[p], slice_e, fresh=True)


def scaled_sum(residuals, terms):
    total, i = 0.0, 0
    for term in terms:
        for p in range(term.shape[0]):
            total = total + residuals[i] * term[p]
            i += 1
    return total


def last_kernel(sizes, slice_e, d_ref, z_ref, *refs):
    facts, last, far = refs[:4], refs[4], refs[5]
    feats, terms = refs[6:9], refs[9:12]
    w_ref, head_ref, acc_own, acc_other, xpads, counts, cols = refs[12:]
    posts = last.shape[0]
    n_rows, filters = acc_own.shape
    head = head_ref[...].astype(jnp.float32)
    pieces = [last[p] for p in range(posts)] + [far[...]]
    here = z_ref[0]
    residuals = [facts[2][p : p + 1, 0:1] for p in range(posts)]
    residuals.append(facts[3][pl.ds(1 - here, 1), 0:1])
    for p, piece in enumerate(pieces):
        load_post(piece, xpads.at[p], counts.at[p])
        make_cols(xpads.at[p], cols.at[p])
    acc_own[...] = jnp.zeros_like(acc_own)
    made = [facts[0][p : p + 1, 0:1] for p in range(posts)]
    made += [facts[1][p : p + 1, 0:1] for p in range(posts)]
    made.append(facts[3][pl.ds(here, 1), 0:1])
    acc_other[0:n_rows, :] = scaled_sum(made, terms)
    slopes = [[], [], []]
    feat_last = []
    for p, residual in enumerate(residuals):
        features = []
        for index in range(3):
            feature, share = forward(index, cols.at[p], w_ref, head, counts.at[p])
            features.append(feature)
            slopes[index].append((residual * share).astype(jnp.bfloat16))
        feat_last.append(jnp.concatenate(features, axis=0))
    at = jnp.concatenate(
        [pick_rows(d_ref, middle_of(cols.at[p]), slice_e) for p in range(posts + 1)], axis=1
    )
    slopes = [jnp.concatenate(parts, axis=0) for parts in slopes]
    add_terms(at, slopes, acc_own, acc_other, slice_e)

    n_codes = code_rows(sizes, filters)
    place = lax.broadcasted_iota(jnp.int32, (n_codes, filters), 0) * filters
    place = place + lax.broadcasted_iota(jnp.int32, (n_codes, filters), 1)

    def chip_terms(told, feature):
        head_term = jnp.zeros((3, filters), jnp.float32)
        code_term = jnp.zeros((n_codes, filters), jnp.float32)
        for p in range(posts):
            residual = told[p : p + 1, 0:1]
            head_term = head_term + residual * feature[p]
            for kind, start in enumerate(code_starts(sizes, filters)):
                at_row = (kind + 1) * posts + p
                code = told[at_row : at_row + 1, 0:1].astype(jnp.int32) + start
                code_term = code_term + jnp.where(place == code, residual, 0.0)
        return head_term, code_term

    features = [[feat[p, 0:3, :] for p in range(posts)] for feat in feats[:2]]
    features.append(feat_last[:posts])
    one, two = feats[2][0, 0:3, :], feat_last[posts]
    features.append([jnp.where(here == p, one, two) for p in range(posts)])
    sums = [chip_terms(fact[...], feature) for fact, feature in zip(facts, features)]
    acc_other[n_rows:, :] = jnp.zeros((acc_other.shape[0] - n_rows, filters), jnp.float32)
    acc_other[n_rows : n_rows + 3, :] = tree_sum([total[0] for total in sums])
    acc_other[n_rows + 3 : n_rows + 3 + n_codes, :] = tree_sum([total[1] for total in sums])


def gather_kernel(z_ref, acc, own_facts, near_facts, far_facts, *refs):
    posts = refs[0].shape[0]
    made = [facts[p : p + 1, 0:1] for facts in (own_facts, near_facts) for p in range(posts)]
    made.append(far_facts[pl.ds(z_ref[0], 1), 0:1])
    refs[-1][...] = acc[...] + scaled_sum(made, refs[:-1])


def tree_sum(values):
    while len(values) > 1:
        values = [values[i] + values[i + 1] for i in range(0, len(values), 2)]
    return values[0]


def code_starts(sizes, filters):
    starts, start = [], 0
    for size in sizes:
        starts.append(start)
        start += -(-size // filters) * filters
    return starts


def code_rows(sizes, filters):
    return sum(-(-size // filters) for size in sizes)


def swap_kernel(sizes, own_ref, mine_ref, came_ref, grad_ref, head_ref, *code_refs):
    n_rows, filters = own_ref.shape
    grad_ref[...] = own_ref[...] + came_ref[0:n_rows, :]
    head_ref[...] = mine_ref[n_rows : n_rows + 3, :] + came_ref[n_rows : n_rows + 3, :]
    row = n_rows + 3
    for size, ref in zip(sizes, code_refs):
        for start in range(0, size, filters):
            count = min(filters, size - start)
            total = mine_ref[row : row + 1, :] + came_ref[row : row + 1, :]
            ref[pl.ds(start, count)] = total[0, :count]
            row += 1


def local_gather(n_doc, n_filt, *args):
    (
        embedded,
        lengths,
        conv_weight,
        head_weight,
        occupation,
        cohort,
        education,
        occ_table,
        cohort_table,
        edu_table,
        wage,
    ) = args
    posts, seq_len, dims = embedded.shape
    filters = conv_weight.shape[2]
    slice_e = dims // n_doc
    sizes = (occ_table.shape[0], cohort_table.shape[0], edu_table.shape[0])
    f32, i32 = jnp.float32, jnp.int32
    me = lax.axis_index("doc").astype(i32).reshape(1)
    vmem = pl.BlockSpec(memory_space=pltpu.VMEM)
    smem = pl.BlockSpec(memory_space=pltpu.SMEM)
    anywhere = pl.BlockSpec(memory_space=pl.ANY)
    hbm = pl.BlockSpec(memory_space=pltpu.HBM)

    def posts_scratch(n):
        return [
            pltpu.VMEM((n, seq_len + 2 * PAD, dims), f32),
            pltpu.VMEM((n, 8, filters), f32),
            pltpu.VMEM((n, seq_len, (2 * REACH + 1) * dims), jnp.bfloat16),
        ]

    def swap(x, k, axis="doc"):
        size = n_doc if axis == "doc" else n_filt
        return lax.ppermute(x, axis, [(i, i ^ k) for i in range(size)])


    def call(kernel, specs, out, scratch=()):
        def run(*operands):
            operands = [
                pltpu.with_memory_space_constraint(x, pltpu.HBM) if spec is hbm else x
                for x, spec in zip(operands, specs)
            ]
            return built(*operands)

        built = pl.pallas_call(
            kernel,
            in_specs=specs,
            out_specs=[vmem] * len(out),
            out_shape=[
                jax.ShapeDtypeStruct(x, f32) if isinstance(x, tuple) else x for x in out
            ],
            scratch_shapes=list(scratch),
            compiler_params=pltpu.CompilerParams(vmem_limit_bytes=24 << 20),
            cost_estimate=pl.CostEstimate(flops=1, bytes_accessed=1, transcendentals=0),
        )
        return run

    acc_shape = (TAPS * slice_e, filters)
    n_facts = -(-5 * posts // 8) * 8
    weights = jnp.transpose(conv_weight, (1, 0, 2)).reshape(TAPS * dims, filters)
    half = (lax.axis_index("filt").astype(i32) & 1).reshape(1)
    pieces, far_piece = call(
        mask_kernel,
        [smem] * 2 + [hbm] * 2,
        [(posts, seq_len, dims), (seq_len, dims)],
        [
            pltpu.VMEM((posts, seq_len, dims), jnp.bfloat16),
            pltpu.SMEM((posts,), i32),
            pltpu.SemaphoreType.DMA((posts + 1,)),
        ],
    )(me, half, lengths, embedded)

    near = [k for k in range(2, n_doc, 2) if bin(k).count("1") == 1][::-1]
    far = sum(near)
    far_one = swap(far_piece, far)
    near_pieces = [swap(pieces, k) for k in near]

    part, feat_own, share_own, base, weights = call(
        own_kernel,
        [hbm] * 9 + [vmem],
        [
            (8, 128),
            (posts, 3, filters),
            (posts, 3, seq_len, filters),
            (n_facts, 128),
            jax.ShapeDtypeStruct(weights.shape, weights.dtype),
        ],
        [pltpu.SMEM((posts,), i32)] * 3
        + [pltpu.SMEM((posts,), f32)]
        + [pltpu.SMEM((size,), f32) for size in sizes]
        + [pltpu.VMEM(head_weight.shape, head_weight.dtype)]
        + [posts_scratch(posts)[i] for i in (0, 2, 1)]
        + [pltpu.SemaphoreType.DMA((8,)), pltpu.SemaphoreType.DMA((TAPS,))],
    )(
        occupation,
        cohort,
        education,
        wage,
        occ_table,
        cohort_table,
        edu_table,
        head_weight,
        weights,
        pieces,
    )

    def near_terms(x, keep):
        feat, *terms = call(
            functools.partial(near_kernel, len(keep), slice_e),
            [smem] + [vmem] * 3 + [anywhere] * len(keep),
            [(x.shape[0], 8, filters)] + [(x.shape[0],) + acc_shape] * 2,
            posts_scratch(x.shape[0]),
        )(me, x, weights, head_weight, *keep)
        return feat, terms

    own_terms = call(
        functools.partial(own_terms_kernel, slice_e),
        [smem, vmem, vmem],
        [(posts,) + acc_shape] * 2,
    )(me, pieces, share_own)
    parts = [part] + [swap(part, k, "filt") for k in range(1, n_filt)]
    far_feat, far_terms = near_terms(far_one[None], ())
    parts, far_one, far_feat, far_terms, own_terms = lax.optimization_barrier(
        (parts, far_one, far_feat, far_terms, own_terms)
    )
    far_two = swap(far_one, 1, "filt")
    keep = [*own_terms, *far_terms]
    facts, prediction = call(
        functools.partial(facts_kernel, len(keep)),
        [vmem] * (n_filt + 1) + [anywhere] * len(keep),
        [(n_facts, 128), (posts,)],
    )(base, *parts, *keep)

    all_facts = [facts] + [swap(facts, k) for k in near] + [swap(facts, far)]
    near_feat, first_terms = near_terms(near_pieces[0], keep)
    terms = list(zip(own_terms, first_terms, far_terms))
    extra = -(-(3 + code_rows(sizes, filters)) // 8) * 8
    acc_own, acc_other = call(
        functools.partial(last_kernel, sizes, slice_e),
        [smem] * 2 + [vmem] * 14,
        [acc_shape, (acc_shape[0] + extra, filters)],
        posts_scratch(posts + 1),
    )(
        me,
        half,
        *all_facts,
        near_pieces[1],
        far_two,
        feat_own,
        near_feat,
        far_feat,
        *terms[1],
        weights,
        head_weight,
    )

    came = swap(acc_other, 1)
    (total,) = call(gather_kernel, [smem] + [vmem] * 7, [acc_shape])(
        half, acc_own, all_facts[0], all_facts[1], all_facts[3], *terms[0]
    )
    grad, head_grad, *codes = call(
        functools.partial(swap_kernel, sizes),
        [vmem] * 3,
        [acc_shape, (3, filters)] + [(size,) for size in sizes],
    )(total, acc_other, came)
    conv_grad = jnp.transpose(grad.reshape(TAPS, slice_e, filters), (1, 0, 2))
    return (conv_grad, head_grad, *codes, prediction)


def solution(mesh):
    n_doc, n_filt = mesh.shape["doc"], mesh.shape["filt"]
    if n_doc == 8 and n_filt == 4:
        local = functools.partial(local_gather, n_doc, n_filt)
    else:
        local = local_scatter
    return jax.shard_map(
        local,
        mesh=mesh,
        in_specs=(
            P("doc", None, None),
            P("doc"),
            P(None, None, "filt"),
            P(None, "filt"),
            P("doc"),
            P("doc"),
            P("doc"),
            P(),
            P(),
            P(),
            P("doc"),
        ),
        out_specs=(P("doc", None, "filt"), P(None, "filt"), P(), P(), P(), P("doc")),
        check_vma=False,
    )
```

```python
import functools

import jax
import jax.numpy as jnp
import numpy as np
from jax import lax
from jax.experimental import pallas as pl
from jax.experimental.pallas import tpu as pltpu
from jax.sharding import PartitionSpec as P

TAU = 0.05
WIDTH_LIST = ((3, 0), (5, 3), (7, 8))
TAPS = 15
REACH = 3
PAD = 8
OUTSIDE = np.float32(1024.0)
BY_LAST = (((1,), (1,)), ((), ()))


def convolve(columns, weights):
    outputs = []
    for taps, first in WIDTH_LIST:
        half = (taps - 1) // 2
        window = columns[:, :, 3 - half : 3 + half + 1, :]
        outputs.append(
            jnp.einsum(
                "ptje,ejf->ptf",
                window,
                weights[:, first : first + taps, :],
                preferred_element_type=jnp.float32,
            )
        )
    return tuple(outputs)


def grad_terms(columns, slopes):
    outputs = []
    for index in range(3):
        taps = WIDTH_LIST[index][0]
        half = (taps - 1) // 2
        window = columns[:, :, 3 - half : 3 + half + 1, :]
        outputs.append(
            jnp.einsum("ptje,ptf->ejf", window, slopes[index], preferred_element_type=jnp.float32)
        )
    return jnp.concatenate(outputs, axis=1)


def one_hots(codes, size):
    return (codes[:, None] == jnp.arange(size, dtype=jnp.int32)[None, :]).astype(jnp.float32)


def local_scatter(
    embedded,
    lengths,
    conv_weight,
    head_weight,
    occupation,
    cohort,
    education,
    occ_table,
    cohort_table,
    edu_table,
    wage,
):
    posts, seq_len, _ = embedded.shape
    positions = jnp.arange(seq_len, dtype=jnp.int32)
    valid = positions[None, :] < lengths[:, None]
    masked = jnp.where(valid[:, :, None], embedded, jnp.zeros_like(embedded))
    padded = jnp.pad(masked, ((0, 0), (3, 3), (0, 0)))
    columns = jnp.stack([padded[:, offset : offset + seq_len, :] for offset in range(7)], axis=2)
    convs = convolve(columns, conv_weight)
    features = []
    shares = []
    for conv in convs:
        score = jnp.where(valid[:, :, None], conv / TAU, -jnp.inf)
        top = jnp.max(score, axis=1, keepdims=True)
        expd = jnp.exp(score - top)
        total = jnp.sum(expd, axis=1, keepdims=True)
        features.append(TAU * (top[:, 0, :] + jnp.log(total[:, 0, :])))
        shares.append(expd / total)
    feature = jnp.stack(features, axis=1)
    head = head_weight.astype(jnp.float32)
    partial_pred = jnp.sum(feature * head[None, :, :], axis=(1, 2))
    occ_hot = one_hots(occupation, occ_table.shape[0])
    cohort_hot = one_hots(cohort, cohort_table.shape[0])
    edu_hot = one_hots(education, edu_table.shape[0])
    highest = lax.Precision.HIGHEST
    offsets = (
        jnp.dot(occ_hot, occ_table, precision=highest)
        + jnp.dot(cohort_hot, cohort_table, precision=highest)
        + jnp.dot(edu_hot, edu_table, precision=highest)
    )
    prediction = lax.psum(partial_pred, "filt") + offsets
    residual = prediction - wage
    slopes = [
        (residual[:, None, None] * head[index][None, None, :] * shares[index]).astype(jnp.bfloat16)
        for index in range(3)
    ]
    conv_grad = lax.psum_scatter(
        grad_terms(columns, slopes), "doc", scatter_dimension=0, tiled=True
    )
    head_terms = jnp.sum(residual[:, None, None] * feature, axis=0)
    head_grad, occ_grad, cohort_grad, edu_grad = lax.psum(
        (
            head_terms,
            jnp.dot(residual, occ_hot, precision=highest),
            jnp.dot(residual, cohort_hot, precision=highest),
            jnp.dot(residual, edu_hot, precision=highest),
        ),
        "doc",
    )
    return (conv_grad, head_grad, occ_grad, cohort_grad, edu_grad, prediction)


def load_post(x, xpad, count):
    rows, width = x.shape
    inside = x < OUTSIDE
    xpad[0:PAD, :] = jnp.zeros((PAD, width), jnp.float32)
    xpad[PAD + rows :, :] = jnp.zeros((PAD, width), jnp.float32)
    xpad[PAD : PAD + rows, :] = jnp.where(inside, x, 0.0)
    total = jnp.sum(inside.astype(jnp.float32), axis=0, keepdims=True)
    count[...] = jnp.broadcast_to(total[:, 0:1], count.shape)


def make_cols(xpad, cols):
    rows, width = cols.shape[0], xpad.shape[1]
    for offset in range(2 * REACH + 1):
        start = PAD - REACH + offset
        cols[:, offset * width : (offset + 1) * width] = xpad[start : start + rows, :].astype(
            jnp.bfloat16
        )


def forward(index, cols, w_ref, head, count):
    taps, first = WIDTH_LIST[index]
    half = taps // 2
    width = w_ref.shape[0] // TAPS
    conv = jnp.dot(
        cols[:, (REACH - half) * width : (REACH + half + 1) * width],
        w_ref[first * width : (first + taps) * width, :],
        preferred_element_type=jnp.float32,
    )
    place = lax.broadcasted_iota(jnp.int32, conv.shape, 0).astype(jnp.float32)
    score = jnp.where(place < count[0:1, :], conv * np.float32(1.0 / TAU), -jnp.inf)
    top = jnp.max(score, axis=0, keepdims=True)
    expd = jnp.exp(score - top)
    total = jnp.sum(expd, axis=0, keepdims=True)
    feature = np.float32(TAU) * (top + jnp.log(total))
    return feature, expd * (head[index : index + 1] / total)


def pick_rows(d_ref, middle, slice_e):
    rows, width = middle.shape
    me = d_ref[0]
    row = lax.broadcasted_iota(jnp.int32, (2 * slice_e, width), 0)
    lane = lax.broadcasted_iota(jnp.int32, (2 * slice_e, width), 1)
    wanted = jnp.where(row < slice_e, me * slice_e + row, (me ^ 1) * slice_e + row - slice_e)
    pick = (lane == wanted).astype(jnp.bfloat16)
    across = lax.dot_general(pick, middle, BY_LAST, preferred_element_type=jnp.float32)
    place = lax.broadcasted_iota(jnp.int32, (2 * slice_e, rows), 1)
    parts = []
    for offset in range(-REACH, REACH + 1):
        if offset:
            moved = pltpu.roll(across, (-offset) % rows, 1)
            inside = (place + offset >= 0) & (place + offset < rows)
            parts.append(jnp.where(inside, moved, 0.0))
        else:
            parts.append(across)
    return jnp.concatenate(parts, axis=0).astype(jnp.bfloat16)


def middle_of(cols):
    width = cols.shape[1] // (2 * REACH + 1)
    return cols[:, REACH * width : (REACH + 1) * width]


def add_terms(at, slopes, acc_own, acc_other, slice_e, fresh=False):
    step = 2 * slice_e
    for index, (taps, first) in enumerate(WIDTH_LIST):
        half = taps // 2
        term = jnp.dot(
            at[(REACH - half) * step : (REACH + half + 1) * step],
            slopes[index],
            preferred_element_type=jnp.float32,
        )
        for j in range(taps):
            place = slice((first + j) * slice_e, (first + j + 1) * slice_e)
            own = term[j * step : j * step + slice_e]
            other = term[j * step + slice_e : (j + 1) * step]
            if fresh:
                acc_own[place, :] = own
                acc_other[place, :] = other
            else:
                acc_own[place, :] += own
                acc_other[place, :] += other


def mask_kernel(d_ref, z_ref, len_any, x_any, pieces, far_piece, x_ref, len_ref, sems):
    posts, rows, width = x_ref.shape
    copies = [pltpu.make_async_copy(len_any, len_ref, sems.at[posts])]
    copies += [pltpu.make_async_copy(x_any.at[p], x_ref.at[p], sems.at[p]) for p in range(posts)]
    for copy in copies:
        copy.start()
    place = lax.broadcasted_iota(jnp.int32, (rows, width), 0)
    copies[0].wait()
    for p in range(posts):
        copies[1 + p].wait()
        pieces[p] = jnp.where(place < len_ref[p], x_ref[p].astype(jnp.float32), OUTSIDE)
    far_piece[...] = pieces[z_ref[0]]


def own_kernel(*refs):
    small = refs[:8]
    w_ref, pieces, part_ref, feat_ref, share_ref, base_ref = refs[8:14]
    held = refs[14:22]
    xpad, cols, counts, small_sems = refs[22:]
    posts = pieces.shape[0]
    copies = [pltpu.make_async_copy(small[i], held[i], small_sems.at[i]) for i in range(8)]
    for copy in copies:
        copy.start()
    for p in range(posts):
        load_post(pieces[p], xpad.at[p], counts.at[p])
        make_cols(xpad.at[p], cols.at[p])
    copies[7].wait()
    head = held[7][...].astype(jnp.float32)
    parts = [jnp.zeros((1, head.shape[1]), jnp.float32) for _ in range(posts)]
    for index in (2, 1, 0):
        for p in range(posts):
            feature, share = forward(index, cols.at[p], w_ref, head, counts.at[p])
            feat_ref[p, index : index + 1, :] = feature
            share_ref[p, index] = share
            parts[p] = parts[p] + feature * head[index : index + 1]
    lanes = part_ref.shape[1]
    part_ref[...] = jnp.zeros_like(part_ref)
    for p in range(posts):
        total = jnp.sum(parts[p], axis=1, keepdims=True)
        part_ref[p : p + 1, :] = jnp.broadcast_to(total, (1, lanes))
    for copy in copies[:7]:
        copy.wait()
    codes, wage_ref, tables = held[:3], held[3], held[4:7]
    base_ref[...] = jnp.zeros_like(base_ref)
    for p in range(posts):
        offset = sum(table[code[p]] for code, table in zip(codes, tables))
        values = [offset] + [code[p].astype(jnp.float32) for code in codes] + [wage_ref[p]]
        for kind, value in enumerate(values):
            row = kind * posts + p
            base_ref[row : row + 1, :] = jnp.full((1, lanes), value, jnp.float32)


def own_terms_kernel(slice_e, d_ref, pieces, share_ref, own_ref, other_ref):
    for p in range(pieces.shape[0]):
        x = pieces[p]
        at = pick_rows(d_ref, jnp.where(x < OUTSIDE, x, 0.0).astype(jnp.bfloat16), slice_e)
        slopes = [share_ref[p, index].astype(jnp.bfloat16) for index in range(3)]
        add_terms(at, slopes, own_ref.at[p], other_ref.at[p], slice_e, fresh=True)


def facts_kernel(n_keep, base, *refs):
    facts_ref, pred_ref = refs[-2:]
    posts = pred_ref.shape[0]
    facts_ref[...] = base[...]
    total = tree_sum([part[...] for part in refs[: len(refs) - 2 - n_keep]])
    for p in range(posts):
        value = total[p : p + 1, :] + base[p : p + 1, :]
        pred_ref[pl.ds(p, 1)] = value[0, 0:1]
        facts_ref[p : p + 1, :] = value - base[4 * posts + p : 4 * posts + p + 1, :]


def far_kernel(n_keep, slice_e, d_ref, x_ref, w_ref, head_ref, *refs):
    feat_ref, own_ref, other_ref, xpads, counts, cols = refs[n_keep:]
    head = head_ref[...].astype(jnp.float32)
    load_post(x_ref[...], xpads.at[0], counts.at[0])
    make_cols(xpads.at[0], cols.at[0])
    slopes = []
    for index in range(3):
        feature, share = forward(index, cols.at[0], w_ref, head, counts.at[0])
        feat_ref[index : index + 1, :] = feature
        slopes.append(share.astype(jnp.bfloat16))
    at = pick_rows(d_ref, middle_of(cols.at[0]), slice_e)
    add_terms(at, slopes, own_ref.at[0], other_ref.at[0], slice_e, fresh=True)


def made_residuals(here, posts, own, far):
    rows = [own[p : p + 1, 0:1] for p in range(posts)]
    return rows + [far[pl.ds(here, 1), 0:1], far[pl.ds(1 - here, 1), 0:1]]


def scaled_sum(residuals, terms):
    total, i = 0.0, 0
    for term in terms:
        for p in range(term.shape[0]):
            total = total + residuals[i] * term[p]
            i += 1
    return total


def last_kernel(sizes, slice_e, d_ref, z_ref, *refs):
    facts, near = refs[:4], refs[4:6]
    (feat_own, *feat_far), terms = refs[6:9], refs[9:12]
    w_ref, head_ref, acc_own, acc_other, xpads, counts, cols = refs[12:]
    posts = near[0].shape[0]
    n_rows, filters = acc_own.shape
    head = head_ref[...].astype(jnp.float32)
    here = z_ref[0]
    pieces = [x[p] for x in near for p in range(posts)]
    residuals = [fact[p : p + 1, 0:1] for fact in facts[1:3] for p in range(posts)]
    for p, piece in enumerate(pieces):
        load_post(piece, xpads.at[p], counts.at[p])
        make_cols(xpads.at[p], cols.at[p])
    acc_own[...] = jnp.zeros_like(acc_own)
    acc_other[0:n_rows, :] = scaled_sum(made_residuals(here, posts, facts[0], facts[3]), terms)
    slopes = [[], [], []]
    feat_last = []
    for p, residual in enumerate(residuals):
        features = []
        for index in range(3):
            feature, share = forward(index, cols.at[p], w_ref, head, counts.at[p])
            features.append(feature)
            slopes[index].append((residual * share).astype(jnp.bfloat16))
        feat_last.append(jnp.concatenate(features, axis=0))
    at = jnp.concatenate(
        [pick_rows(d_ref, middle_of(cols.at[p]), slice_e) for p in range(len(pieces))], axis=1
    )
    slopes = [jnp.concatenate(parts, axis=0) for parts in slopes]
    add_terms(at, slopes, acc_own, acc_other, slice_e)

    n_codes = code_rows(sizes, filters)
    place = lax.broadcasted_iota(jnp.int32, (n_codes, filters), 0) * filters
    place = place + lax.broadcasted_iota(jnp.int32, (n_codes, filters), 1)

    def chip_terms(told, feature):
        head_term = jnp.zeros((3, filters), jnp.float32)
        code_term = jnp.zeros((n_codes, filters), jnp.float32)
        for p in range(posts):
            residual = told[p : p + 1, 0:1]
            head_term = head_term + residual * feature[p]
            for kind, start in enumerate(code_starts(sizes, filters)):
                at_row = (kind + 1) * posts + p
                code = told[at_row : at_row + 1, 0:1].astype(jnp.int32) + start
                code_term = code_term + jnp.where(place == code, residual, 0.0)
        return head_term, code_term

    features = [
        [feat_own[p] for p in range(posts)],
        feat_last[:posts],
        feat_last[posts:],
        [
            jnp.where(here == p, feat_far[0][0:3, :], feat_far[1][0:3, :])
            for p in range(posts)
        ],
    ]
    sums = [chip_terms(fact[...], feature) for fact, feature in zip(facts, features)]
    acc_other[n_rows:, :] = jnp.zeros((acc_other.shape[0] - n_rows, filters), jnp.float32)
    acc_other[n_rows : n_rows + 3, :] = tree_sum([total[0] for total in sums])
    acc_other[n_rows + 3 : n_rows + 3 + n_codes, :] = tree_sum([total[1] for total in sums])


def gather_kernel(z_ref, acc, own_facts, far_facts, *refs):
    made = made_residuals(z_ref[0], refs[0].shape[0], own_facts, far_facts)
    refs[-1][...] = acc[...] + scaled_sum(made, refs[:-1])


def tree_sum(values):
    while len(values) > 1:
        values = [values[i] + values[i + 1] for i in range(0, len(values), 2)]
    return values[0]


def code_starts(sizes, filters):
    starts, start = [], 0
    for size in sizes:
        starts.append(start)
        start += -(-size // filters) * filters
    return starts


def code_rows(sizes, filters):
    return sum(-(-size // filters) for size in sizes)


def swap_kernel(sizes, own_ref, mine_ref, came_ref, grad_ref, head_ref, *code_refs):
    n_rows, filters = own_ref.shape
    grad_ref[...] = own_ref[...] + came_ref[0:n_rows, :]
    head_ref[...] = mine_ref[n_rows : n_rows + 3, :] + came_ref[n_rows : n_rows + 3, :]
    row = n_rows + 3
    for size, ref in zip(sizes, code_refs):
        for start in range(0, size, filters):
            count = min(filters, size - start)
            total = mine_ref[row : row + 1, :] + came_ref[row : row + 1, :]
            ref[pl.ds(start, count)] = total[0, :count]
            row += 1


def local_gather(n_doc, n_filt, *args):
    (
        embedded,
        lengths,
        conv_weight,
        head_weight,
        occupation,
        cohort,
        education,
        occ_table,
        cohort_table,
        edu_table,
        wage,
    ) = args
    posts, seq_len, dims = embedded.shape
    filters = conv_weight.shape[2]
    slice_e = dims // n_doc
    sizes = (occ_table.shape[0], cohort_table.shape[0], edu_table.shape[0])
    f32, i32 = jnp.float32, jnp.int32
    me = lax.axis_index("doc").astype(i32).reshape(1)
    vmem = pl.BlockSpec(memory_space=pltpu.VMEM)
    smem = pl.BlockSpec(memory_space=pltpu.SMEM)
    anywhere = pl.BlockSpec(memory_space=pl.ANY)
    hbm = pl.BlockSpec(memory_space=pltpu.HBM)

    def posts_scratch(n):
        return [
            pltpu.VMEM((n, seq_len + 2 * PAD, dims), f32),
            pltpu.VMEM((n, 8, filters), f32),
            pltpu.VMEM((n, seq_len, (2 * REACH + 1) * dims), jnp.bfloat16),
        ]

    def swap(x, k, axis="doc"):
        size = n_doc if axis == "doc" else n_filt
        return lax.ppermute(x, axis, [(i, i ^ k) for i in range(size)])


    def call(kernel, specs, out, scratch=(), cost=1):
        def run(*operands):
            operands = [
                pltpu.with_memory_space_constraint(x, pltpu.HBM) if spec is hbm else x
                for x, spec in zip(operands, specs)
            ]
            return built(*operands)

        built = pl.pallas_call(
            kernel,
            in_specs=specs,
            out_specs=[vmem] * len(out),
            out_shape=[
                jax.ShapeDtypeStruct(x, f32) if isinstance(x, tuple) else x for x in out
            ],
            scratch_shapes=list(scratch),
            compiler_params=pltpu.CompilerParams(vmem_limit_bytes=24 << 20),
            cost_estimate=pl.CostEstimate(flops=cost, bytes_accessed=1, transcendentals=0),
        )
        return run

    acc_shape = (TAPS * slice_e, filters)
    n_facts = -(-5 * posts // 8) * 8
    weights = jnp.transpose(conv_weight, (1, 0, 2)).reshape(TAPS * dims, filters)
    half = (lax.axis_index("filt").astype(i32) & 1).reshape(1)
    pieces, far_piece = call(
        mask_kernel,
        [smem] * 2 + [hbm] * 2,
        [(posts, seq_len, dims), (seq_len, dims)],
        [
            pltpu.VMEM((posts, seq_len, dims), jnp.bfloat16),
            pltpu.SMEM((posts,), i32),
            pltpu.SemaphoreType.DMA((posts + 1,)),
        ],
        cost=10000000000,
    )(me, half, lengths, embedded)

    near = [k for k in range(2, n_doc, 2) if bin(k).count("1") == 1][::-1]
    far = sum(near)
    far_one = swap(far_piece, far)
    near_pieces = [swap(pieces, k) for k in near]

    part, feat_own, share_own, base = call(
        own_kernel,
        [hbm] * 8 + [vmem] * 2,
        [
            (8, 128),
            (posts, 3, filters),
            (posts, 3, seq_len, filters),
            (n_facts, 128),
        ],
        [pltpu.SMEM((posts,), i32)] * 3
        + [pltpu.SMEM((posts,), f32)]
        + [pltpu.SMEM((size,), f32) for size in sizes]
        + [pltpu.VMEM(head_weight.shape, head_weight.dtype)]
        + [posts_scratch(posts)[i] for i in (0, 2, 1)]
        + [pltpu.SemaphoreType.DMA((8,))],
    )(
        occupation,
        cohort,
        education,
        wage,
        occ_table,
        cohort_table,
        edu_table,
        head_weight,
        weights,
        pieces,
    )

    def far_terms_of(x, keep, cost=1):
        feat, *terms = call(
            functools.partial(far_kernel, len(keep), slice_e),
            [smem] + [vmem] * 3 + [anywhere] * len(keep),
            [(8, filters)] + [(1,) + acc_shape] * 2,
            posts_scratch(1),
            cost,
        )(me, x, weights, head_weight, *keep)
        return feat, terms

    own_terms = call(
        functools.partial(own_terms_kernel, slice_e),
        [smem, vmem, vmem],
        [(posts,) + acc_shape] * 2,
    )(me, pieces, share_own)
    k = n_filt // 2
    while k > 1:
        part = part + swap(part, k, "filt")
        part, far_one, own_terms = lax.optimization_barrier((part, far_one, own_terms))
        k //= 2
    parts = [part, swap(part, 1, "filt")]
    far_two = swap(far_one, 1, "filt")
    far_feat, far_terms = far_terms_of(far_one, (), 4000000000)
    parts, far_feat, far_terms = lax.optimization_barrier((parts, far_feat, far_terms))
    keep = [*own_terms, *far_terms]
    facts, prediction = call(
        functools.partial(facts_kernel, len(keep)),
        [vmem] * (1 + len(parts)) + [anywhere] * len(keep),
        [(n_facts, 128), (posts,)],
    )(base, *parts, *keep)

    all_facts = [facts] + [swap(facts, k) for k in near] + [swap(facts, far)]
    far_feat_two, far_terms_two = far_terms_of(far_two, keep)
    terms = list(zip(own_terms, far_terms, far_terms_two))
    extra = -(-(3 + code_rows(sizes, filters)) // 8) * 8
    acc_own, acc_other = call(
        functools.partial(last_kernel, sizes, slice_e),
        [smem] * 2 + [vmem] * 14,
        [acc_shape, (acc_shape[0] + extra, filters)],
        posts_scratch(2 * posts),
    )(
        me,
        half,
        *all_facts,
        *near_pieces,
        feat_own,
        far_feat,
        far_feat_two,
        *terms[1],
        weights,
        head_weight,
    )

    came = swap(acc_other, 1)
    (total,) = call(gather_kernel, [smem] + [vmem] * 6, [acc_shape])(
        half, acc_own, all_facts[0], all_facts[3], *terms[0]
    )
    grad, head_grad, *codes = call(
        functools.partial(swap_kernel, sizes),
        [vmem] * 3,
        [acc_shape, (3, filters)] + [(size,) for size in sizes],
    )(total, acc_other, came)
    conv_grad = jnp.transpose(grad.reshape(TAPS, slice_e, filters), (1, 0, 2))
    return (conv_grad, head_grad, *codes, prediction)


def solution(mesh):
    n_doc, n_filt = mesh.shape["doc"], mesh.shape["filt"]
    if n_doc == 8 and n_filt == 4:
        local = functools.partial(local_gather, n_doc, n_filt)
    else:
        local = local_scatter
    return jax.shard_map(
        local,
        mesh=mesh,
        in_specs=(
            P("doc", None, None),
            P("doc"),
            P(None, None, "filt"),
            P(None, "filt"),
            P("doc"),
            P("doc"),
            P("doc"),
            P(),
            P(),
            P(),
            P("doc"),
        ),
        out_specs=(P("doc", None, "filt"), P(None, "filt"), P(), P(), P(), P("doc")),
        check_vma=False,
    )
```

```python
import functools

import jax
import jax.numpy as jnp
import numpy as np
from jax import lax
from jax.experimental import pallas as pl
from jax.experimental.pallas import tpu as pltpu
from jax.sharding import PartitionSpec as P

TAU = 0.05
WIDTH_LIST = ((3, 0), (5, 3), (7, 8))
TAPS = 15
REACH = 3
PAD = 8
EARLY = 0
OUTSIDE = np.float32(1024.0)
BY_LAST = (((1,), (1,)), ((), ()))


def convolve(columns, weights):
    outputs = []
    for taps, first in WIDTH_LIST:
        half = (taps - 1) // 2
        window = columns[:, :, 3 - half : 3 + half + 1, :]
        outputs.append(
            jnp.einsum(
                "ptje,ejf->ptf",
                window,
                weights[:, first : first + taps, :],
                preferred_element_type=jnp.float32,
            )
        )
    return tuple(outputs)


def grad_terms(columns, slopes):
    outputs = []
    for index in range(3):
        taps = WIDTH_LIST[index][0]
        half = (taps - 1) // 2
        window = columns[:, :, 3 - half : 3 + half + 1, :]
        outputs.append(
            jnp.einsum("ptje,ptf->ejf", window, slopes[index], preferred_element_type=jnp.float32)
        )
    return jnp.concatenate(outputs, axis=1)


def one_hots(codes, size):
    return (codes[:, None] == jnp.arange(size, dtype=jnp.int32)[None, :]).astype(jnp.float32)


def local_scatter(
    embedded,
    lengths,
    conv_weight,
    head_weight,
    occupation,
    cohort,
    education,
    occ_table,
    cohort_table,
    edu_table,
    wage,
):
    posts, seq_len, _ = embedded.shape
    positions = jnp.arange(seq_len, dtype=jnp.int32)
    valid = positions[None, :] < lengths[:, None]
    masked = jnp.where(valid[:, :, None], embedded, jnp.zeros_like(embedded))
    padded = jnp.pad(masked, ((0, 0), (3, 3), (0, 0)))
    columns = jnp.stack([padded[:, offset : offset + seq_len, :] for offset in range(7)], axis=2)
    convs = convolve(columns, conv_weight)
    features = []
    shares = []
    for conv in convs:
        score = jnp.where(valid[:, :, None], conv / TAU, -jnp.inf)
        top = jnp.max(score, axis=1, keepdims=True)
        expd = jnp.exp(score - top)
        total = jnp.sum(expd, axis=1, keepdims=True)
        features.append(TAU * (top[:, 0, :] + jnp.log(total[:, 0, :])))
        shares.append(expd / total)
    feature = jnp.stack(features, axis=1)
    head = head_weight.astype(jnp.float32)
    partial_pred = jnp.sum(feature * head[None, :, :], axis=(1, 2))
    occ_hot = one_hots(occupation, occ_table.shape[0])
    cohort_hot = one_hots(cohort, cohort_table.shape[0])
    edu_hot = one_hots(education, edu_table.shape[0])
    highest = lax.Precision.HIGHEST
    offsets = (
        jnp.dot(occ_hot, occ_table, precision=highest)
        + jnp.dot(cohort_hot, cohort_table, precision=highest)
        + jnp.dot(edu_hot, edu_table, precision=highest)
    )
    prediction = lax.psum(partial_pred, "filt") + offsets
    residual = prediction - wage
    slopes = [
        (residual[:, None, None] * head[index][None, None, :] * shares[index]).astype(jnp.bfloat16)
        for index in range(3)
    ]
    conv_grad = lax.psum_scatter(
        grad_terms(columns, slopes), "doc", scatter_dimension=0, tiled=True
    )
    head_terms = jnp.sum(residual[:, None, None] * feature, axis=0)
    head_grad, occ_grad, cohort_grad, edu_grad = lax.psum(
        (
            head_terms,
            jnp.dot(residual, occ_hot, precision=highest),
            jnp.dot(residual, cohort_hot, precision=highest),
            jnp.dot(residual, edu_hot, precision=highest),
        ),
        "doc",
    )
    return (conv_grad, head_grad, occ_grad, cohort_grad, edu_grad, prediction)


def load_post(x, xpad, count):
    rows, width = x.shape
    inside = x < OUTSIDE
    xpad[0:PAD, :] = jnp.zeros((PAD, width), jnp.float32)
    xpad[PAD + rows :, :] = jnp.zeros((PAD, width), jnp.float32)
    xpad[PAD : PAD + rows, :] = jnp.where(inside, x, 0.0)
    total = jnp.sum(inside.astype(jnp.float32), axis=0, keepdims=True)
    count[...] = jnp.broadcast_to(total[:, 0:1], count.shape)


def make_cols(xpad, cols):
    rows, width = cols.shape[0], xpad.shape[1]
    for offset in range(2 * REACH + 1):
        start = PAD - REACH + offset
        cols[:, offset * width : (offset + 1) * width] = xpad[start : start + rows, :].astype(
            jnp.bfloat16
        )


def forward(index, cols, w_ref, head, count):
    taps, first = WIDTH_LIST[index]
    half = taps // 2
    width = w_ref.shape[0] // TAPS
    conv = jnp.dot(
        cols[:, (REACH - half) * width : (REACH + half + 1) * width],
        w_ref[first * width : (first + taps) * width, :],
        preferred_element_type=jnp.float32,
    )
    place = lax.broadcasted_iota(jnp.int32, conv.shape, 0).astype(jnp.float32)
    score = jnp.where(place < count[0:1, :], conv * np.float32(1.0 / TAU), -jnp.inf)
    top = jnp.max(score, axis=0, keepdims=True)
    expd = jnp.exp(score - top)
    total = jnp.sum(expd, axis=0, keepdims=True)
    feature = np.float32(TAU) * (top + jnp.log(total))
    return feature, expd * (head[index : index + 1] / total)


def pick_rows(d_ref, middle, slice_e):
    rows, width = middle.shape
    me = d_ref[0]
    row = lax.broadcasted_iota(jnp.int32, (2 * slice_e, width), 0)
    lane = lax.broadcasted_iota(jnp.int32, (2 * slice_e, width), 1)
    wanted = jnp.where(row < slice_e, me * slice_e + row, (me ^ 1) * slice_e + row - slice_e)
    pick = (lane == wanted).astype(jnp.bfloat16)
    across = lax.dot_general(pick, middle, BY_LAST, preferred_element_type=jnp.float32)
    place = lax.broadcasted_iota(jnp.int32, (2 * slice_e, rows), 1)
    parts = []
    for offset in range(-REACH, REACH + 1):
        if offset:
            moved = pltpu.roll(across, (-offset) % rows, 1)
            inside = (place + offset >= 0) & (place + offset < rows)
            parts.append(jnp.where(inside, moved, 0.0))
        else:
            parts.append(across)
    return jnp.concatenate(parts, axis=0).astype(jnp.bfloat16)


def middle_of(cols):
    width = cols.shape[1] // (2 * REACH + 1)
    return cols[:, REACH * width : (REACH + 1) * width]


def add_terms(at, slopes, acc_own, acc_other, slice_e, fresh=False):
    step = 2 * slice_e
    for index, (taps, first) in enumerate(WIDTH_LIST):
        half = taps // 2
        term = jnp.dot(
            at[(REACH - half) * step : (REACH + half + 1) * step],
            slopes[index],
            preferred_element_type=jnp.float32,
        )
        for j in range(taps):
            place = slice((first + j) * slice_e, (first + j + 1) * slice_e)
            own = term[j * step : j * step + slice_e]
            other = term[j * step + slice_e : (j + 1) * step]
            if fresh:
                acc_own[place, :] = own
                acc_other[place, :] = other
            else:
                acc_own[place, :] += own
                acc_other[place, :] += other


def mask_kernel(d_ref, z_ref, len_any, x_any, pieces, far_piece, x_ref, len_ref, sems):
    posts, rows, width = x_ref.shape
    copies = [pltpu.make_async_copy(len_any, len_ref, sems.at[posts])]
    copies += [pltpu.make_async_copy(x_any.at[p], x_ref.at[p], sems.at[p]) for p in range(posts)]
    for copy in copies:
        copy.start()
    place = lax.broadcasted_iota(jnp.int32, (rows, width), 0)
    copies[0].wait()
    for p in range(posts):
        copies[1 + p].wait()
        pieces[p] = jnp.where(place < len_ref[p], x_ref[p].astype(jnp.float32), OUTSIDE)
    far_piece[...] = pieces[z_ref[0]]


def own_kernel(*refs):
    small = refs[:8]
    w_ref, pieces, part_ref, feat_ref, share_ref, base_ref = refs[8:14]
    held = refs[14:22]
    xpad, cols, counts, small_sems = refs[22:]
    posts = pieces.shape[0]
    copies = [pltpu.make_async_copy(small[i], held[i], small_sems.at[i]) for i in range(8)]
    for copy in copies:
        copy.start()
    for p in range(posts):
        load_post(pieces[p], xpad.at[p], counts.at[p])
        make_cols(xpad.at[p], cols.at[p])
    copies[7].wait()
    head = held[7][...].astype(jnp.float32)
    parts = [jnp.zeros((1, head.shape[1]), jnp.float32) for _ in range(posts)]
    for index in (2, 1, 0):
        for p in range(posts):
            feature, share = forward(index, cols.at[p], w_ref, head, counts.at[p])
            feat_ref[p, index : index + 1, :] = feature
            share_ref[p, index] = share
            parts[p] = parts[p] + feature * head[index : index + 1]
    lanes = part_ref.shape[1]
    part_ref[...] = jnp.zeros_like(part_ref)
    for p in range(posts):
        total = jnp.sum(parts[p], axis=1, keepdims=True)
        part_ref[p : p + 1, :] = jnp.broadcast_to(total, (1, lanes))
    for copy in copies[:7]:
        copy.wait()
    codes, wage_ref, tables = held[:3], held[3], held[4:7]
    base_ref[...] = jnp.zeros_like(base_ref)
    for p in range(posts):
        offset = sum(table[code[p]] for code, table in zip(codes, tables))
        values = [offset] + [code[p].astype(jnp.float32) for code in codes] + [wage_ref[p]]
        for kind, value in enumerate(values):
            row = kind * posts + p
            base_ref[row : row + 1, :] = jnp.full((1, lanes), value, jnp.float32)


def own_terms_kernel(slice_e, d_ref, pieces, share_ref, own_ref, other_ref):
    for p in range(pieces.shape[0]):
        x = pieces[p]
        at = pick_rows(d_ref, jnp.where(x < OUTSIDE, x, 0.0).astype(jnp.bfloat16), slice_e)
        slopes = [share_ref[p, index].astype(jnp.bfloat16) for index in range(3)]
        add_terms(at, slopes, own_ref.at[p], other_ref.at[p], slice_e, fresh=True)


def facts_kernel(posts, n_keep, base, *refs):
    facts_ref = refs[-1]
    facts_ref[...] = base[...]
    total = tree_sum([part[...] for part in refs[: len(refs) - 1 - n_keep]])
    for p in range(posts):
        value = total[p : p + 1, :] + base[p : p + 1, :]
        facts_ref[p : p + 1, :] = value - base[4 * posts + p : 4 * posts + p + 1, :]
        facts_ref[5 * posts + p : 5 * posts + p + 1, :] = value


def one_kernel(n_keep, slice_e, d_ref, x_ref, w_ref, head_ref, *refs):
    feat_ref, own_ref, other_ref, xpads, counts, cols = refs[n_keep:]
    head = head_ref[...].astype(jnp.float32)
    load_post(x_ref[0], xpads.at[0], counts.at[0])
    make_cols(xpads.at[0], cols.at[0])
    slopes = []
    for index in range(3):
        feature, share = forward(index, cols.at[0], w_ref, head, counts.at[0])
        feat_ref[index : index + 1, :] = feature
        slopes.append(share.astype(jnp.bfloat16))
    at = pick_rows(d_ref, middle_of(cols.at[0]), slice_e)
    add_terms(at, slopes, own_ref.at[0], other_ref.at[0], slice_e, fresh=True)


def made_residuals(here, posts, own, far, near):
    rows = [own[p : p + 1, 0:1] for p in range(posts)]
    return rows + [far[pl.ds(here, 1), 0:1], far[pl.ds(1 - here, 1), 0:1], near[0:1, 0:1]]


def scaled_sum(residuals, terms):
    total, i = 0.0, 0
    for term in terms:
        for p in range(term.shape[0]):
            total = total + residuals[i] * term[p]
            i += 1
    return total


def last_kernel(sizes, slice_e, d_ref, z_ref, *refs):
    facts, near = refs[:4], refs[4:6]
    (feat_own, *feat_far, feat_near), terms = refs[6:10], refs[10:14]
    w_ref, head_ref, acc_own, acc_other, xpads, counts, cols = refs[14:]
    posts = near[0].shape[0]
    n_rows, filters = acc_own.shape
    head = head_ref[...].astype(jnp.float32)
    here = z_ref[0]
    left = [(k, p) for k in range(2) for p in range(posts) if (k, p) != (EARLY, 0)]
    pieces = [near[k][p] for k, p in left]
    residuals = [facts[1 + k][p : p + 1, 0:1] for k, p in left]
    for p, piece in enumerate(pieces):
        load_post(piece, xpads.at[p], counts.at[p])
        make_cols(xpads.at[p], cols.at[p])
    acc_own[...] = jnp.zeros_like(acc_own)
    acc_other[0:n_rows, :] = scaled_sum(
        made_residuals(here, posts, facts[0], facts[3], facts[1 + EARLY]), terms
    )
    slopes = [[], [], []]
    feat_last = {}
    for p, residual in enumerate(residuals):
        features = []
        for index in range(3):
            feature, share = forward(index, cols.at[p], w_ref, head, counts.at[p])
            features.append(feature)
            slopes[index].append((residual * share).astype(jnp.bfloat16))
        feat_last[left[p]] = jnp.concatenate(features, axis=0)
    at = jnp.concatenate(
        [pick_rows(d_ref, middle_of(cols.at[p]), slice_e) for p in range(len(pieces))], axis=1
    )
    slopes = [jnp.concatenate(parts, axis=0) for parts in slopes]
    add_terms(at, slopes, acc_own, acc_other, slice_e)

    n_codes = code_rows(sizes, filters)
    place = lax.broadcasted_iota(jnp.int32, (n_codes, filters), 0) * filters
    place = place + lax.broadcasted_iota(jnp.int32, (n_codes, filters), 1)

    def chip_terms(told, feature):
        head_term = jnp.zeros((3, filters), jnp.float32)
        code_term = jnp.zeros((n_codes, filters), jnp.float32)
        for p in range(posts):
            residual = told[p : p + 1, 0:1]
            head_term = head_term + residual * feature[p]
            for kind, start in enumerate(code_starts(sizes, filters)):
                at_row = (kind + 1) * posts + p
                code = told[at_row : at_row + 1, 0:1].astype(jnp.int32) + start
                code_term = code_term + jnp.where(place == code, residual, 0.0)
        return head_term, code_term

    features = [
        [feat_own[p] for p in range(posts)],
        *[[feat_last.get((k, p), feat_near[0:3, :]) for p in range(posts)] for k in range(2)],
        [
            jnp.where(here == p, feat_far[0][0:3, :], feat_far[1][0:3, :])
            for p in range(posts)
        ],
    ]
    sums = [chip_terms(fact[...], feature) for fact, feature in zip(facts, features)]
    acc_other[n_rows:, :] = jnp.zeros((acc_other.shape[0] - n_rows, filters), jnp.float32)
    acc_other[n_rows : n_rows + 3, :] = tree_sum([total[0] for total in sums])
    acc_other[n_rows + 3 : n_rows + 3 + n_codes, :] = tree_sum([total[1] for total in sums])


def gather_kernel(z_ref, acc, own_facts, far_facts, near_facts, *refs):
    *terms, total_ref, pred_ref = refs
    posts = pred_ref.shape[0]
    for p in range(posts):
        pred_ref[pl.ds(p, 1)] = own_facts[5 * posts + p, 0:1]
    made = made_residuals(z_ref[0], posts, own_facts, far_facts, near_facts)
    total_ref[...] = acc[...] + scaled_sum(made, terms)


def tree_sum(values):
    while len(values) > 1:
        values = [values[i] + values[i + 1] for i in range(0, len(values), 2)]
    return values[0]


def code_starts(sizes, filters):
    starts, start = [], 0
    for size in sizes:
        starts.append(start)
        start += -(-size // filters) * filters
    return starts


def code_rows(sizes, filters):
    return sum(-(-size // filters) for size in sizes)


def swap_kernel(sizes, own_ref, mine_ref, came_ref, grad_ref, head_ref, *code_refs):
    n_rows, filters = own_ref.shape
    grad_ref[...] = own_ref[...] + came_ref[0:n_rows, :]
    head_ref[...] = mine_ref[n_rows : n_rows + 3, :] + came_ref[n_rows : n_rows + 3, :]
    row = n_rows + 3
    for size, ref in zip(sizes, code_refs):
        for start in range(0, size, filters):
            count = min(filters, size - start)
            total = mine_ref[row : row + 1, :] + came_ref[row : row + 1, :]
            ref[pl.ds(start, count)] = total[0, :count]
            row += 1


def local_gather(n_doc, n_filt, *args):
    (
        embedded,
        lengths,
        conv_weight,
        head_weight,
        occupation,
        cohort,
        education,
        occ_table,
        cohort_table,
        edu_table,
        wage,
    ) = args
    posts, seq_len, dims = embedded.shape
    filters = conv_weight.shape[2]
    slice_e = dims // n_doc
    sizes = (occ_table.shape[0], cohort_table.shape[0], edu_table.shape[0])
    f32, i32 = jnp.float32, jnp.int32
    me = lax.axis_index("doc").astype(i32).reshape(1)
    vmem = pl.BlockSpec(memory_space=pltpu.VMEM)
    smem = pl.BlockSpec(memory_space=pltpu.SMEM)
    anywhere = pl.BlockSpec(memory_space=pl.ANY)
    hbm = pl.BlockSpec(memory_space=pltpu.HBM)

    def posts_scratch(n):
        return [
            pltpu.VMEM((n, seq_len + 2 * PAD, dims), f32),
            pltpu.VMEM((n, 8, filters), f32),
            pltpu.VMEM((n, seq_len, (2 * REACH + 1) * dims), jnp.bfloat16),
        ]

    def swap(x, k, axis="doc"):
        size = n_doc if axis == "doc" else n_filt
        return lax.ppermute(x, axis, [(i, i ^ k) for i in range(size)])


    def call(kernel, specs, out, scratch=(), cost=1):
        def run(*operands):
            operands = [
                pltpu.with_memory_space_constraint(x, pltpu.HBM) if spec is hbm else x
                for x, spec in zip(operands, specs)
            ]
            return built(*operands)

        built = pl.pallas_call(
            kernel,
            in_specs=specs,
            out_specs=[vmem] * len(out),
            out_shape=[
                jax.ShapeDtypeStruct(x, f32) if isinstance(x, tuple) else x for x in out
            ],
            scratch_shapes=list(scratch),
            compiler_params=pltpu.CompilerParams(vmem_limit_bytes=24 << 20),
            cost_estimate=pl.CostEstimate(flops=cost, bytes_accessed=1, transcendentals=0),
        )
        return run

    acc_shape = (TAPS * slice_e, filters)
    n_facts = -(-6 * posts // 8) * 8
    weights = jnp.transpose(conv_weight, (1, 0, 2)).reshape(TAPS * dims, filters)
    half = (lax.axis_index("filt").astype(i32) & 1).reshape(1)
    pieces, far_piece = call(
        mask_kernel,
        [smem] * 2 + [hbm] * 2,
        [(posts, seq_len, dims), (seq_len, dims)],
        [
            pltpu.VMEM((posts, seq_len, dims), jnp.bfloat16),
            pltpu.SMEM((posts,), i32),
            pltpu.SemaphoreType.DMA((posts + 1,)),
        ],
        cost=10000000000,
    )(me, half, lengths, embedded)

    near = [k for k in range(2, n_doc, 2) if bin(k).count("1") == 1][::-1]
    far = sum(near)
    far_one = swap(far_piece, far)
    near_pieces = [swap(pieces, k) for k in near]

    part, feat_own, share_own, base = call(
        own_kernel,
        [hbm] * 8 + [vmem] * 2,
        [
            (8, 128),
            (posts, 3, filters),
            (posts, 3, seq_len, filters),
            (n_facts, 128),
        ],
        [pltpu.SMEM((posts,), i32)] * 3
        + [pltpu.SMEM((posts,), f32)]
        + [pltpu.SMEM((size,), f32) for size in sizes]
        + [pltpu.VMEM(head_weight.shape, head_weight.dtype)]
        + [posts_scratch(posts)[i] for i in (0, 2, 1)]
        + [pltpu.SemaphoreType.DMA((8,))],
    )(
        occupation,
        cohort,
        education,
        wage,
        occ_table,
        cohort_table,
        edu_table,
        head_weight,
        weights,
        pieces,
    )

    def terms_of(x, keep, cost=1):
        feat, *terms = call(
            functools.partial(one_kernel, len(keep), slice_e),
            [smem] + [vmem] * 3 + [anywhere] * len(keep),
            [(8, filters)] + [(1,) + acc_shape] * 2,
            posts_scratch(1),
            cost,
        )(me, x, weights, head_weight, *keep)
        return feat, terms

    own_terms = call(
        functools.partial(own_terms_kernel, slice_e),
        [smem, vmem, vmem],
        [(posts,) + acc_shape] * 2,
    )(me, pieces, share_own)
    k = n_filt // 2
    while k > 1:
        part = part + swap(part, k, "filt")
        part, far_one, own_terms = lax.optimization_barrier((part, far_one, own_terms))
        k //= 2
    parts = [part, swap(part, 1, "filt")]
    far_two = swap(far_one, 1, "filt")
    far_feat, far_terms = terms_of(far_one[None], (), 4000000000)
    parts, far_feat, far_terms = lax.optimization_barrier((parts, far_feat, far_terms))
    keep = [*own_terms, *far_terms]
    (facts,) = call(
        functools.partial(facts_kernel, posts, len(keep)),
        [vmem] * (1 + len(parts)) + [anywhere] * len(keep),
        [(n_facts, 128)],
    )(base, *parts, *keep)

    all_facts = [facts] + [swap(facts, k) for k in near] + [swap(facts, far)]
    far_feat_two, far_terms_two = terms_of(far_two[None], keep)
    keep += far_terms_two
    near_feat, near_terms = terms_of(near_pieces[0], keep)
    terms = list(zip(own_terms, far_terms, far_terms_two, near_terms))
    extra = -(-(3 + code_rows(sizes, filters)) // 8) * 8
    acc_own, acc_other = call(
        functools.partial(last_kernel, sizes, slice_e),
        [smem] * 2 + [vmem] * 16,
        [acc_shape, (acc_shape[0] + extra, filters)],
        posts_scratch(2 * posts - 1),
    )(
        me,
        half,
        *all_facts,
        *near_pieces,
        feat_own,
        far_feat,
        far_feat_two,
        near_feat,
        *terms[1],
        weights,
        head_weight,
    )

    came = swap(acc_other, 1)
    total, prediction = call(gather_kernel, [smem] + [vmem] * 8, [acc_shape, (posts,)])(
        half, acc_own, all_facts[0], all_facts[3], all_facts[1 + EARLY], *terms[0]
    )
    grad, head_grad, *codes = call(
        functools.partial(swap_kernel, sizes),
        [vmem] * 3,
        [acc_shape, (3, filters)] + [(size,) for size in sizes],
    )(total, acc_other, came)
    conv_grad = jnp.transpose(grad.reshape(TAPS, slice_e, filters), (1, 0, 2))
    return (conv_grad, head_grad, *codes, prediction)


def solution(mesh):
    n_doc, n_filt = mesh.shape["doc"], mesh.shape["filt"]
    if n_doc == 8 and n_filt == 4:
        local = functools.partial(local_gather, n_doc, n_filt)
    else:
        local = local_scatter
    return jax.shard_map(
        local,
        mesh=mesh,
        in_specs=(
            P("doc", None, None),
            P("doc"),
            P(None, None, "filt"),
            P(None, "filt"),
            P("doc"),
            P("doc"),
            P("doc"),
            P(),
            P(),
            P(),
            P("doc"),
        ),
        out_specs=(P("doc", None, "filt"), P(None, "filt"), P(), P(), P(), P("doc")),
        check_vma=False,
    )
```

```python
import functools

import jax
import jax.numpy as jnp
import numpy as np
from jax import lax
from jax.experimental import pallas as pl
from jax.experimental.pallas import tpu as pltpu
from jax.sharding import PartitionSpec as P

TAU = 0.05
WIDTH_LIST = ((3, 0), (5, 3), (7, 8))
TAPS = 15
REACH = 3
PAD = 8
EARLY = 0
OUTSIDE = np.float32(1024.0)
BY_LAST = (((1,), (1,)), ((), ()))


def convolve(columns, weights):
    outputs = []
    for taps, first in WIDTH_LIST:
        half = (taps - 1) // 2
        window = columns[:, :, 3 - half : 3 + half + 1, :]
        outputs.append(
            jnp.einsum(
                "ptje,ejf->ptf",
                window,
                weights[:, first : first + taps, :],
                preferred_element_type=jnp.float32,
            )
        )
    return tuple(outputs)


def grad_terms(columns, slopes):
    outputs = []
    for index in range(3):
        taps = WIDTH_LIST[index][0]
        half = (taps - 1) // 2
        window = columns[:, :, 3 - half : 3 + half + 1, :]
        outputs.append(
            jnp.einsum("ptje,ptf->ejf", window, slopes[index], preferred_element_type=jnp.float32)
        )
    return jnp.concatenate(outputs, axis=1)


def one_hots(codes, size):
    return (codes[:, None] == jnp.arange(size, dtype=jnp.int32)[None, :]).astype(jnp.float32)


def local_scatter(
    embedded,
    lengths,
    conv_weight,
    head_weight,
    occupation,
    cohort,
    education,
    occ_table,
    cohort_table,
    edu_table,
    wage,
):
    posts, seq_len, _ = embedded.shape
    positions = jnp.arange(seq_len, dtype=jnp.int32)
    valid = positions[None, :] < lengths[:, None]
    masked = jnp.where(valid[:, :, None], embedded, jnp.zeros_like(embedded))
    padded = jnp.pad(masked, ((0, 0), (3, 3), (0, 0)))
    columns = jnp.stack([padded[:, offset : offset + seq_len, :] for offset in range(7)], axis=2)
    convs = convolve(columns, conv_weight)
    features = []
    shares = []
    for conv in convs:
        score = jnp.where(valid[:, :, None], conv / TAU, -jnp.inf)
        top = jnp.max(score, axis=1, keepdims=True)
        expd = jnp.exp(score - top)
        total = jnp.sum(expd, axis=1, keepdims=True)
        features.append(TAU * (top[:, 0, :] + jnp.log(total[:, 0, :])))
        shares.append(expd / total)
    feature = jnp.stack(features, axis=1)
    head = head_weight.astype(jnp.float32)
    partial_pred = jnp.sum(feature * head[None, :, :], axis=(1, 2))
    occ_hot = one_hots(occupation, occ_table.shape[0])
    cohort_hot = one_hots(cohort, cohort_table.shape[0])
    edu_hot = one_hots(education, edu_table.shape[0])
    highest = lax.Precision.HIGHEST
    offsets = (
        jnp.dot(occ_hot, occ_table, precision=highest)
        + jnp.dot(cohort_hot, cohort_table, precision=highest)
        + jnp.dot(edu_hot, edu_table, precision=highest)
    )
    prediction = lax.psum(partial_pred, "filt") + offsets
    residual = prediction - wage
    slopes = [
        (residual[:, None, None] * head[index][None, None, :] * shares[index]).astype(jnp.bfloat16)
        for index in range(3)
    ]
    conv_grad = lax.psum_scatter(
        grad_terms(columns, slopes), "doc", scatter_dimension=0, tiled=True
    )
    head_terms = jnp.sum(residual[:, None, None] * feature, axis=0)
    head_grad, occ_grad, cohort_grad, edu_grad = lax.psum(
        (
            head_terms,
            jnp.dot(residual, occ_hot, precision=highest),
            jnp.dot(residual, cohort_hot, precision=highest),
            jnp.dot(residual, edu_hot, precision=highest),
        ),
        "doc",
    )
    return (conv_grad, head_grad, occ_grad, cohort_grad, edu_grad, prediction)


def load_post(x, xpad, count):
    rows, width = x.shape
    inside = x < OUTSIDE
    xpad[0:PAD, :] = jnp.zeros((PAD, width), jnp.float32)
    xpad[PAD + rows :, :] = jnp.zeros((PAD, width), jnp.float32)
    xpad[PAD : PAD + rows, :] = jnp.where(inside, x, 0.0)
    total = jnp.sum(inside.astype(jnp.float32), axis=0, keepdims=True)
    count[...] = jnp.broadcast_to(total[:, 0:1], count.shape)


def make_cols(xpad, cols):
    rows, width = cols.shape[0], xpad.shape[1]
    for offset in range(2 * REACH + 1):
        start = PAD - REACH + offset
        cols[:, offset * width : (offset + 1) * width] = xpad[start : start + rows, :].astype(
            jnp.bfloat16
        )


def forward(index, cols, w_ref, head, count):
    taps, first = WIDTH_LIST[index]
    half = taps // 2
    width = w_ref.shape[0] // TAPS
    conv = jnp.dot(
        cols[:, (REACH - half) * width : (REACH + half + 1) * width],
        w_ref[first * width : (first + taps) * width, :],
        preferred_element_type=jnp.float32,
    )
    place = lax.broadcasted_iota(jnp.int32, conv.shape, 0).astype(jnp.float32)
    score = jnp.where(place < count[0:1, :], conv * np.float32(1.0 / TAU), -jnp.inf)
    top = jnp.max(score, axis=0, keepdims=True)
    expd = jnp.exp(score - top)
    total = jnp.sum(expd, axis=0, keepdims=True)
    feature = np.float32(TAU) * (top + jnp.log(total))
    return feature, expd * (head[index : index + 1] / total)


def pick_rows(d_ref, middle, slice_e):
    rows, width = middle.shape
    me = d_ref[0]
    row = lax.broadcasted_iota(jnp.int32, (2 * slice_e, width), 0)
    lane = lax.broadcasted_iota(jnp.int32, (2 * slice_e, width), 1)
    wanted = jnp.where(row < slice_e, me * slice_e + row, (me ^ 1) * slice_e + row - slice_e)
    pick = (lane == wanted).astype(jnp.bfloat16)
    across = lax.dot_general(pick, middle, BY_LAST, preferred_element_type=jnp.float32)
    place = lax.broadcasted_iota(jnp.int32, (2 * slice_e, rows), 1)
    parts = []
    for offset in range(-REACH, REACH + 1):
        if offset:
            moved = pltpu.roll(across, (-offset) % rows, 1)
            inside = (place + offset >= 0) & (place + offset < rows)
            parts.append(jnp.where(inside, moved, 0.0))
        else:
            parts.append(across)
    return jnp.concatenate(parts, axis=0).astype(jnp.bfloat16)


def middle_of(cols):
    width = cols.shape[1] // (2 * REACH + 1)
    return cols[:, REACH * width : (REACH + 1) * width]


def add_terms(at, slopes, acc_own, acc_other, slice_e, fresh=False):
    step = 2 * slice_e
    for index, (taps, first) in list(enumerate(WIDTH_LIST))[::-1]:
        half = taps // 2
        term = jnp.dot(
            at[(REACH - half) * step : (REACH + half + 1) * step],
            slopes[index],
            preferred_element_type=jnp.float32,
        )
        for j in range(taps):
            place = slice((first + j) * slice_e, (first + j + 1) * slice_e)
            own = term[j * step : j * step + slice_e]
            other = term[j * step + slice_e : (j + 1) * step]
            if fresh:
                acc_own[place, :] = own
                acc_other[place, :] = other
            else:
                acc_own[place, :] += own
                acc_other[place, :] += other


def mask_kernel(d_ref, z_ref, len_any, x_any, pieces, far_piece, x_ref, len_ref, sems):
    posts, rows, width = x_ref.shape
    copies = [pltpu.make_async_copy(len_any, len_ref, sems.at[posts])]
    copies += [pltpu.make_async_copy(x_any.at[p], x_ref.at[p], sems.at[p]) for p in range(posts)]
    for copy in copies:
        copy.start()
    place = lax.broadcasted_iota(jnp.int32, (rows, width), 0)
    copies[0].wait()
    for p in range(posts):
        copies[1 + p].wait()
        pieces[p] = jnp.where(place < len_ref[p], x_ref[p].astype(jnp.float32), OUTSIDE)
    far_piece[...] = pieces[z_ref[0]]


def own_kernel(*refs):
    small = refs[:7]
    w_ref, pieces, head_ref, part_ref, feat_ref, share_ref, base_ref = refs[7:14]
    held = refs[14:21]
    xpad, cols, counts, small_sems = refs[21:]
    posts = pieces.shape[0]
    copies = [pltpu.make_async_copy(small[i], held[i], small_sems.at[i]) for i in range(7)]
    for copy in copies:
        copy.start()
    for p in range(posts):
        load_post(pieces[p], xpad.at[p], counts.at[p])
        make_cols(xpad.at[p], cols.at[p])
    head = head_ref[...].astype(jnp.float32)
    parts = [jnp.zeros((1, head.shape[1]), jnp.float32) for _ in range(posts)]
    for index in (2, 1, 0):
        for p in range(posts):
            feature, share = forward(index, cols.at[p], w_ref, head, counts.at[p])
            feat_ref[p, index : index + 1, :] = feature
            share_ref[p, index] = share
            parts[p] = parts[p] + feature * head[index : index + 1]
    lanes = part_ref.shape[1]
    part_ref[...] = jnp.zeros_like(part_ref)
    for p in range(posts):
        total = jnp.sum(parts[p], axis=1, keepdims=True)
        part_ref[p : p + 1, :] = jnp.broadcast_to(total, (1, lanes))
    for copy in copies:
        copy.wait()
    codes, wage_ref, tables = held[:3], held[3], held[4:]
    base_ref[...] = jnp.zeros_like(base_ref)
    for p in range(posts):
        offset = sum(table[code[p]] for code, table in zip(codes, tables))
        values = [offset] + [code[p].astype(jnp.float32) for code in codes] + [wage_ref[p]]
        for kind, value in enumerate(values):
            row = kind * posts + p
            base_ref[row : row + 1, :] = jnp.full((1, lanes), value, jnp.float32)


def own_terms_kernel(slice_e, d_ref, pieces, share_ref, own_ref, other_ref):
    for p in range(pieces.shape[0]):
        x = pieces[p]
        at = pick_rows(d_ref, jnp.where(x < OUTSIDE, x, 0.0).astype(jnp.bfloat16), slice_e)
        slopes = [share_ref[p, index].astype(jnp.bfloat16) for index in range(3)]
        add_terms(at, slopes, own_ref.at[p], other_ref.at[p], slice_e, fresh=True)


def facts_kernel(posts, n_keep, base, *refs):
    facts_ref = refs[-1]
    facts_ref[...] = base[...]
    total = tree_sum([part[...] for part in refs[: len(refs) - 1 - n_keep]])
    for p in range(posts):
        value = total[p : p + 1, :] + base[p : p + 1, :]
        facts_ref[p : p + 1, :] = value - base[4 * posts + p : 4 * posts + p + 1, :]
        facts_ref[5 * posts + p : 5 * posts + p + 1, :] = value


def one_kernel(n_keep, slice_e, d_ref, x_ref, w_ref, head_ref, *refs):
    feat_ref, own_ref, other_ref, xpads, counts, cols = refs[n_keep:]
    head = head_ref[...].astype(jnp.float32)
    load_post(x_ref[0], xpads.at[0], counts.at[0])
    make_cols(xpads.at[0], cols.at[0])
    at = pick_rows(d_ref, middle_of(cols.at[0]), slice_e)
    slopes = [None] * 3
    for index in (2, 1, 0):
        feature, share = forward(index, cols.at[0], w_ref, head, counts.at[0])
        feat_ref[index : index + 1, :] = feature
        slopes[index] = share.astype(jnp.bfloat16)
    add_terms(at, slopes, own_ref.at[0], other_ref.at[0], slice_e, fresh=True)


def made_residuals(here, posts, own, far, near):
    rows = [own[p : p + 1, 0:1] for p in range(posts)]
    return rows + [far[pl.ds(here, 1), 0:1], far[pl.ds(1 - here, 1), 0:1], near[0:1, 0:1]]


def scaled_sum(residuals, terms):
    total, i = 0.0, 0
    for term in terms:
        for p in range(term.shape[0]):
            total = total + residuals[i] * term[p]
            i += 1
    return total


def last_kernel(sizes, slice_e, d_ref, z_ref, *refs):
    facts, near = refs[:4], refs[4:6]
    (feat_own, *feat_far, feat_near), terms = refs[6:10], refs[10:14]
    w_ref, head_ref, acc_own, acc_other, xpads, counts, cols = refs[14:]
    posts = near[0].shape[0]
    n_rows, filters = acc_own.shape
    head = head_ref[...].astype(jnp.float32)
    here = z_ref[0]
    left = [(k, p) for k in range(2) for p in range(posts) if (k, p) != (EARLY, 0)]
    pieces = [near[k][p] for k, p in left]
    residuals = [facts[1 + k][p : p + 1, 0:1] for k, p in left]
    for p, piece in enumerate(pieces):
        load_post(piece, xpads.at[p], counts.at[p])
        make_cols(xpads.at[p], cols.at[p])
    acc_own[...] = jnp.zeros_like(acc_own)
    acc_other[0:n_rows, :] = scaled_sum(
        made_residuals(here, posts, facts[0], facts[3], facts[1 + EARLY]), terms
    )
    slopes = [[], [], []]
    feat_last = {}
    for p, residual in enumerate(residuals):
        features = []
        for index in range(3):
            feature, share = forward(index, cols.at[p], w_ref, head, counts.at[p])
            features.append(feature)
            slopes[index].append((residual * share).astype(jnp.bfloat16))
        feat_last[left[p]] = jnp.concatenate(features, axis=0)
    at = jnp.concatenate(
        [pick_rows(d_ref, middle_of(cols.at[p]), slice_e) for p in range(len(pieces))], axis=1
    )
    slopes = [jnp.concatenate(parts, axis=0) for parts in slopes]
    add_terms(at, slopes, acc_own, acc_other, slice_e)

    n_codes = code_rows(sizes, filters)
    place = lax.broadcasted_iota(jnp.int32, (n_codes, filters), 0) * filters
    place = place + lax.broadcasted_iota(jnp.int32, (n_codes, filters), 1)

    def chip_terms(told, feature):
        head_term = jnp.zeros((3, filters), jnp.float32)
        code_term = jnp.zeros((n_codes, filters), jnp.float32)
        for p in range(posts):
            residual = told[p : p + 1, 0:1]
            head_term = head_term + residual * feature[p]
            for kind, start in enumerate(code_starts(sizes, filters)):
                at_row = (kind + 1) * posts + p
                code = told[at_row : at_row + 1, 0:1].astype(jnp.int32) + start
                code_term = code_term + jnp.where(place == code, residual, 0.0)
        return head_term, code_term

    features = [
        [feat_own[p] for p in range(posts)],
        *[[feat_last.get((k, p), feat_near[0:3, :]) for p in range(posts)] for k in range(2)],
        [
            jnp.where(here == p, feat_far[0][0:3, :], feat_far[1][0:3, :])
            for p in range(posts)
        ],
    ]
    sums = [chip_terms(fact[...], feature) for fact, feature in zip(facts, features)]
    acc_other[n_rows:, :] = jnp.zeros((acc_other.shape[0] - n_rows, filters), jnp.float32)
    acc_other[n_rows : n_rows + 3, :] = tree_sum([total[0] for total in sums])
    acc_other[n_rows + 3 : n_rows + 3 + n_codes, :] = tree_sum([total[1] for total in sums])


def gather_kernel(z_ref, acc, own_facts, far_facts, near_facts, *refs):
    *terms, total_ref, pred_ref = refs
    posts = pred_ref.shape[0]
    for p in range(posts):
        pred_ref[pl.ds(p, 1)] = own_facts[5 * posts + p, 0:1]
    made = made_residuals(z_ref[0], posts, own_facts, far_facts, near_facts)
    total_ref[...] = acc[...] + scaled_sum(made, terms)


def tree_sum(values):
    while len(values) > 1:
        values = [values[i] + values[i + 1] for i in range(0, len(values), 2)]
    return values[0]


def code_starts(sizes, filters):
    starts, start = [], 0
    for size in sizes:
        starts.append(start)
        start += -(-size // filters) * filters
    return starts


def code_rows(sizes, filters):
    return sum(-(-size // filters) for size in sizes)


def swap_kernel(sizes, own_ref, mine_ref, came_ref, grad_ref, head_ref, *code_refs):
    n_rows, filters = own_ref.shape
    grad_ref[...] = own_ref[...] + came_ref[0:n_rows, :]
    head_ref[...] = mine_ref[n_rows : n_rows + 3, :] + came_ref[n_rows : n_rows + 3, :]
    row = n_rows + 3
    for size, ref in zip(sizes, code_refs):
        for start in range(0, size, filters):
            count = min(filters, size - start)
            total = mine_ref[row : row + 1, :] + came_ref[row : row + 1, :]
            ref[pl.ds(start, count)] = total[0, :count]
            row += 1


def local_gather(n_doc, n_filt, *args):
    (
        embedded,
        lengths,
        conv_weight,
        head_weight,
        occupation,
        cohort,
        education,
        occ_table,
        cohort_table,
        edu_table,
        wage,
    ) = args
    posts, seq_len, dims = embedded.shape
    filters = conv_weight.shape[2]
    slice_e = dims // n_doc
    sizes = (occ_table.shape[0], cohort_table.shape[0], edu_table.shape[0])
    f32, i32 = jnp.float32, jnp.int32
    me = lax.axis_index("doc").astype(i32).reshape(1)
    vmem = pl.BlockSpec(memory_space=pltpu.VMEM)
    smem = pl.BlockSpec(memory_space=pltpu.SMEM)
    anywhere = pl.BlockSpec(memory_space=pl.ANY)
    hbm = pl.BlockSpec(memory_space=pltpu.HBM)

    def posts_scratch(n):
        return [
            pltpu.VMEM((n, seq_len + 2 * PAD, dims), f32),
            pltpu.VMEM((n, 8, filters), f32),
            pltpu.VMEM((n, seq_len, (2 * REACH + 1) * dims), jnp.bfloat16),
        ]

    def swap(x, k, axis="doc"):
        size = n_doc if axis == "doc" else n_filt
        return lax.ppermute(x, axis, [(i, i ^ k) for i in range(size)])


    def call(kernel, specs, out, scratch=(), cost=1):
        def run(*operands):
            operands = [
                pltpu.with_memory_space_constraint(x, pltpu.HBM) if spec is hbm else x
                for x, spec in zip(operands, specs)
            ]
            return built(*operands)

        built = pl.pallas_call(
            kernel,
            in_specs=specs,
            out_specs=[vmem] * len(out),
            out_shape=[
                jax.ShapeDtypeStruct(x, f32) if isinstance(x, tuple) else x for x in out
            ],
            scratch_shapes=list(scratch),
            compiler_params=pltpu.CompilerParams(vmem_limit_bytes=24 << 20),
            cost_estimate=pl.CostEstimate(flops=cost, bytes_accessed=1, transcendentals=0),
        )
        return run

    acc_shape = (TAPS * slice_e, filters)
    n_facts = -(-6 * posts // 8) * 8
    weights = jnp.transpose(conv_weight, (1, 0, 2)).reshape(TAPS * dims, filters)
    half = (lax.axis_index("filt").astype(i32) & 1).reshape(1)
    pieces, far_piece = call(
        mask_kernel,
        [smem] * 2 + [hbm] * 2,
        [(posts, seq_len, dims), (seq_len, dims)],
        [
            pltpu.VMEM((posts, seq_len, dims), jnp.bfloat16),
            pltpu.SMEM((posts,), i32),
            pltpu.SemaphoreType.DMA((posts + 1,)),
        ],
        cost=10000000000,
    )(me, half, lengths, embedded)

    near = [k for k in range(2, n_doc, 2) if bin(k).count("1") == 1][::-1]
    far = sum(near)
    far_one = swap(far_piece, far)
    near_pieces = [swap(pieces, k) for k in near]

    part, feat_own, share_own, base = call(
        own_kernel,
        [hbm] * 7 + [vmem] * 3,
        [
            (8, 128),
            (posts, 3, filters),
            (posts, 3, seq_len, filters),
            (n_facts, 128),
        ],
        [pltpu.SMEM((posts,), i32)] * 3
        + [pltpu.SMEM((posts,), f32)]
        + [pltpu.SMEM((size,), f32) for size in sizes]
        + [posts_scratch(posts)[i] for i in (0, 2, 1)]
        + [pltpu.SemaphoreType.DMA((7,))],
    )(
        occupation,
        cohort,
        education,
        wage,
        occ_table,
        cohort_table,
        edu_table,
        weights,
        pieces,
        head_weight,
    )

    def terms_of(x, keep, cost=1):
        feat, *terms = call(
            functools.partial(one_kernel, len(keep), slice_e),
            [smem] + [vmem] * 3 + [anywhere] * len(keep),
            [(8, filters)] + [(1,) + acc_shape] * 2,
            posts_scratch(1),
            cost,
        )(me, x, weights, head_weight, *keep)
        return feat, terms

    own_terms = call(
        functools.partial(own_terms_kernel, slice_e),
        [smem, vmem, vmem],
        [(posts,) + acc_shape] * 2,
        cost=1,
    )(me, pieces, share_own)
    parts = [part] + [swap(part, k, "filt") for k in range(2, n_filt)]
    first_part, far_one = lax.optimization_barrier((part, far_one))
    parts.insert(1, swap(first_part, 1, "filt"))
    parts[-1], share_held = lax.optimization_barrier((parts[-1], share_own))
    far_two = swap(far_one, 1, "filt")
    far_feat, far_terms = terms_of(far_one[None], (), 4000000000)
    parts, far_feat, far_terms, own_terms = lax.optimization_barrier(
        (parts, far_feat, far_terms, own_terms)
    )
    keep = [*own_terms, *far_terms]
    (facts,) = call(
        functools.partial(facts_kernel, posts, len(keep)),
        [vmem] * (1 + len(parts)) + [anywhere] * len(keep),
        [(n_facts, 128)],
    )(base, *parts, *keep)

    all_facts = [facts] + [swap(facts, k) for k in near] + [swap(facts, far)]
    far_feat_two, far_terms_two = terms_of(far_two[None], keep)
    keep += far_terms_two
    near_feat, near_terms = terms_of(near_pieces[0], keep)
    terms = list(zip(own_terms, far_terms, far_terms_two, near_terms))
    extra = -(-(3 + code_rows(sizes, filters)) // 8) * 8
    acc_own, acc_other = call(
        functools.partial(last_kernel, sizes, slice_e),
        [smem] * 2 + [vmem] * 16,
        [acc_shape, (acc_shape[0] + extra, filters)],
        posts_scratch(2 * posts - 1),
    )(
        me,
        half,
        *all_facts,
        *near_pieces,
        feat_own,
        far_feat,
        far_feat_two,
        near_feat,
        *terms[1],
        weights,
        head_weight,
    )

    came = swap(acc_other, 1)
    total, prediction = call(gather_kernel, [smem] + [vmem] * 8, [acc_shape, (posts,)])(
        half, acc_own, all_facts[0], all_facts[3], all_facts[1 + EARLY], *terms[0]
    )
    grad, head_grad, *codes = call(
        functools.partial(swap_kernel, sizes),
        [vmem] * 3,
        [acc_shape, (3, filters)] + [(size,) for size in sizes],
    )(total, acc_other, came)
    conv_grad = jnp.transpose(grad.reshape(TAPS, slice_e, filters), (1, 0, 2))
    return (conv_grad, head_grad, *codes, prediction)


def solution(mesh):
    n_doc, n_filt = mesh.shape["doc"], mesh.shape["filt"]
    if n_doc == 8 and n_filt == 4:
        local = functools.partial(local_gather, n_doc, n_filt)
    else:
        local = local_scatter
    return jax.shard_map(
        local,
        mesh=mesh,
        in_specs=(
            P("doc", None, None),
            P("doc"),
            P(None, None, "filt"),
            P(None, "filt"),
            P("doc"),
            P("doc"),
            P("doc"),
            P(),
            P(),
            P(),
            P("doc"),
        ),
        out_specs=(P("doc", None, "filt"), P(None, "filt"), P(), P(), P(), P("doc")),
        check_vma=False,
    )
```

```python
import functools

import jax
import jax.numpy as jnp
import numpy as np
from jax import lax
from jax.experimental import pallas as pl
from jax.experimental.pallas import tpu as pltpu
from jax.sharding import PartitionSpec as P

TAU = 0.05
WIDTH_LIST = ((3, 0), (5, 3), (7, 8))
TAPS = 15
REACH = 3
PAD = 8
EARLY = 0
OUTSIDE = np.float32(1024.0)
BY_LAST = (((1,), (1,)), ((), ()))


def convolve(columns, weights):
    outputs = []
    for taps, first in WIDTH_LIST:
        half = (taps - 1) // 2
        window = columns[:, :, 3 - half : 3 + half + 1, :]
        outputs.append(
            jnp.einsum(
                "ptje,ejf->ptf",
                window,
                weights[:, first : first + taps, :],
                preferred_element_type=jnp.float32,
            )
        )
    return tuple(outputs)


def grad_terms(columns, slopes):
    outputs = []
    for index in range(3):
        taps = WIDTH_LIST[index][0]
        half = (taps - 1) // 2
        window = columns[:, :, 3 - half : 3 + half + 1, :]
        outputs.append(
            jnp.einsum("ptje,ptf->ejf", window, slopes[index], preferred_element_type=jnp.float32)
        )
    return jnp.concatenate(outputs, axis=1)


def one_hots(codes, size):
    return (codes[:, None] == jnp.arange(size, dtype=jnp.int32)[None, :]).astype(jnp.float32)


def local_scatter(
    embedded,
    lengths,
    conv_weight,
    head_weight,
    occupation,
    cohort,
    education,
    occ_table,
    cohort_table,
    edu_table,
    wage,
):
    posts, seq_len, _ = embedded.shape
    positions = jnp.arange(seq_len, dtype=jnp.int32)
    valid = positions[None, :] < lengths[:, None]
    masked = jnp.where(valid[:, :, None], embedded, jnp.zeros_like(embedded))
    padded = jnp.pad(masked, ((0, 0), (3, 3), (0, 0)))
    columns = jnp.stack([padded[:, offset : offset + seq_len, :] for offset in range(7)], axis=2)
    convs = convolve(columns, conv_weight)
    features = []
    shares = []
    for conv in convs:
        score = jnp.where(valid[:, :, None], conv / TAU, -jnp.inf)
        top = jnp.max(score, axis=1, keepdims=True)
        expd = jnp.exp(score - top)
        total = jnp.sum(expd, axis=1, keepdims=True)
        features.append(TAU * (top[:, 0, :] + jnp.log(total[:, 0, :])))
        shares.append(expd / total)
    feature = jnp.stack(features, axis=1)
    head = head_weight.astype(jnp.float32)
    partial_pred = jnp.sum(feature * head[None, :, :], axis=(1, 2))
    occ_hot = one_hots(occupation, occ_table.shape[0])
    cohort_hot = one_hots(cohort, cohort_table.shape[0])
    edu_hot = one_hots(education, edu_table.shape[0])
    highest = lax.Precision.HIGHEST
    offsets = (
        jnp.dot(occ_hot, occ_table, precision=highest)
        + jnp.dot(cohort_hot, cohort_table, precision=highest)
        + jnp.dot(edu_hot, edu_table, precision=highest)
    )
    prediction = lax.psum(partial_pred, "filt") + offsets
    residual = prediction - wage
    slopes = [
        (residual[:, None, None] * head[index][None, None, :] * shares[index]).astype(jnp.bfloat16)
        for index in range(3)
    ]
    conv_grad = lax.psum_scatter(
        grad_terms(columns, slopes), "doc", scatter_dimension=0, tiled=True
    )
    head_terms = jnp.sum(residual[:, None, None] * feature, axis=0)
    head_grad, occ_grad, cohort_grad, edu_grad = lax.psum(
        (
            head_terms,
            jnp.dot(residual, occ_hot, precision=highest),
            jnp.dot(residual, cohort_hot, precision=highest),
            jnp.dot(residual, edu_hot, precision=highest),
        ),
        "doc",
    )
    return (conv_grad, head_grad, occ_grad, cohort_grad, edu_grad, prediction)


def load_post(x, xpad, count):
    rows, width = x.shape
    inside = x < OUTSIDE
    xpad[0:PAD, :] = jnp.zeros((PAD, width), jnp.float32)
    xpad[PAD + rows :, :] = jnp.zeros((PAD, width), jnp.float32)
    xpad[PAD : PAD + rows, :] = jnp.where(inside, x, 0.0)
    total = jnp.sum(inside.astype(jnp.float32), axis=0, keepdims=True)
    count[...] = jnp.broadcast_to(total[:, 0:1], count.shape)


def make_cols(xpad, cols):
    rows, width = cols.shape[0], xpad.shape[1]
    for offset in range(2 * REACH + 1):
        start = PAD - REACH + offset
        cols[:, offset * width : (offset + 1) * width] = xpad[start : start + rows, :].astype(
            jnp.bfloat16
        )


def forward(index, cols, w_ref, head, count):
    taps, first = WIDTH_LIST[index]
    half = taps // 2
    width = w_ref.shape[0] // TAPS
    conv = jnp.dot(
        cols[:, (REACH - half) * width : (REACH + half + 1) * width],
        w_ref[first * width : (first + taps) * width, :],
        preferred_element_type=jnp.float32,
    )
    place = lax.broadcasted_iota(jnp.int32, conv.shape, 0).astype(jnp.float32)
    score = jnp.where(place < count[0:1, :], conv * np.float32(1.0 / TAU), -jnp.inf)
    top = jnp.max(score, axis=0, keepdims=True)
    expd = jnp.exp(score - top)
    total = jnp.sum(expd, axis=0, keepdims=True)
    feature = np.float32(TAU) * (top + jnp.log(total))
    return feature, expd * (head[index : index + 1] / total)


def pick_rows(d_ref, middle, slice_e):
    rows, width = middle.shape
    me = d_ref[0]
    row = lax.broadcasted_iota(jnp.int32, (2 * slice_e, width), 0)
    lane = lax.broadcasted_iota(jnp.int32, (2 * slice_e, width), 1)
    wanted = jnp.where(row < slice_e, me * slice_e + row, (me ^ 1) * slice_e + row - slice_e)
    pick = (lane == wanted).astype(jnp.bfloat16)
    across = lax.dot_general(pick, middle, BY_LAST, preferred_element_type=jnp.float32)
    place = lax.broadcasted_iota(jnp.int32, (2 * slice_e, rows), 1)
    parts = []
    for offset in range(-REACH, REACH + 1):
        if offset:
            moved = pltpu.roll(across, (-offset) % rows, 1)
            inside = (place + offset >= 0) & (place + offset < rows)
            parts.append(jnp.where(inside, moved, 0.0))
        else:
            parts.append(across)
    return jnp.concatenate(parts, axis=0).astype(jnp.bfloat16)


def middle_of(cols):
    width = cols.shape[1] // (2 * REACH + 1)
    return cols[:, REACH * width : (REACH + 1) * width]


def add_terms(at, slopes, acc_own, acc_other, slice_e, fresh=False):
    step = 2 * slice_e
    for index, (taps, first) in list(enumerate(WIDTH_LIST))[::-1]:
        half = taps // 2
        term = jnp.dot(
            at[(REACH - half) * step : (REACH + half + 1) * step],
            slopes[index],
            preferred_element_type=jnp.float32,
        )
        for j in range(taps):
            place = slice((first + j) * slice_e, (first + j + 1) * slice_e)
            own = term[j * step : j * step + slice_e]
            other = term[j * step + slice_e : (j + 1) * step]
            if fresh:
                acc_own[place, :] = own
                acc_other[place, :] = other
            else:
                acc_own[place, :] += own
                acc_other[place, :] += other


def mask_kernel(d_ref, z_ref, len_any, x_any, pieces, far_piece, x_ref, len_ref, sems):
    posts, rows, width = x_ref.shape
    copies = [pltpu.make_async_copy(len_any, len_ref, sems.at[posts])]
    copies += [pltpu.make_async_copy(x_any.at[p], x_ref.at[p], sems.at[p]) for p in range(posts)]
    for copy in copies:
        copy.start()
    place = lax.broadcasted_iota(jnp.int32, (rows, width), 0)
    copies[0].wait()
    for p in range(posts):
        copies[1 + p].wait()
        pieces[p] = jnp.where(place < len_ref[p], x_ref[p].astype(jnp.float32), OUTSIDE)
    far_piece[...] = pieces[z_ref[0]]


def own_kernel(*refs):
    small = refs[:7]
    w_ref, pieces, head_ref, part_ref, feat_ref, share_ref, base_ref = refs[7:14]
    held = refs[14:21]
    xpad, cols, counts, small_sems = refs[21:]
    posts = pieces.shape[0]
    copies = [pltpu.make_async_copy(small[i], held[i], small_sems.at[i]) for i in range(7)]
    for copy in copies:
        copy.start()
    for p in range(posts):
        load_post(pieces[p], xpad.at[p], counts.at[p])
        make_cols(xpad.at[p], cols.at[p])
    head = head_ref[...].astype(jnp.float32)
    parts = [jnp.zeros((1, head.shape[1]), jnp.float32) for _ in range(posts)]
    for index in (2, 1, 0):
        for p in range(posts):
            feature, share = forward(index, cols.at[p], w_ref, head, counts.at[p])
            feat_ref[p, index : index + 1, :] = feature
            share_ref[p, index] = share
            parts[p] = parts[p] + feature * head[index : index + 1]
    lanes = part_ref.shape[1]
    part_ref[...] = jnp.zeros_like(part_ref)
    for p in range(posts):
        total = jnp.sum(parts[p], axis=1, keepdims=True)
        part_ref[p : p + 1, :] = jnp.broadcast_to(total, (1, lanes))
    for copy in copies:
        copy.wait()
    codes, wage_ref, tables = held[:3], held[3], held[4:]
    base_ref[...] = jnp.zeros_like(base_ref)
    for p in range(posts):
        offset = sum(table[code[p]] for code, table in zip(codes, tables))
        values = [offset] + [code[p].astype(jnp.float32) for code in codes] + [wage_ref[p]]
        for kind, value in enumerate(values):
            row = kind * posts + p
            base_ref[row : row + 1, :] = jnp.full((1, lanes), value, jnp.float32)


def own_terms_kernel(slice_e, d_ref, pieces, share_ref, own_ref, other_ref):
    for p in range(pieces.shape[0]):
        x = pieces[p]
        at = pick_rows(d_ref, jnp.where(x < OUTSIDE, x, 0.0).astype(jnp.bfloat16), slice_e)
        slopes = [share_ref[p, index].astype(jnp.bfloat16) for index in range(3)]
        add_terms(at, slopes, own_ref.at[p], other_ref.at[p], slice_e, fresh=True)


def facts_kernel(posts, n_keep, base, *refs):
    facts_ref = refs[-1]
    facts_ref[...] = base[...]
    total = tree_sum([part[...] for part in refs[: len(refs) - 1 - n_keep]])
    for p in range(posts):
        value = total[p : p + 1, :] + base[p : p + 1, :]
        facts_ref[p : p + 1, :] = value - base[4 * posts + p : 4 * posts + p + 1, :]
        facts_ref[5 * posts + p : 5 * posts + p + 1, :] = value


def one_kernel(n_keep, slice_e, d_ref, x_ref, w_ref, head_ref, *refs):
    feat_ref, own_ref, other_ref, xpads, counts, cols = refs[n_keep:]
    head = head_ref[...].astype(jnp.float32)
    load_post(x_ref[0], xpads.at[0], counts.at[0])
    make_cols(xpads.at[0], cols.at[0])
    at = pick_rows(d_ref, middle_of(cols.at[0]), slice_e)
    slopes = [None] * 3
    for index in (2, 1, 0):
        feature, share = forward(index, cols.at[0], w_ref, head, counts.at[0])
        feat_ref[index : index + 1, :] = feature
        slopes[index] = share.astype(jnp.bfloat16)
    add_terms(at, slopes, own_ref.at[0], other_ref.at[0], slice_e, fresh=True)


def made_residuals(here, posts, own, far, near):
    rows = [own[p : p + 1, 0:1] for p in range(posts)]
    return rows + [far[pl.ds(here, 1), 0:1], far[pl.ds(1 - here, 1), 0:1], near[0:1, 0:1]]


def scaled_sum(residuals, terms):
    total, i = 0.0, 0
    for term in terms:
        for p in range(term.shape[0]):
            total = total + residuals[i] * term[p]
            i += 1
    return total


def last_kernel(sizes, slice_e, d_ref, z_ref, *refs):
    facts, near = refs[:4], refs[4:6]
    (feat_own, *feat_far, feat_near), terms = refs[6:10], refs[10:14]
    w_ref, head_ref, acc_own, acc_other, xpads, counts, cols = refs[14:]
    posts = near[0].shape[0]
    n_rows, filters = acc_own.shape
    head = head_ref[...].astype(jnp.float32)
    here = z_ref[0]
    left = [(k, p) for k in range(2) for p in range(posts) if (k, p) != (EARLY, 0)]
    pieces = [near[k][p] for k, p in left]
    residuals = [facts[1 + k][p : p + 1, 0:1] for k, p in left]
    for p, piece in enumerate(pieces):
        load_post(piece, xpads.at[p], counts.at[p])
        make_cols(xpads.at[p], cols.at[p])
    acc_own[...] = jnp.zeros_like(acc_own)
    acc_other[0:n_rows, :] = scaled_sum(
        made_residuals(here, posts, facts[0], facts[3], facts[1 + EARLY]), terms
    )
    slopes = [[], [], []]
    feat_last = {}
    for p, residual in enumerate(residuals):
        features = []
        for index in range(3):
            feature, share = forward(index, cols.at[p], w_ref, head, counts.at[p])
            features.append(feature)
            slopes[index].append((residual * share).astype(jnp.bfloat16))
        feat_last[left[p]] = jnp.concatenate(features, axis=0)
    at = jnp.concatenate(
        [pick_rows(d_ref, middle_of(cols.at[p]), slice_e) for p in range(len(pieces))], axis=1
    )
    slopes = [jnp.concatenate(parts, axis=0) for parts in slopes]
    add_terms(at, slopes, acc_own, acc_other, slice_e)

    n_codes = code_rows(sizes, filters)
    place = lax.broadcasted_iota(jnp.int32, (n_codes, filters), 0) * filters
    place = place + lax.broadcasted_iota(jnp.int32, (n_codes, filters), 1)

    def chip_terms(told, feature):
        head_term = jnp.zeros((3, filters), jnp.float32)
        code_term = jnp.zeros((n_codes, filters), jnp.float32)
        for p in range(posts):
            residual = told[p : p + 1, 0:1]
            head_term = head_term + residual * feature[p]
            for kind, start in enumerate(code_starts(sizes, filters)):
                at_row = (kind + 1) * posts + p
                code = told[at_row : at_row + 1, 0:1].astype(jnp.int32) + start
                code_term = code_term + jnp.where(place == code, residual, 0.0)
        return head_term, code_term

    features = [
        [feat_own[p] for p in range(posts)],
        *[[feat_last.get((k, p), feat_near[0:3, :]) for p in range(posts)] for k in range(2)],
        [
            jnp.where(here == p, feat_far[0][0:3, :], feat_far[1][0:3, :])
            for p in range(posts)
        ],
    ]
    sums = [chip_terms(fact[...], feature) for fact, feature in zip(facts, features)]
    acc_other[n_rows:, :] = jnp.zeros((acc_other.shape[0] - n_rows, filters), jnp.float32)
    acc_other[n_rows : n_rows + 3, :] = tree_sum([total[0] for total in sums])
    acc_other[n_rows + 3 : n_rows + 3 + n_codes, :] = tree_sum([total[1] for total in sums])


def gather_kernel(z_ref, acc, own_facts, far_facts, near_facts, *refs):
    *terms, total_ref, pred_ref = refs
    posts = pred_ref.shape[0]
    for p in range(posts):
        pred_ref[pl.ds(p, 1)] = own_facts[5 * posts + p, 0:1]
    made = made_residuals(z_ref[0], posts, own_facts, far_facts, near_facts)
    total_ref[...] = acc[...] + scaled_sum(made, terms)


def tree_sum(values):
    while len(values) > 1:
        values = [values[i] + values[i + 1] for i in range(0, len(values), 2)]
    return values[0]


def code_starts(sizes, filters):
    starts, start = [], 0
    for size in sizes:
        starts.append(start)
        start += -(-size // filters) * filters
    return starts


def code_rows(sizes, filters):
    return sum(-(-size // filters) for size in sizes)


def swap_kernel(sizes, own_ref, mine_ref, came_ref, grad_ref, head_ref, *code_refs):
    n_rows, filters = own_ref.shape
    grad_ref[...] = own_ref[...] + came_ref[0:n_rows, :]
    head_ref[...] = mine_ref[n_rows : n_rows + 3, :] + came_ref[n_rows : n_rows + 3, :]
    row = n_rows + 3
    for size, ref in zip(sizes, code_refs):
        for start in range(0, size, filters):
            count = min(filters, size - start)
            total = mine_ref[row : row + 1, :] + came_ref[row : row + 1, :]
            ref[pl.ds(start, count)] = total[0, :count]
            row += 1


def local_gather(n_doc, n_filt, *args):
    (
        embedded,
        lengths,
        conv_weight,
        head_weight,
        occupation,
        cohort,
        education,
        occ_table,
        cohort_table,
        edu_table,
        wage,
    ) = args
    posts, seq_len, dims = embedded.shape
    filters = conv_weight.shape[2]
    slice_e = dims // n_doc
    sizes = (occ_table.shape[0], cohort_table.shape[0], edu_table.shape[0])
    f32, i32 = jnp.float32, jnp.int32
    me = lax.axis_index("doc").astype(i32).reshape(1)
    vmem = pl.BlockSpec(memory_space=pltpu.VMEM)
    smem = pl.BlockSpec(memory_space=pltpu.SMEM)
    anywhere = pl.BlockSpec(memory_space=pl.ANY)
    hbm = pl.BlockSpec(memory_space=pltpu.HBM)

    def posts_scratch(n):
        return [
            pltpu.VMEM((n, seq_len + 2 * PAD, dims), f32),
            pltpu.VMEM((n, 8, filters), f32),
            pltpu.VMEM((n, seq_len, (2 * REACH + 1) * dims), jnp.bfloat16),
        ]

    def swap(x, k, axis="doc"):
        size = n_doc if axis == "doc" else n_filt
        return lax.ppermute(x, axis, [(i, i ^ k) for i in range(size)])

    def call(kernel, specs, out, scratch=(), cost=1):
        def run(*operands):
            operands = [
                pltpu.with_memory_space_constraint(x, pltpu.HBM) if spec is hbm else x
                for x, spec in zip(operands, specs)
            ]
            return built(*operands)

        built = pl.pallas_call(
            kernel,
            in_specs=specs,
            out_specs=[vmem] * len(out),
            out_shape=[
                jax.ShapeDtypeStruct(x, f32) if isinstance(x, tuple) else x for x in out
            ],
            scratch_shapes=list(scratch),
            compiler_params=pltpu.CompilerParams(vmem_limit_bytes=24 << 20),
            cost_estimate=pl.CostEstimate(flops=cost, bytes_accessed=1, transcendentals=0),
        )
        return run

    acc_shape = (TAPS * slice_e, filters)
    n_facts = -(-6 * posts // 8) * 8
    weights = jnp.transpose(conv_weight, (1, 0, 2)).reshape(TAPS * dims, filters)
    half = (lax.axis_index("filt").astype(i32) & 1).reshape(1)
    pieces, far_piece = call(
        mask_kernel,
        [smem] * 2 + [hbm] * 2,
        [(posts, seq_len, dims), (seq_len, dims)],
        [
            pltpu.VMEM((posts, seq_len, dims), jnp.bfloat16),
            pltpu.SMEM((posts,), i32),
            pltpu.SemaphoreType.DMA((posts + 1,)),
        ],
        cost=10**10,
    )(me, half, lengths, embedded)

    near = [k for k in range(2, n_doc, 2) if bin(k).count("1") == 1][::-1]
    far = sum(near)
    far_one = swap(far_piece, far)
    near_pieces = [swap(pieces, k) for k in near]

    part, feat_own, share_own, base = call(
        own_kernel,
        [hbm] * 7 + [vmem] * 3,
        [
            (8, 128),
            (posts, 3, filters),
            (posts, 3, seq_len, filters),
            (n_facts, 128),
        ],
        [pltpu.SMEM((posts,), i32)] * 3
        + [pltpu.SMEM((posts,), f32)]
        + [pltpu.SMEM((size,), f32) for size in sizes]
        + [posts_scratch(posts)[i] for i in (0, 2, 1)]
        + [pltpu.SemaphoreType.DMA((7,))],
    )(
        occupation,
        cohort,
        education,
        wage,
        occ_table,
        cohort_table,
        edu_table,
        weights,
        pieces,
        head_weight,
    )

    def terms_of(x, keep, cost=1):
        feat, *terms = call(
            functools.partial(one_kernel, len(keep), slice_e),
            [smem] + [vmem] * 3 + [anywhere] * len(keep),
            [(8, filters)] + [(1,) + acc_shape] * 2,
            posts_scratch(1),
            cost,
        )(me, x, weights, head_weight, *keep)
        return feat, terms

    parts = [part] + [swap(part, k, "filt") for k in range(2, n_filt)]
    first_part, far_one = lax.optimization_barrier((part, far_one))
    parts.insert(1, swap(first_part, 1, "filt"))
    own_terms = call(
        functools.partial(own_terms_kernel, slice_e),
        [smem, vmem, vmem],
        [(posts,) + acc_shape] * 2,
    )(me, pieces, share_own)
    far_two = swap(far_one, 1, "filt")
    far_feat, far_terms = terms_of(far_one[None], (), 4 * 10**9)
    parts, far_feat, far_terms, own_terms = lax.optimization_barrier(
        (parts, far_feat, far_terms, own_terms)
    )
    keep = [*own_terms, *far_terms]
    (facts,) = call(
        functools.partial(facts_kernel, posts, len(keep)),
        [vmem] * (1 + len(parts)) + [anywhere] * len(keep),
        [(n_facts, 128)],
    )(base, *parts, *keep)

    all_facts = [facts] + [swap(facts, k) for k in near] + [swap(facts, far)]
    far_feat_two, far_terms_two = terms_of(far_two[None], keep)
    keep += far_terms_two
    near_feat, near_terms = terms_of(near_pieces[0], keep)
    terms = list(zip(own_terms, far_terms, far_terms_two, near_terms))
    extra = -(-(3 + code_rows(sizes, filters)) // 8) * 8
    acc_own, acc_other = call(
        functools.partial(last_kernel, sizes, slice_e),
        [smem] * 2 + [vmem] * 16,
        [acc_shape, (acc_shape[0] + extra, filters)],
        posts_scratch(2 * posts - 1),
    )(
        me,
        half,
        *all_facts,
        *near_pieces,
        feat_own,
        far_feat,
        far_feat_two,
        near_feat,
        *terms[1],
        weights,
        head_weight,
    )

    came = swap(acc_other, 1)
    total, prediction = call(gather_kernel, [smem] + [vmem] * 8, [acc_shape, (posts,)])(
        half, acc_own, all_facts[0], all_facts[3], all_facts[1 + EARLY], *terms[0]
    )
    grad, head_grad, *codes = call(
        functools.partial(swap_kernel, sizes),
        [vmem] * 3,
        [acc_shape, (3, filters)] + [(size,) for size in sizes],
    )(total, acc_other, came)
    conv_grad = jnp.transpose(grad.reshape(TAPS, slice_e, filters), (1, 0, 2))
    return (conv_grad, head_grad, *codes, prediction)


def solution(mesh):
    n_doc, n_filt = mesh.shape["doc"], mesh.shape["filt"]

    def local(*args):
        if (n_doc, n_filt, args[0].shape[0]) == (8, 4, 2):
            return local_gather(n_doc, n_filt, *args)
        return local_scatter(*args)

    return jax.shard_map(
        local,
        mesh=mesh,
        in_specs=(
            P("doc", None, None),
            P("doc"),
            P(None, None, "filt"),
            P(None, "filt"),
            P("doc"),
            P("doc"),
            P("doc"),
            P(),
            P(),
            P(),
            P("doc"),
        ),
        out_specs=(P("doc", None, "filt"), P(None, "filt"), P(), P(), P(), P("doc")),
        check_vma=False,
    )
```

```python
import functools

import jax
import jax.numpy as jnp
import numpy as np
from jax import lax
from jax.experimental import pallas as pl
from jax.experimental.pallas import tpu as pltpu
from jax.sharding import PartitionSpec as P

TAU = 0.05
WIDTH_LIST = ((3, 0), (5, 3), (7, 8))
TAPS = 15
REACH = 3
PAD = 8
EARLY = 0
OUTSIDE = np.float32(1024.0)
BY_LAST = (((1,), (1,)), ((), ()))


def convolve(columns, weights):
    outputs = []
    for taps, first in WIDTH_LIST:
        half = (taps - 1) // 2
        window = columns[:, :, 3 - half : 3 + half + 1, :]
        outputs.append(
            jnp.einsum(
                "ptje,ejf->ptf",
                window,
                weights[:, first : first + taps, :],
                preferred_element_type=jnp.float32,
            )
        )
    return tuple(outputs)


def grad_terms(columns, slopes):
    outputs = []
    for index in range(3):
        taps = WIDTH_LIST[index][0]
        half = (taps - 1) // 2
        window = columns[:, :, 3 - half : 3 + half + 1, :]
        outputs.append(
            jnp.einsum("ptje,ptf->ejf", window, slopes[index], preferred_element_type=jnp.float32)
        )
    return jnp.concatenate(outputs, axis=1)


def one_hots(codes, size):
    return (codes[:, None] == jnp.arange(size, dtype=jnp.int32)[None, :]).astype(jnp.float32)


def local_scatter(
    embedded,
    lengths,
    conv_weight,
    head_weight,
    occupation,
    cohort,
    education,
    occ_table,
    cohort_table,
    edu_table,
    wage,
):
    posts, seq_len, _ = embedded.shape
    positions = jnp.arange(seq_len, dtype=jnp.int32)
    valid = positions[None, :] < lengths[:, None]
    masked = jnp.where(valid[:, :, None], embedded, jnp.zeros_like(embedded))
    padded = jnp.pad(masked, ((0, 0), (3, 3), (0, 0)))
    columns = jnp.stack([padded[:, offset : offset + seq_len, :] for offset in range(7)], axis=2)
    convs = convolve(columns, conv_weight)
    features = []
    shares = []
    for conv in convs:
        score = jnp.where(valid[:, :, None], conv / TAU, -jnp.inf)
        top = jnp.max(score, axis=1, keepdims=True)
        expd = jnp.exp(score - top)
        total = jnp.sum(expd, axis=1, keepdims=True)
        features.append(TAU * (top[:, 0, :] + jnp.log(total[:, 0, :])))
        shares.append(expd / total)
    feature = jnp.stack(features, axis=1)
    head = head_weight.astype(jnp.float32)
    partial_pred = jnp.sum(feature * head[None, :, :], axis=(1, 2))
    occ_hot = one_hots(occupation, occ_table.shape[0])
    cohort_hot = one_hots(cohort, cohort_table.shape[0])
    edu_hot = one_hots(education, edu_table.shape[0])
    highest = lax.Precision.HIGHEST
    offsets = (
        jnp.dot(occ_hot, occ_table, precision=highest)
        + jnp.dot(cohort_hot, cohort_table, precision=highest)
        + jnp.dot(edu_hot, edu_table, precision=highest)
    )
    prediction = lax.psum(partial_pred, "filt") + offsets
    residual = prediction - wage
    slopes = [
        (residual[:, None, None] * head[index][None, None, :] * shares[index]).astype(jnp.bfloat16)
        for index in range(3)
    ]
    conv_grad = lax.psum_scatter(
        grad_terms(columns, slopes), "doc", scatter_dimension=0, tiled=True
    )
    head_terms = jnp.sum(residual[:, None, None] * feature, axis=0)
    head_grad, occ_grad, cohort_grad, edu_grad = lax.psum(
        (
            head_terms,
            jnp.dot(residual, occ_hot, precision=highest),
            jnp.dot(residual, cohort_hot, precision=highest),
            jnp.dot(residual, edu_hot, precision=highest),
        ),
        "doc",
    )
    return (conv_grad, head_grad, occ_grad, cohort_grad, edu_grad, prediction)


def load_post(x, xpad, count):
    rows, width = x.shape
    inside = x < OUTSIDE
    xpad[0:PAD, :] = jnp.zeros((PAD, width), jnp.float32)
    xpad[PAD + rows :, :] = jnp.zeros((PAD, width), jnp.float32)
    xpad[PAD : PAD + rows, :] = jnp.where(inside, x, 0.0)
    total = jnp.sum(inside.astype(jnp.float32), axis=0, keepdims=True)
    count[...] = jnp.broadcast_to(total[:, 0:1], count.shape)


def make_cols(xpad, cols):
    rows, width = cols.shape[0], xpad.shape[1]
    for offset in range(2 * REACH + 1):
        start = PAD - REACH + offset
        cols[:, offset * width : (offset + 1) * width] = xpad[start : start + rows, :].astype(
            jnp.bfloat16
        )


def forward(index, cols, w_ref, head, count):
    taps, first = WIDTH_LIST[index]
    half = taps // 2
    width = w_ref.shape[0] // TAPS
    conv = jnp.dot(
        cols[:, (REACH - half) * width : (REACH + half + 1) * width],
        w_ref[first * width : (first + taps) * width, :],
        preferred_element_type=jnp.float32,
    )
    place = lax.broadcasted_iota(jnp.int32, conv.shape, 0).astype(jnp.float32)
    score = jnp.where(place < count[0:1, :], conv * np.float32(1.0 / TAU), -jnp.inf)
    top = jnp.max(score, axis=0, keepdims=True)
    expd = jnp.exp(score - top)
    total = jnp.sum(expd, axis=0, keepdims=True)
    feature = np.float32(TAU) * (top + jnp.log(total))
    return feature, expd * (head[index : index + 1] / total)


def pick_rows(d_ref, middle, slice_e):
    rows, width = middle.shape
    me = d_ref[0]
    row = lax.broadcasted_iota(jnp.int32, (2 * slice_e, width), 0)
    lane = lax.broadcasted_iota(jnp.int32, (2 * slice_e, width), 1)
    wanted = jnp.where(row < slice_e, me * slice_e + row, (me ^ 1) * slice_e + row - slice_e)
    pick = (lane == wanted).astype(jnp.bfloat16)
    across = lax.dot_general(pick, middle, BY_LAST, preferred_element_type=jnp.float32)
    place = lax.broadcasted_iota(jnp.int32, (2 * slice_e, rows), 1)
    parts = []
    for offset in range(-REACH, REACH + 1):
        if offset:
            moved = pltpu.roll(across, (-offset) % rows, 1)
            inside = (place + offset >= 0) & (place + offset < rows)
            parts.append(jnp.where(inside, moved, 0.0))
        else:
            parts.append(across)
    return jnp.concatenate(parts, axis=0).astype(jnp.bfloat16)


def middle_of(cols):
    width = cols.shape[1] // (2 * REACH + 1)
    return cols[:, REACH * width : (REACH + 1) * width]


def add_terms(at, slopes, acc_own, acc_other, slice_e, fresh=False):
    step = 2 * slice_e
    for index in (2, 1, 0) if fresh else (0, 1, 2):
        taps, first = WIDTH_LIST[index]
        half = taps // 2
        term = jnp.dot(
            at[(REACH - half) * step : (REACH + half + 1) * step],
            slopes[index],
            preferred_element_type=jnp.float32,
        )
        for j in range(taps):
            place = slice((first + j) * slice_e, (first + j + 1) * slice_e)
            own = term[j * step : j * step + slice_e]
            other = term[j * step + slice_e : (j + 1) * step]
            if fresh:
                acc_own[place, :] = own
                acc_other[place, :] = other
            else:
                acc_own[place, :] += own
                acc_other[place, :] += other


def mask_kernel(d_ref, z_ref, len_any, x_any, pieces, far_piece, x_ref, len_ref, sems):
    posts, rows, width = x_ref.shape
    copies = [pltpu.make_async_copy(len_any, len_ref, sems.at[posts])]
    copies += [pltpu.make_async_copy(x_any.at[p], x_ref.at[p], sems.at[p]) for p in range(posts)]
    for copy in copies:
        copy.start()
    place = lax.broadcasted_iota(jnp.int32, (rows, width), 0)
    copies[0].wait()
    for p in range(posts):
        copies[1 + p].wait()
        pieces[p] = jnp.where(place < len_ref[p], x_ref[p].astype(jnp.float32), OUTSIDE)
    far_piece[...] = pieces[z_ref[0]]


def own_kernel(*refs):
    small = refs[:7]
    w_ref, pieces, head_ref, part_ref, feat_ref, share_ref, base_ref = refs[7:14]
    held = refs[14:21]
    xpad, cols, counts, small_sems = refs[21:]
    posts = pieces.shape[0]
    copies = [pltpu.make_async_copy(small[i], held[i], small_sems.at[i]) for i in range(7)]
    for copy in copies:
        copy.start()
    for p in range(posts):
        load_post(pieces[p], xpad.at[p], counts.at[p])
        make_cols(xpad.at[p], cols.at[p])
    head = head_ref[...].astype(jnp.float32)
    parts = [jnp.zeros((1, head.shape[1]), jnp.float32) for _ in range(posts)]
    for index in (2, 1, 0):
        for p in range(posts):
            feature, share = forward(index, cols.at[p], w_ref, head, counts.at[p])
            feat_ref[p, index : index + 1, :] = feature
            share_ref[p, index] = share
            parts[p] = parts[p] + feature * head[index : index + 1]
    lanes = part_ref.shape[1]
    part_ref[...] = jnp.zeros_like(part_ref)
    for p in range(posts):
        total = jnp.sum(parts[p], axis=1, keepdims=True)
        part_ref[p : p + 1, :] = jnp.broadcast_to(total, (1, lanes))
    for copy in copies:
        copy.wait()
    codes, wage_ref, tables = held[:3], held[3], held[4:]
    base_ref[...] = jnp.zeros_like(base_ref)
    for p in range(posts):
        offset = sum(table[code[p]] for code, table in zip(codes, tables))
        values = [offset] + [code[p].astype(jnp.float32) for code in codes] + [wage_ref[p]]
        for kind, value in enumerate(values):
            row = kind * posts + p
            base_ref[row : row + 1, :] = jnp.full((1, lanes), value, jnp.float32)


def own_terms_kernel(slice_e, d_ref, pieces, share_ref, own_ref, other_ref):
    for p in range(pieces.shape[0]):
        x = pieces[p]
        at = pick_rows(d_ref, jnp.where(x < OUTSIDE, x, 0.0).astype(jnp.bfloat16), slice_e)
        slopes = [share_ref[p, index].astype(jnp.bfloat16) for index in range(3)]
        add_terms(at, slopes, own_ref.at[p], other_ref.at[p], slice_e, fresh=True)


def facts_kernel(posts, n_keep, base, *refs):
    facts_ref = refs[-1]
    facts_ref[...] = base[...]
    total = tree_sum([part[...] for part in refs[: len(refs) - 1 - n_keep]])
    for p in range(posts):
        value = total[p : p + 1, :] + base[p : p + 1, :]
        facts_ref[p : p + 1, :] = value - base[4 * posts + p : 4 * posts + p + 1, :]
        facts_ref[5 * posts + p : 5 * posts + p + 1, :] = value


def one_kernel(n_keep, slice_e, d_ref, x_ref, w_ref, head_ref, *refs):
    feat_ref, own_ref, other_ref, xpads, counts, cols = refs[n_keep:]
    head = head_ref[...].astype(jnp.float32)
    load_post(x_ref[0], xpads.at[0], counts.at[0])
    make_cols(xpads.at[0], cols.at[0])
    at = pick_rows(d_ref, middle_of(cols.at[0]), slice_e)
    slopes = [None] * 3
    for index in (2, 1, 0):
        feature, share = forward(index, cols.at[0], w_ref, head, counts.at[0])
        feat_ref[index : index + 1, :] = feature
        slopes[index] = share.astype(jnp.bfloat16)
    add_terms(at, slopes, own_ref.at[0], other_ref.at[0], slice_e, fresh=True)


def made_residuals(here, posts, own, far, near):
    rows = [own[p : p + 1, 0:1] for p in range(posts)]
    return rows + [far[pl.ds(here, 1), 0:1], far[pl.ds(1 - here, 1), 0:1], near[0:1, 0:1]]


def scaled_sum(residuals, terms):
    total, i = 0.0, 0
    for term in terms:
        for p in range(term.shape[0]):
            total = total + residuals[i] * term[p]
            i += 1
    return total


def last_kernel(sizes, slice_e, d_ref, z_ref, *refs):
    facts, near = refs[:4], refs[4:6]
    (feat_own, *feat_far, feat_near), terms = refs[6:10], refs[10:14]
    w_ref, head_ref, acc_own, acc_other, xpads, counts, cols = refs[14:]
    posts = near[0].shape[0]
    n_rows, filters = acc_own.shape
    head = head_ref[...].astype(jnp.float32)
    here = z_ref[0]
    left = [(k, p) for k in range(2) for p in range(posts) if (k, p) != (EARLY, 0)]
    pieces = [near[k][p] for k, p in left]
    residuals = [facts[1 + k][p : p + 1, 0:1] for k, p in left]
    for p, piece in enumerate(pieces):
        load_post(piece, xpads.at[p], counts.at[p])
        make_cols(xpads.at[p], cols.at[p])
    acc_own[...] = jnp.zeros_like(acc_own)
    acc_other[0:n_rows, :] = scaled_sum(
        made_residuals(here, posts, facts[0], facts[3], facts[1 + EARLY]), terms
    )
    slopes = [[], [], []]
    feat_last = {}
    for p, residual in enumerate(residuals):
        features = []
        for index in range(3):
            feature, share = forward(index, cols.at[p], w_ref, head, counts.at[p])
            features.append(feature)
            slopes[index].append((residual * share).astype(jnp.bfloat16))
        feat_last[left[p]] = jnp.concatenate(features, axis=0)
    at = jnp.concatenate(
        [pick_rows(d_ref, middle_of(cols.at[p]), slice_e) for p in range(len(pieces))], axis=1
    )
    slopes = [jnp.concatenate(parts, axis=0) for parts in slopes]
    add_terms(at, slopes, acc_own, acc_other, slice_e)

    n_codes = code_rows(sizes, filters)
    place = lax.broadcasted_iota(jnp.int32, (n_codes, filters), 0) * filters
    place = place + lax.broadcasted_iota(jnp.int32, (n_codes, filters), 1)

    def chip_terms(told, feature):
        head_term = jnp.zeros((3, filters), jnp.float32)
        code_term = jnp.zeros((n_codes, filters), jnp.float32)
        for p in range(posts):
            residual = told[p : p + 1, 0:1]
            head_term = head_term + residual * feature[p]
            for kind, start in enumerate(code_starts(sizes, filters)):
                at_row = (kind + 1) * posts + p
                code = told[at_row : at_row + 1, 0:1].astype(jnp.int32) + start
                code_term = code_term + jnp.where(place == code, residual, 0.0)
        return head_term, code_term

    features = [
        [feat_own[p] for p in range(posts)],
        *[[feat_last.get((k, p), feat_near[0:3, :]) for p in range(posts)] for k in range(2)],
        [
            jnp.where(here == p, feat_far[0][0:3, :], feat_far[1][0:3, :])
            for p in range(posts)
        ],
    ]
    sums = [chip_terms(fact[...], feature) for fact, feature in zip(facts, features)]
    acc_other[n_rows:, :] = jnp.zeros((acc_other.shape[0] - n_rows, filters), jnp.float32)
    acc_other[n_rows : n_rows + 3, :] = tree_sum([total[0] for total in sums])
    acc_other[n_rows + 3 : n_rows + 3 + n_codes, :] = tree_sum([total[1] for total in sums])


def gather_kernel(z_ref, acc, own_facts, far_facts, near_facts, *refs):
    *terms, total_ref, pred_ref = refs
    posts = pred_ref.shape[0]
    for p in range(posts):
        pred_ref[pl.ds(p, 1)] = own_facts[5 * posts + p, 0:1]
    made = made_residuals(z_ref[0], posts, own_facts, far_facts, near_facts)
    total_ref[...] = acc[...] + scaled_sum(made, terms)


def tree_sum(values):
    while len(values) > 1:
        values = [values[i] + values[i + 1] for i in range(0, len(values), 2)]
    return values[0]


def code_starts(sizes, filters):
    starts, start = [], 0
    for size in sizes:
        starts.append(start)
        start += -(-size // filters) * filters
    return starts


def code_rows(sizes, filters):
    return sum(-(-size // filters) for size in sizes)


def swap_kernel(sizes, own_ref, mine_ref, came_ref, grad_ref, head_ref, *code_refs):
    n_rows, filters = own_ref.shape
    grad_ref[...] = own_ref[...] + came_ref[0:n_rows, :]
    head_ref[...] = mine_ref[n_rows : n_rows + 3, :] + came_ref[n_rows : n_rows + 3, :]
    row = n_rows + 3
    for size, ref in zip(sizes, code_refs):
        for start in range(0, size, filters):
            count = min(filters, size - start)
            total = mine_ref[row : row + 1, :] + came_ref[row : row + 1, :]
            ref[pl.ds(start, count)] = total[0, :count]
            row += 1


def local_gather(n_doc, n_filt, *args):
    (
        embedded,
        lengths,
        conv_weight,
        head_weight,
        occupation,
        cohort,
        education,
        occ_table,
        cohort_table,
        edu_table,
        wage,
    ) = args
    posts, seq_len, dims = embedded.shape
    filters = conv_weight.shape[2]
    slice_e = dims // n_doc
    sizes = (occ_table.shape[0], cohort_table.shape[0], edu_table.shape[0])
    f32, i32 = jnp.float32, jnp.int32
    me = lax.axis_index("doc").astype(i32).reshape(1)
    vmem = pl.BlockSpec(memory_space=pltpu.VMEM)
    smem = pl.BlockSpec(memory_space=pltpu.SMEM)
    anywhere = pl.BlockSpec(memory_space=pl.ANY)
    hbm = pl.BlockSpec(memory_space=pltpu.HBM)

    def posts_scratch(n):
        return [
            pltpu.VMEM((n, seq_len + 2 * PAD, dims), f32),
            pltpu.VMEM((n, 8, filters), f32),
            pltpu.VMEM((n, seq_len, (2 * REACH + 1) * dims), jnp.bfloat16),
        ]

    def swap(x, k, axis="doc"):
        size = n_doc if axis == "doc" else n_filt
        return lax.ppermute(x, axis, [(i, i ^ k) for i in range(size)])

    def call(kernel, specs, out, scratch=(), cost=1):
        def run(*operands):
            operands = [
                pltpu.with_memory_space_constraint(x, pltpu.HBM) if spec is hbm else x
                for x, spec in zip(operands, specs)
            ]
            return built(*operands)

        built = pl.pallas_call(
            kernel,
            in_specs=specs,
            out_specs=[vmem] * len(out),
            out_shape=[
                jax.ShapeDtypeStruct(x, f32) if isinstance(x, tuple) else x for x in out
            ],
            scratch_shapes=list(scratch),
            compiler_params=pltpu.CompilerParams(vmem_limit_bytes=24 << 20),
            cost_estimate=pl.CostEstimate(flops=cost, bytes_accessed=1, transcendentals=0),
        )
        return run

    acc_shape = (TAPS * slice_e, filters)
    n_facts = -(-6 * posts // 8) * 8
    weights = jnp.transpose(conv_weight, (1, 0, 2)).reshape(TAPS * dims, filters)
    half = (lax.axis_index("filt").astype(i32) & 1).reshape(1)
    pieces, far_piece = call(
        mask_kernel,
        [smem] * 2 + [hbm] * 2,
        [(posts, seq_len, dims), (seq_len, dims)],
        [
            pltpu.VMEM((posts, seq_len, dims), jnp.bfloat16),
            pltpu.SMEM((posts,), i32),
            pltpu.SemaphoreType.DMA((posts + 1,)),
        ],
        cost=10**10,
    )(me, half, lengths, embedded)

    near = [k for k in range(2, n_doc, 2) if bin(k).count("1") == 1][::-1]
    far = sum(near)
    far_one = swap(far_piece, far)
    near_pieces = [swap(pieces, k) for k in near]

    part, feat_own, share_own, base = call(
        own_kernel,
        [hbm] * 7 + [vmem] * 3,
        [
            (8, 128),
            (posts, 3, filters),
            (posts, 3, seq_len, filters),
            (n_facts, 128),
        ],
        [pltpu.SMEM((posts,), i32)] * 3
        + [pltpu.SMEM((posts,), f32)]
        + [pltpu.SMEM((size,), f32) for size in sizes]
        + [posts_scratch(posts)[i] for i in (0, 2, 1)]
        + [pltpu.SemaphoreType.DMA((7,))],
    )(
        occupation,
        cohort,
        education,
        wage,
        occ_table,
        cohort_table,
        edu_table,
        weights,
        pieces,
        head_weight,
    )

    def terms_of(x, keep, cost=1):
        feat, *terms = call(
            functools.partial(one_kernel, len(keep), slice_e),
            [smem] + [vmem] * 3 + [anywhere] * len(keep),
            [(8, filters)] + [(1,) + acc_shape] * 2,
            posts_scratch(1),
            cost,
        )(me, x, weights, head_weight, *keep)
        return feat, terms

    parts = [part] + [swap(part, k, "filt") for k in range(2, n_filt)]
    first_part, far_one = lax.optimization_barrier((part, far_one))
    parts.insert(1, swap(first_part, 1, "filt"))
    own_terms = call(
        functools.partial(own_terms_kernel, slice_e),
        [smem, vmem, vmem],
        [(posts,) + acc_shape] * 2,
    )(me, pieces, share_own)
    far_two = swap(far_one, 1, "filt")
    far_feat, far_terms = terms_of(far_one[None], (), 4 * 10**9)
    parts, far_feat, far_terms, own_terms = lax.optimization_barrier(
        (parts, far_feat, far_terms, own_terms)
    )
    keep = [*own_terms, *far_terms]
    (facts,) = call(
        functools.partial(facts_kernel, posts, len(keep)),
        [vmem] * (1 + len(parts)) + [anywhere] * len(keep),
        [(n_facts, 128)],
    )(base, *parts, *keep)

    all_facts = [facts] + [swap(facts, k) for k in near] + [swap(facts, far)]
    far_feat_two, far_terms_two = terms_of(far_two[None], keep)
    keep += far_terms_two
    near_feat, near_terms = terms_of(near_pieces[0], keep)
    terms = list(zip(own_terms, far_terms, far_terms_two, near_terms))
    extra = -(-(3 + code_rows(sizes, filters)) // 8) * 8
    acc_own, acc_other = call(
        functools.partial(last_kernel, sizes, slice_e),
        [smem] * 2 + [vmem] * 16,
        [acc_shape, (acc_shape[0] + extra, filters)],
        posts_scratch(2 * posts - 1),
    )(
        me,
        half,
        *all_facts,
        *near_pieces,
        feat_own,
        far_feat,
        far_feat_two,
        near_feat,
        *terms[1],
        weights,
        head_weight,
    )

    came = swap(acc_other, 1)
    total, prediction = call(gather_kernel, [smem] + [vmem] * 8, [acc_shape, (posts,)])(
        half, acc_own, all_facts[0], all_facts[3], all_facts[1 + EARLY], *terms[0]
    )
    grad, head_grad, *codes = call(
        functools.partial(swap_kernel, sizes),
        [vmem] * 3,
        [acc_shape, (3, filters)] + [(size,) for size in sizes],
    )(total, acc_other, came)
    conv_grad = jnp.transpose(grad.reshape(TAPS, slice_e, filters), (1, 0, 2))
    return (conv_grad, head_grad, *codes, prediction)


def solution(mesh):
    n_doc, n_filt = mesh.shape["doc"], mesh.shape["filt"]

    def local(*args):
        if (n_doc, n_filt, args[0].shape[0]) == (8, 4, 2):
            return local_gather(n_doc, n_filt, *args)
        return local_scatter(*args)

    return jax.shard_map(
        local,
        mesh=mesh,
        in_specs=(
            P("doc", None, None),
            P("doc"),
            P(None, None, "filt"),
            P(None, "filt"),
            P("doc"),
            P("doc"),
            P("doc"),
            P(),
            P(),
            P(),
            P("doc"),
        ),
        out_specs=(P("doc", None, "filt"), P(None, "filt"), P(), P(), P(), P("doc")),
        check_vma=False,
    )
```
